32 devices in a mesh: section: 2 (over core), dp: 16 (over z, y, x).
Axes of the slice: x: 2, y: 2, z: 4, core: 2. Of those that a mesh axis runs over, the one named last changes fastest.
Arguments:
- tokens: bfloat16 [6, 16, 128, 768], P(None, 'dp'), may hold values from -6 to 6
- cotangent: bfloat16 [6, 16, 128, 768], P(None, 'dp'), may hold values from -6 to 6
- lengths: int32 [6, 16], P(None, 'dp'), may hold values from 1 to 64, 768 in all within a row
- mixer_gain: float32 [2, 768], P('section'), may hold values from 0.5 to 1.5
- mixer_bias: float32 [2, 768], P('section'), may hold values from -2 to 2
- project_in: bfloat16 [2, 768, 2304], P('section'), may hold values from -0.21875 to 0.21875
- project_out: bfloat16 [2, 768, 768], P('section'), may hold values from -0.875 to 0.875
- dense_gain: float32 [2, 768], P('section'), may hold values from 0.5 to 1.5
- dense_bias: float32 [2, 768], P('section'), may hold values from -2 to 2
- up_weight: bfloat16 [2, 768, 3072], P('section'), may hold values from -0.21875 to 0.21875
- down_weight: bfloat16 [2, 3072, 768], P('section'), may hold values from -0.109375 to 0.109375
Outputs:
- layer_out: bfloat16 [2, 6, 16, 128, 768], P('section', None, 'dp')
- input_grads: bfloat16 [2, 6, 16, 128, 768], P('section', None, 'dp')
- grad_mixer_gain: float32 [2, 768], P('section', 'dp')
- grad_mixer_bias: float32 [2, 768], P('section', 'dp')
- grad_project_in: float32 [2, 768, 2304], P('section', 'dp')
- grad_project_out: float32 [2, 768, 768], P('section', 'dp')
- grad_dense_gain: float32 [2, 768], P('section', 'dp')
- grad_dense_bias: float32 [2, 768], P('section', 'dp')
- grad_up_weight: float32 [2, 768, 3072], P('section', 'dp')
- grad_down_weight: float32 [2, 3072, 768], P('section', 'dp')
The draws below stay inside these ranges and needn't reach their ends.
Inputs may be any that keep to these rules, and one draw needn't show every extreme that they name: In each micro-batch the lengths of the 16 sequences add up to 768, and one of them is 64.
All inputs are finite; a program needn't handle non-finite values. No bound on the sum of `lengths` on one device may be relied on, other than what follows from the above.
Results may differ from the reference program's by a relative error of at most 0.018.
Values may be sent and summed in bfloat16 or wider, within the bound.
No kernel may reach another device: no remote copies, remote signals or barrier semaphores. Data moves between devices by JAX's collectives and lax.ppermute only.
A program may use at most 384 MiB of HBM per device.

```python
import math
import jax
import jax.numpy as jnp
import numpy as np
from jax import lax

D = 768
HEADS = 12
HEAD = 64
FF = 3072
BLK = 16
SEQ = 64
MICRO = 6
BATCH = 16


def raised(values, key, source, target, parts, factor):
    def block_of(dim):
        return (jnp.arange(values.shape[dim]) // (values.shape[dim] // parts)).reshape((-1,) + (1,) * (values.ndim - 1 - dim))

    near = jax.random.permutation(key, parts)[block_of(target)]
    far = (block_of(target) + parts // 2) % parts
    return jnp.where((block_of(source) == near) | (block_of(source) == far), factor * values, values)


def steps_of(stream_key, dims, cuts, smallest, high):
    factor_of = 1.0
    for axis_at, shards_of in cuts:
        steps = jax.random.uniform(jax.random.fold_in(jax.random.fold_in(stream_key, 6), axis_at), (shards_of,), jnp.float32, smallest / len(cuts), high / len(cuts))
        factor_of = factor_of * jnp.repeat(jnp.exp(steps), dims[axis_at] // shards_of).reshape((-1,) + (1,) * (len(dims) - 1 - axis_at))
    return factor_of


def length_profile(count, total, bound, lean):
    portions = [(1 << 20) // math.isqrt(rank ** lean) + 1 for rank in range(2, count + 1)]
    spare, counts = total - bound - (count - 1), [1] * (count - 1)
    while spare > 0:
        candidates = [i for i in range(count - 1) if counts[i] < bound]
        mass, budget = sum([portions[i] for i in candidates]), spare
        for i in candidates:
            extra = min(bound - counts[i], max(1, budget * portions[i] // mass), spare)
            counts[i] = counts[i] + extra
            spare = spare - extra
    return np.array([bound] + counts)


def ragged(own_key, amount, total, limit, slope):
    if amount == 2:
        one = jax.random.randint(own_key, (), max(1, total - limit), min(limit, total - 1) + 1)
        return jnp.stack([one, total - one])
    sizes = jnp.asarray(length_profile(amount, total, limit, slope), jnp.int32)
    couples = (amount - 1) // 2
    donor, receiver = sizes[1:1 + 2 * couples:2], sizes[2:2 + 2 * couples:2]
    slack = jnp.minimum(donor - 1, limit - receiver)
    moved = jax.random.randint(jax.random.fold_in(own_key, 1), (couples,), 0, 1 << 20) % (slack + 1)
    sizes = sizes.at[1:1 + 2 * couples:2].set(donor - moved).at[2:2 + 2 * couples:2].set(receiver + moved)
    return sizes[jax.random.permutation(jax.random.fold_in(own_key, 2), amount)]


def bell_draw(rng, dims, scale, most, split=(), kind=jnp.bfloat16):
    values = jax.random.normal(rng, dims, jnp.float32) * scale
    if len(split) > 0:
        values = steps_of(rng, dims, split, -0.22, 0.18) * values
    return jnp.clip(values, min=-most, max=most).astype(kind)


def bell_draw_with(key, extent, deviation, bound, split, heavy, dtype=jnp.bfloat16):
    drawn = deviation * jax.random.normal(key, extent, jnp.float32)
    if split:
        drawn = drawn * steps_of(key, extent, split, -0.22, 0.18)
    return jnp.clip(raised(drawn, jax.random.fold_in(key, 3), *heavy), -bound, bound).astype(dtype)


def setup_inputs(seed: int = 0) -> dict:
    seeds = jax.random.split(jax.random.key(seed), 12)
    return {
        "tokens": bell_draw_with(seeds[0], (MICRO, BATCH, 2 * SEQ, D), 1.0, 6.0, ((1, 16),), (1, 3, 16, 2.0)),
        "cotangent": bell_draw(seeds[1], (MICRO, BATCH, 2 * SEQ, D), 1.0, 6.0, ((1, 16),)),
        "lengths": jax.vmap(lambda own: ragged(own, BATCH, 3 * BATCH * SEQ // 4, SEQ, 1))(jax.random.split(seeds[2], MICRO)).reshape((MICRO, BATCH)).astype(jnp.int32),
        "mixer_gain": jnp.clip(1.0 + 0.1 * jax.random.normal(seeds[3], (2, D), jnp.float32), 0.5, 1.5),
        "mixer_bias": bell_draw(seeds[4], (2, D), 0.3, 2.0, ((0, 2),), jnp.float32),
        "project_in": bell_draw(seeds[5], (2, D, 3 * D), D ** -0.5, 0.21875, ((0, 2),)),
        "project_out": bell_draw(seeds[6], (2, D, D), (D // 16) ** -0.5, 0.875, ((0, 2),)),
        "dense_gain": jnp.clip(1.0 + 0.1 * jax.random.normal(seeds[7], (2, D), jnp.float32), 0.5, 1.5),
        "dense_bias": bell_draw(seeds[8], (2, D), 0.3, 2.0, ((0, 2),), jnp.float32),
        "up_weight": bell_draw(seeds[9], (2, D, FF), D ** -0.5, 0.21875, ((0, 2),)),
        "down_weight": bell_draw(seeds[10], (2, FF, D), FF ** -0.5, 0.109375, ((0, 2),)),
    }


@jax.custom_vjp
def low(v):
    return lax.optimization_barrier(v.astype(jnp.bfloat16)).astype(jnp.float32)

@jax.custom_vjp
def low_back(v):
    return v

def low_keep(v):
    return (low(v), None)

def low_pass(kept, grad):
    return (grad,)

def back_keep(v):
    return (v, None)

def back_low(kept, grad):
    return (low(grad),)
low.defvjp(low_keep, low_pass)
low_back.defvjp(back_keep, back_low)
norm_eps = 1e-05
masked_score = -1000000000.0
highest = lax.Precision.HIGHEST

def matmul_high(left, right):
    return jnp.dot(left, right, precision=highest)

def rotary_tables():
    places = (jnp.arange(2 * SEQ) % SEQ).astype(jnp.float32)
    halfway = HEAD // 2
    freqs = 10000.0 ** (-jnp.arange(halfway).astype(jnp.float32) * 2.0 / HEAD)
    angles = places[:, None] * freqs[None, :]
    return (jnp.cos(angles)[:, None, :], jnp.sin(angles)[:, None, :])

def rotate(values, cosine, sine):
    halfway = values.shape[-1] // 2
    first_half = values[..., :halfway]
    second_half = values[..., halfway:]
    return jnp.concatenate([first_half * cosine - second_half * sine, second_half * cosine + first_half * sine], axis=-1)

def open_keys(length):
    slots = jnp.arange(2 * SEQ)
    clean = slots >= SEQ
    places = slots % SEQ
    blocks = places // BLK
    same_block = blocks[:, None] == blocks[None, :]
    earlier = blocks[None, :] < blocks[:, None]
    up_to = blocks[None, :] <= blocks[:, None]
    query_clean = clean[:, None]
    key_clean = clean[None, :]
    structure = ~query_clean & ~key_clean & same_block | ~query_clean & key_clean & earlier | query_clean & key_clean & up_to
    present = (places[None, :] < length) | (slots[:, None] == slots[None, :])
    return structure & present

def layer_norm(values, gain, bias):
    centered = values - lax.optimization_barrier(jnp.mean(values, axis=-1, keepdims=True))
    spread = lax.optimization_barrier(jnp.mean(centered * centered, axis=-1, keepdims=True))
    return centered * lax.rsqrt(spread + norm_eps) * gain + bias

def layer(inputs, weights, allowed, cosine, sine):
    mixer_gain, mixer_bias, project_in, project_out, dense_gain, dense_bias, up_weight, down_weight = weights
    slots = inputs.shape[0]
    normed = low(layer_norm(inputs, mixer_gain, mixer_bias))
    projected = low_back(matmul_high(normed, project_in))
    queries = low(rotate(projected[:, :D].reshape(slots, HEADS, HEAD), cosine, sine))
    keys_rot = low(rotate(projected[:, D:2 * D].reshape(slots, HEADS, HEAD), cosine, sine))
    values_all = low(projected[:, 2 * D:].reshape(slots, HEADS, HEAD))
    scores = low_back(jnp.einsum('qhd,khd->hqk', queries, keys_rot, precision=highest) * HEAD ** (-0.5))
    scores = jnp.where(allowed[None], scores, masked_score)
    largest = lax.optimization_barrier(jnp.max(scores, axis=-1, keepdims=True))
    weighted = jnp.exp(scores - largest)
    probs = low(weighted / lax.optimization_barrier(jnp.sum(weighted, axis=-1, keepdims=True)))
    mixed = jnp.einsum('hqk,khd->qhd', probs, values_all, precision=highest).reshape(slots, D)
    mixed = low(low_back(mixed))
    hidden = inputs + low_back(matmul_high(mixed, project_out))
    dense_in = low(layer_norm(hidden, dense_gain, dense_bias))
    upward = low_back(matmul_high(dense_in, up_weight))
    active = low(jax.nn.gelu(upward, approximate=True))
    return hidden + low_back(matmul_high(active, down_weight))

def reference(tokens, cotangent, lengths, mixer_gain, mixer_bias, project_in, project_out, dense_gain, dense_bias, up_weight, down_weight):
    params = tuple((weight.astype(jnp.float32) for weight in (mixer_gain, mixer_bias, project_in, project_out, dense_gain, dense_bias, up_weight, down_weight)))
    cosine, sine = rotary_tables()
    rows_in = tokens.reshape(MICRO * BATCH, 2 * SEQ, D)
    rows_cot = cotangent.reshape(MICRO * BATCH, 2 * SEQ, D)
    rows_len = lengths.reshape(MICRO * BATCH)

    def forward(inputs, offset, weights, allowed):
        first_layer = layer(inputs, tuple((weight[0] for weight in weights)), allowed, cosine, sine)
        middle = low_back(low(first_layer) + offset)
        second_layer = layer(middle, tuple((weight[1] for weight in weights)), allowed, cosine, sine)
        return (second_layer, low(first_layer))

    def one_row(totals, row):
        inputs, row_cot, length = row
        allowed = open_keys(length)
        offset = jnp.zeros((2 * SEQ, D), jnp.float32)
        result, pullback, middle = jax.vjp(lambda first_arg, second_arg, third_arg: forward(first_arg, second_arg, third_arg, allowed), inputs.astype(jnp.float32), offset, params, has_aux=True)
        input_grad, middle_grad, weight_grads = pullback(row_cot.astype(jnp.float32))
        totals = jax.tree.map(lambda first_arg, second_arg: first_arg + second_arg, totals, weight_grads)
        return (totals, (middle.astype(jnp.bfloat16), result.astype(jnp.bfloat16), input_grad.astype(jnp.bfloat16), middle_grad.astype(jnp.bfloat16)))
    zeros = tuple((jnp.zeros_like(weight) for weight in params))
    totals, kept = lax.scan(one_row, zeros, (rows_in, rows_cot, rows_len))
    middles, results, in_grads, mid_grads = kept
    full_shape = (MICRO, BATCH, 2 * SEQ, D)
    layer_out = jnp.stack([middles.reshape(full_shape), results.reshape(full_shape)])
    input_grads = jnp.stack([in_grads.reshape(full_shape), mid_grads.reshape(full_shape)])
    return (layer_out, input_grads, totals[0], totals[1], totals[2], totals[3], totals[4], totals[5], totals[6], totals[7])
```

```python
import functools
import math

import jax
import jax.numpy as jnp
import numpy as np
from jax import lax
from jax.experimental import pallas as pl
from jax.experimental.pallas import tpu as pltpu
from jax.sharding import PartitionSpec as P

D = 768
HEADS = 12
HEAD = 64
FF = 3072
BLK = 16
SEQ = 64
SLOTS = 2 * SEQ
PAIRS = HEADS // 2
LANES = 2 * HEAD
BLOCKS = 16
FT = 512
NFT = FF // FT

norm_eps = 1e-05
masked_score = -1000000000.0
gelu_c = math.sqrt(2.0 / math.pi)
gelu_a = 0.044715

F32 = jnp.float32
BF16 = jnp.bfloat16
VMEM_LIMIT = 56 * 1024 * 1024


def dot(a, b, ca=1, cb=0):
    return lax.dot_general(a, b, (((ca,), (cb,)), ((), ())), preferred_element_type=F32)


def rotary_tables():
    places = (np.arange(SLOTS) % SEQ).astype(np.float32)
    half = HEAD // 2
    freqs = (10000.0 ** (-np.arange(half).astype(np.float32) * 2.0 / HEAD)).astype(np.float32)
    angles = (places[:, None] * freqs[None, :]).astype(np.float32)
    cos, sin = np.cos(angles), np.sin(angles)
    return np.stack(
        [
            np.concatenate([cos] * 4, axis=1),
            np.concatenate([-sin, sin, -sin, sin], axis=1),
        ]
    ).astype(np.float32)


def swap_halves(v):
    lane = lax.broadcasted_iota(jnp.int32, v.shape, 1)
    first = lax.rem(lane, HEAD) < HEAD // 2
    return jnp.where(first, pltpu.roll(v, LANES - 32, 1), pltpu.roll(v, 32, 1))


def open_keys_t(length):
    key = lax.broadcasted_iota(jnp.int32, (SLOTS, SLOTS), 0)
    query = lax.broadcasted_iota(jnp.int32, (SLOTS, SLOTS), 1)
    key_clean, query_clean = key >= SEQ, query >= SEQ
    key_place, query_place = lax.rem(key, SEQ), lax.rem(query, SEQ)
    kb, qb = lax.div(key_place, BLK), lax.div(query_place, BLK)
    both_noisy = jnp.logical_and(jnp.logical_not(key_clean), jnp.logical_not(query_clean))
    both_clean = jnp.logical_and(key_clean, query_clean)
    crossed = jnp.logical_and(key_clean, jnp.logical_not(query_clean))
    structure = (
        (both_noisy & (kb == qb)) | (crossed & (kb < qb)) | (both_clean & (kb <= qb))
    )
    return structure & ((key_place < length) | (key == query))


def norm_stats(v):
    centered = v - jnp.mean(v, axis=-1, keepdims=True)
    spread = jnp.mean(centered * centered, axis=-1, keepdims=True)
    return centered, lax.rsqrt(spread + norm_eps)


def norm_back(dy, source, gain):
    centered, scale = norm_stats(source)
    xhat = centered * scale
    g = dy * gain
    part = scale * (
        g
        - jnp.mean(g, axis=-1, keepdims=True)
        - xhat * jnp.mean(g * xhat, axis=-1, keepdims=True)
    )
    return part, jnp.sum(dy * xhat, axis=0, keepdims=True), jnp.sum(dy, axis=0, keepdims=True)


def start_from(own, mine, other, pieces, dst, sems):
    @pl.when(own)
    def _():
        for i, piece in enumerate(pieces):
            pltpu.make_async_copy(mine.at[piece], dst.at[piece], sems.at[i]).start()

    @pl.when(jnp.logical_not(own))
    def _():
        for i, piece in enumerate(pieces):
            pltpu.make_async_copy(other.at[piece], dst.at[piece], sems.at[i]).start()


def wait_from(mine, piece, dst, sem):
    pltpu.make_async_copy(mine.at[piece], dst.at[piece], sem).wait()


def col_pieces(rows, cols, n):
    w = cols // n
    return [(slice(0, rows), slice(i * w, (i + 1) * w)) for i in range(n)]


def row_pieces(rows, cols, n):
    w = rows // n
    return [(slice(i * w, (i + 1) * w), slice(0, cols)) for i in range(n)]


IN_PIECES = col_pieces(D, 3 * D, 3)
OUT_PIECES = row_pieces(D, D, 1)
UP_PIECES = col_pieces(D, FF, NFT)
DOWN_PIECES = row_pieces(FF, D, NFT)


def attn_fwd_kernel(
    layer, seqs, scal, x_ref, vec_mine, vec_other, rot_ref, in_mine, in_other, out_mine, out_other,
    acts_ref, qkv_ref, probs_ref, hidden_ref,
    w_in, w_out, mask, sems,
):
    own = scal[0] == layer
    start_from(own, in_mine, in_other, IN_PIECES, w_in, sems)
    start_from(own, out_mine, out_other, OUT_PIECES, w_out, sems.at[pl.ds(3, 1)])
    vec = jnp.where(own, vec_mine[...], vec_other[...])
    x = x_ref[...].astype(F32)
    centered, scale = norm_stats(x)
    acts_ref[:, 0:D] = (centered * scale * vec[0:1] + vec[1:2]).astype(BF16)
    for s in range(seqs):
        keep = open_keys_t(scal[1 + scal[0] * seqs + s])
        mask[s] = jnp.where(keep, 0.0, 1.0)
    cos, sin = rot_ref[0], rot_ref[1]
    for part in range(3):
        wait_from(in_mine, IN_PIECES[part], w_in, sems.at[part])
        for t in range(D // 256):
            lo = part * D + t * 256
            val = dot(acts_ref[:, 0:D], w_in[:, lo : lo + 256])
            if part == 2:
                qkv_ref[:, lo : lo + 256] = val.astype(BF16)
                continue
            for u in range(2):
                for s in range(seqs):
                    v = val[s * SLOTS : (s + 1) * SLOTS, u * LANES : (u + 1) * LANES]
                    v = v * cos + swap_halves(v) * sin
                    if part == 0:
                        v = v * HEAD ** (-0.5)
                    qkv_ref[
                        s * SLOTS : (s + 1) * SLOTS, lo + u * LANES : lo + (u + 1) * LANES
                    ] = v.astype(BF16)
    lane = lax.broadcasted_iota(jnp.int32, (SLOTS, LANES), 1)
    left = lane < HEAD
    zero = jnp.zeros((SLOTS, LANES), BF16)
    for s in range(seqs):
        rows = slice(s * SLOTS, (s + 1) * SLOTS)
        shut = mask[s] > 0.5
        for p in range(PAIRS):
            q = qkv_ref[rows, p * LANES : (p + 1) * LANES]
            k = qkv_ref[rows, D + p * LANES : D + (p + 1) * LANES]
            v = qkv_ref[rows, 2 * D + p * LANES : 2 * D + (p + 1) * LANES]
            lows = []
            for h in range(2):
                qm = jnp.where(left, q, zero) if h == 0 else jnp.where(left, zero, q)
                st = jnp.where(shut, masked_score, dot(k, qm, 1, 1))
                e = jnp.exp(st - jnp.max(st, axis=0, keepdims=True))
                pr = e * (1.0 / jnp.sum(e, axis=0, keepdims=True))
                probs_ref[s * PAIRS + p, :, h * SLOTS : (h + 1) * SLOTS] = pr
                lows.append(pr.astype(BF16))
            vm = jnp.concatenate([jnp.where(left, v, zero), jnp.where(left, zero, v)], axis=0)
            mixed = dot(jnp.concatenate(lows, axis=0), vm, 0, 0)
            acts_ref[rows, D + p * LANES : D + (p + 1) * LANES] = mixed.astype(BF16)
    wait_from(out_mine, OUT_PIECES[0], w_out, sems.at[3])
    hidden = x_ref[...].astype(F32) + dot(acts_ref[:, D : 2 * D], w_out[...])
    hidden_ref[...] = hidden
    centered, scale = norm_stats(hidden)
    acts_ref[:, 2 * D : 3 * D] = (centered * scale * vec[2:3] + vec[3:4]).astype(BF16)


def ff_fwd_kernel(
    layer, scal, acts_ref, hidden_ref, up_mine, up_other, down_mine, down_other,
    y_ref, active_ref, upward_ref,
    w_up, w_down, upward, active, acc, sems, out_sems,
):
    own = scal[0] == layer
    start_from(own, up_mine, up_other, UP_PIECES, w_up, sems)
    start_from(own, down_mine, down_other, DOWN_PIECES, w_down, sems.at[pl.ds(NFT, NFT)])
    copies = []
    for t in range(NFT):
        cols = slice(t * FT, (t + 1) * FT)
        wait_from(up_mine, UP_PIECES[t], w_up, sems.at[t])
        for h in range(FT // 256):
            cut = slice(t * FT + h * 256, t * FT + (h + 1) * 256)
            u = dot(acts_ref[...], w_up[:, cut])
            upward[:, cut] = u
            th = jnp.tanh(gelu_c * (u + gelu_a * (u * u * u)))
            active[:, cut] = (0.5 * u * (1.0 + th)).astype(BF16)
        wait_from(down_mine, DOWN_PIECES[t], w_down, sems.at[NFT + t])
        part = dot(active[:, cols], w_down[cols, :])
        if t == 0:
            acc[...] = hidden_ref[...] + part
        elif t < NFT - 1:
            acc[...] += part
        else:
            y_ref[...] = (acc[...] + part).astype(BF16)
        for j, (src, dst) in enumerate(((upward, upward_ref), (active, active_ref))):
            c = pltpu.make_async_copy(src.at[:, cols], dst.at[:, cols], out_sems.at[2 * t + j])
            c.start()
            copies.append(c)
    for c in copies:
        c.wait()


def ff_bwd_kernel(
    layer, scal, r_ref, hidden_ref, vec_mine, vec_other, upward_ref,
    up_mine, up_other, down_mine, down_other, out_mine, out_other,
    ug_ref, bgrad_ref, hgrad_ref, mgrad_ref, vgrad_ref,
    w_up, w_down, w_out, upward, acc, sems, u_sems,
):
    own = scal[0] == layer
    loads = []
    for t in range(NFT):
        cols = slice(t * FT, (t + 1) * FT)
        c = pltpu.make_async_copy(upward_ref.at[:, cols], upward.at[:, cols], u_sems.at[t])
        loads.append(c)
    loads[0].start()
    start_from(own, down_mine, down_other, DOWN_PIECES[:1], w_down, sems.at[pl.ds(NFT, 1)])
    start_from(own, up_mine, up_other, UP_PIECES[:1], w_up, sems)
    for t in range(1, NFT):
        loads[t].start()
    start_from(own, down_mine, down_other, DOWN_PIECES[1:], w_down, sems.at[pl.ds(NFT + 1, NFT - 1)])
    start_from(own, up_mine, up_other, UP_PIECES[1:], w_up, sems.at[pl.ds(1, NFT - 1)])
    start_from(own, out_mine, out_other, OUT_PIECES, w_out, sems.at[pl.ds(2 * NFT, 1)])
    vec = jnp.where(own, vec_mine[...], vec_other[...])
    for t in range(NFT):
        cols = slice(t * FT, (t + 1) * FT)
        loads[t].wait()
        wait_from(down_mine, DOWN_PIECES[t], w_down, sems.at[NFT + t])
        for h in range(FT // 256):
            cut = slice(t * FT + h * 256, t * FT + (h + 1) * 256)
            ag = dot(r_ref[...], w_down[cut, :], 1, 1)
            u = upward[:, cut]
            u2 = u * u
            th = jnp.tanh(gelu_c * (u + gelu_a * (u2 * u)))
            slope = 0.5 * (1.0 + th) + (0.5 * gelu_c) * u * (1.0 - th * th) * (
                1.0 + (3.0 * gelu_a) * u2
            )
            ug_ref[:, cut] = (ag * slope).astype(BF16)
        wait_from(up_mine, UP_PIECES[t], w_up, sems.at[t])
        part = dot(ug_ref[:, cols], w_up[:, cols], 1, 1)
        if t == 0:
            acc[...] = part
        else:
            acc[...] += part
    part, dg, db = norm_back(acc[...], hidden_ref[...], vec[2:3])
    vgrad_ref[0:1] = dg
    vgrad_ref[1:2] = db
    hgrad = r_ref[...].astype(F32) + part
    hgrad_ref[...] = hgrad
    bgrad_ref[...] = hgrad.astype(BF16)
    wait_from(out_mine, OUT_PIECES[0], w_out, sems.at[2 * NFT])
    mgrad_ref[...] = dot(bgrad_ref[...], w_out[...], 1, 1).astype(BF16)


def attn_bwd_kernel(
    layer, seqs, scal, x_ref, qkv_ref, probs_ref, mgrad_ref, hgrad_ref, vec_mine, vec_other, rot_ref,
    in_mine, in_other,
    pgrad_ref, xgrad_ref, vgrad_ref,
    w_in, sems,
):
    own = scal[0] == layer
    start_from(own, in_mine, in_other, IN_PIECES, w_in, sems)
    vec = jnp.where(own, vec_mine[...], vec_other[...])
    cos, sin = rot_ref[0], rot_ref[1]
    lane = lax.broadcasted_iota(jnp.int32, (SLOTS, LANES), 1)
    left = lane < HEAD
    zero = jnp.zeros((SLOTS, LANES), BF16)

    def both(v):
        return jnp.concatenate([jnp.where(left, v, zero), jnp.where(left, zero, v)], axis=0)

    for s in range(seqs):
        rows = slice(s * SLOTS, (s + 1) * SLOTS)
        for p in range(PAIRS):
            cut = slice(p * LANES, (p + 1) * LANES)
            q = qkv_ref[rows, p * LANES : (p + 1) * LANES]
            k = qkv_ref[rows, D + p * LANES : D + (p + 1) * LANES]
            v = qkv_ref[rows, 2 * D + p * LANES : 2 * D + (p + 1) * LANES]
            dm = both(mgrad_ref[rows, cut])
            pt = probs_ref[s * PAIRS + p]
            dpt = dot(v, dm, 1, 1)
            dst = pt * (dpt - jnp.sum(pt * dpt, axis=0, keepdims=True))
            dst = dst.astype(BF16)
            dv = dot(pt.astype(BF16), dm)
            dk = dot(dst, both(q))
            stacked = jnp.concatenate([dst[:, 0:SLOTS], dst[:, SLOTS : 2 * SLOTS]], axis=0)
            dq = dot(stacked, both(k), 0, 0) * HEAD ** (-0.5)
            dq = dq * cos - swap_halves(dq) * sin
            dk = dk * cos - swap_halves(dk) * sin
            pgrad_ref[rows, p * LANES : (p + 1) * LANES] = dq.astype(BF16)
            pgrad_ref[rows, D + p * LANES : D + (p + 1) * LANES] = dk.astype(BF16)
            pgrad_ref[rows, 2 * D + p * LANES : 2 * D + (p + 1) * LANES] = dv.astype(BF16)
    for part in range(3):
        wait_from(in_mine, IN_PIECES[part], w_in, sems.at[part])
    ngrad = dot(pgrad_ref[...], w_in[...], 1, 1)
    part, dg, db = norm_back(ngrad, x_ref[...].astype(F32), vec[0:1])
    vgrad_ref[0:1] = dg
    vgrad_ref[1:2] = db
    xgrad_ref[...] = (hgrad_ref[...] + part).astype(BF16)


def wgrad_kernel(terms, scal, *refs):
    ins, (keep_ref, send_ref, res) = refs[: 4 * len(terms)], refs[4 * len(terms) :]
    base = 0
    for i, (rows, width, tile_rows) in enumerate(terms):
        a0, a1, b0, b1 = ins[4 * i : 4 * i + 4]
        step = min(width, 512) if width % 512 == 0 else 384
        for c in range(width // step):
            cut = slice(c * step, (c + 1) * step)
            for t in range(rows // tile_rows):
                trows = slice(t * tile_rows, (t + 1) * tile_rows)
                res[trows, base + c * step : base + (c + 1) * step] = dot(
                    a0[:, trows], b0[:, cut], 0, 0
                ) + dot(a1[:, trows], b1[:, cut], 0, 0)
        base += width
    per = terms[0][0] // BLOCKS
    for r in range(BLOCKS):
        at = pl.multiple_of(scal[1 + r] * per, per)
        block = res[pl.ds(at, per), :].astype(BF16)
        if r < BLOCKS // 2:
            keep_ref[r] = block
        else:
            send_ref[r - BLOCKS // 2] = block


def whole(shape):
    return pl.BlockSpec(shape, lambda i, s: (0,) * len(shape))


def call(kernel, scal, ins, in_specs, outs, out_specs, scratch, flops, moved):
    return pl.pallas_call(
        kernel,
        grid_spec=pltpu.PrefetchScalarGridSpec(
            num_scalar_prefetch=1,
            grid=(1,),
            in_specs=in_specs,
            out_specs=out_specs,
            scratch_shapes=scratch,
        ),
        out_shape=outs,
        compiler_params=pltpu.CompilerParams(vmem_limit_bytes=VMEM_LIMIT),
        cost_estimate=pl.CostEstimate(flops=flops, bytes_accessed=moved, transcendentals=0),
    )(scal, *ins)


def shape_of(shape, dtype):
    return jax.ShapeDtypeStruct(shape, dtype)


HBM = pl.BlockSpec(memory_space=pl.ANY)


class Layer:
    def __init__(self, index, seqs, scal, mine, other, rot):
        self.index, self.seqs, self.scal = index, seqs, scal
        self.mine, self.other, self.rot = mine, other, rot
        self.tokens = seqs * SLOTS

    def attn_fwd(self, x, half_spec):
        t = self.tokens
        m, o = self.mine, self.other
        return call(
            functools.partial(attn_fwd_kernel, self.index, self.seqs),
            self.scal,
            (x, m["vec"], o["vec"], self.rot, m["in"], o["in"], m["out"], o["out"]),
            [half_spec, whole((4, D)), whole((4, D)), whole((2, SLOTS, LANES)), HBM, HBM, HBM, HBM],
            [
                shape_of((t, 3 * D), BF16),
                shape_of((t, 3 * D), BF16),
                shape_of((self.seqs * PAIRS, SLOTS, 2 * SLOTS), F32),
                shape_of((t, D), F32),
            ],
            [
                whole((t, 3 * D)),
                whole((t, 3 * D)),
                whole((self.seqs * PAIRS, SLOTS, 2 * SLOTS)),
                whole((t, D)),
            ],
            [
                pltpu.VMEM((D, 3 * D), BF16),
                pltpu.VMEM((D, D), BF16),
                pltpu.VMEM((self.seqs, SLOTS, SLOTS), F32),
                pltpu.SemaphoreType.DMA((4,)),
            ],
            2 * t * D * 4 * D * 2,
            20 * 2**20,
        )

    def ff_fwd(self, acts, hidden):
        t = self.tokens
        m, o = self.mine, self.other
        return call(
            functools.partial(ff_fwd_kernel, self.index),
            self.scal,
            (acts, hidden, m["up"], o["up"], m["down"], o["down"]),
            [pl.BlockSpec((t, D), lambda i, s: (0, 2)), whole((t, D)), HBM, HBM, HBM, HBM],
            [shape_of((t, D), BF16), shape_of((t, FF), BF16), shape_of((t, FF), F32)],
            [whole((t, D)), HBM, HBM],
            [
                pltpu.VMEM((D, FF), BF16),
                pltpu.VMEM((FF, D), BF16),
                pltpu.VMEM((t, FF), F32),
                pltpu.VMEM((t, FF), BF16),
                pltpu.VMEM((t, D), F32),
                pltpu.SemaphoreType.DMA((2 * NFT,)),
                pltpu.SemaphoreType.DMA((2 * NFT,)),
            ],
            2 * t * D * FF * 2,
            20 * 2**20,
        )

    def ff_bwd(self, r, r_spec, hidden, upward):
        t = self.tokens
        m, o = self.mine, self.other
        return call(
            functools.partial(ff_bwd_kernel, self.index),
            self.scal,
            (r, hidden, m["vec"], o["vec"], upward, m["up"], o["up"], m["down"], o["down"], m["out"], o["out"]),
            [r_spec, whole((t, D)), whole((4, D)), whole((4, D))] + [HBM] * 7,
            [
                shape_of((t, FF), BF16),
                shape_of((t, D), BF16),
                shape_of((t, D), F32),
                shape_of((t, D), BF16),
                shape_of((2, D), F32),
            ],
            [whole((t, FF)), whole((t, D)), whole((t, D)), whole((t, D)), whole((2, D))],
            [
                pltpu.VMEM((D, FF), BF16),
                pltpu.VMEM((FF, D), BF16),
                pltpu.VMEM((D, D), BF16),
                pltpu.VMEM((t, FF), F32),
                pltpu.VMEM((t, D), F32),
                pltpu.SemaphoreType.DMA((2 * NFT + 1,)),
                pltpu.SemaphoreType.DMA((NFT,)),
            ],
            2 * t * D * FF * 3,
            24 * 2**20,
        )

    def attn_bwd(self, x, half_spec, qkv, probs, mgrad, hgrad):
        t = self.tokens
        m, o = self.mine, self.other
        return call(
            functools.partial(attn_bwd_kernel, self.index, self.seqs),
            self.scal,
            (x, qkv, probs, mgrad, hgrad, m["vec"], o["vec"], self.rot, m["in"], o["in"]),
            [
                half_spec,
                whole((t, 3 * D)),
                whole((self.seqs * PAIRS, SLOTS, 2 * SLOTS)),
                whole((t, D)),
                whole((t, D)),
                whole((4, D)),
                whole((4, D)),
                whole((2, SLOTS, LANES)),
                HBM,
                HBM,
            ],
            [shape_of((t, 3 * D), BF16), shape_of((t, D), BF16), shape_of((2, D), F32)],
            [whole((t, 3 * D)), whole((t, D)), whole((2, D))],
            [pltpu.VMEM((D, 3 * D), BF16), pltpu.SemaphoreType.DMA((3,))],
            2 * t * D * 3 * D * 2,
            20 * 2**20,
        )


def wgrad(scal, t, terms):
    ins, specs, plan = [], [], []
    for (a0, a1), a_spec, rows, (b0, b1), b_specs, width in terms:
        ins += [a0, a1, b0, b1]
        specs += [a_spec, a_spec, b_specs[0], b_specs[1]]
        plan.append((rows, width, 768))
    rows, width = terms[0][2], sum(term[5] for term in terms)
    per = rows // BLOCKS
    half = (BLOCKS // 2, per, width)
    return call(
        functools.partial(wgrad_kernel, plan),
        scal,
        ins,
        specs,
        [shape_of(half, BF16), shape_of(half, BF16)],
        [whole(half), whole(half)],
        [pltpu.VMEM((rows, width), F32)],
        2 * 2 * t * rows * width,
        8 * 2**20,
    )


def axis_pairs(first, second, size):
    return [(i, i ^ first) for i in range(size)] + [
        (size + i, size + (i ^ second)) for i in range(size)
    ]


def body(
    tokens, cotangent, lengths, mixer_gain, mixer_bias, project_in, project_out,
    dense_gain, dense_bias, up_weight, down_weight,
):
    micro, rows = tokens.shape[:2]
    total = micro * rows
    seqs = total // 2
    t = seqs * SLOTS
    core = lax.axis_index("section")
    first = core == 0
    me = lax.axis_index("dp")
    dp = lax.axis_size("dp")
    fast = dp == BLOCKS
    both = ("section", "dp")

    def other_core(v):
        return lax.ppermute(v, "section", [(0, 1), (1, 0)])

    mine = {
        "vec": jnp.concatenate([mixer_gain, mixer_bias, dense_gain, dense_bias], axis=0),
        "in": project_in[0],
        "out": project_out[0],
        "up": up_weight[0],
        "down": down_weight[0],
    }
    other = {name: other_core(mine[name]) for name in ("vec", "in", "out", "up", "down")}
    rot = jnp.asarray(rotary_tables())
    scal = jnp.concatenate([core.reshape(1), lengths.reshape(total)]).astype(jnp.int32)

    xy_bits = ((1, 2), (2, 1), (4, 4), (8, 8))
    z_bits = ((4, 4), (8, 8), (1, 2), (2, 1))

    def places(bits):
        if not fast:
            table = np.arange(BLOCKS)
            return jnp.concatenate([core.reshape(1), jnp.asarray(table, jnp.int32)]).astype(jnp.int32)
        rel = np.zeros((2, BLOCKS), np.int32)
        for c in range(2):
            for r in range(BLOCKS):
                for stage in range(4):
                    if r >> (3 - stage) & 1:
                        rel[c, r] ^= bits[stage][c]
        dest = me ^ jnp.where(first, jnp.asarray(rel[0]), jnp.asarray(rel[1]))
        return jnp.concatenate([core.reshape(1), dest]).astype(jnp.int32)

    xy_scal, z_scal = places(xy_bits), places(z_bits)

    def reduce(pair, bits):
        keep, send = pair
        per, width = keep.shape[1:]
        if not fast:
            flat = jnp.concatenate([keep, send], axis=0).reshape(BLOCKS * per, width)
            return lax.psum_scatter(flat.astype(F32), "dp", scatter_dimension=0, tiled=True)
        for stage in range(4):
            got = lax.ppermute(send, both, axis_pairs(*bits[stage], dp))
            half = keep.shape[0] // 2
            if half:
                send = keep[half:] + got[half:]
                keep = keep[:half] + got[:half]
        return keep[0].astype(F32) + got[0].astype(F32)

    x0 = tokens.reshape(total * SLOTS, D)
    cot = cotangent.reshape(total * SLOTS, D)
    half_spec = pl.BlockSpec((t, D), lambda i, s: (s[0], 0))
    full_spec = whole((t, D))

    layers = [Layer(i, seqs, scal, mine, other, rot) for i in range(2)]
    acts, qkv, probs, hidden, active, upward = ([None] * 2 for _ in range(6))
    ys = [None] * 2
    x, x_spec = x0, half_spec
    inputs = []
    for i, layer in enumerate(layers):
        inputs.append((x, x_spec))
        acts[i], qkv[i], probs[i], hidden[i] = layer.attn_fwd(x, x_spec)
        ys[i], active[i], upward[i] = layer.ff_fwd(acts[i], hidden[i])
        x, x_spec = ys[i], full_spec
    acts_o = [other_core(v) for v in acts]
    active_o = [other_core(v) for v in active]

    def at(col):
        return pl.BlockSpec((t, D), lambda i, s: (0, col))

    def mine_cols(width):
        return pl.BlockSpec((t, width), lambda i, s: (0, s[0]))

    shards = [None] * 2
    vgrads = [None] * 2
    xgrads = [None] * 2
    r, r_spec = cot, half_spec
    for i in (1, 0):
        layer = layers[i]
        ug, bgrad, hgrad, mgrad, vec_dense = layer.ff_bwd(r, r_spec, hidden[i], upward[i])
        ug_o, bgrad_o = other_core(ug), other_core(bgrad)
        if i == 1:
            r_pair = (cot, cot)
            r_specs = (
                pl.BlockSpec((t, D // 2), lambda i, s: (s[0], s[0])),
                pl.BlockSpec((t, D // 2), lambda i, s: (1 - s[0], s[0])),
            )
        else:
            r_pair = (r, xgrad_o)
            r_specs = (mine_cols(D // 2),) * 2
        down = wgrad(
            xy_scal, t, [((active[i], active_o[i]), whole((t, FF)), FF, r_pair, r_specs, D // 2)]
        )
        red_down = reduce(down, xy_bits)
        x, x_spec = inputs[i]
        pgrad, xgrad, vec_mixer = layer.attn_bwd(x, x_spec, qkv[i], probs[i], mgrad, hgrad)
        pgrad_o, xgrad_o = other_core(pgrad), other_core(xgrad)
        up = wgrad(
            xy_scal,
            t,
            [((acts[i], acts_o[i]), at(2), D, (ug, ug_o), (mine_cols(FF // 2),) * 2, FF // 2)],
        )
        red_up = reduce(up, xy_bits)
        attn_bits = z_bits if i == 1 else xy_bits
        attn = wgrad(
            z_scal if i == 1 else xy_scal,
            t,
            [
                ((acts[i], acts_o[i]), at(0), D, (pgrad, pgrad_o), (mine_cols(3 * D // 2),) * 2, 3 * D // 2),
                ((acts[i], acts_o[i]), at(1), D, (bgrad, bgrad_o), (mine_cols(D // 2),) * 2, D // 2),
            ],
        )
        red_attn = reduce(attn, attn_bits)
        shards[i] = (red_attn[:, : 3 * D // 2], red_attn[:, 3 * D // 2 :], red_up, red_down)
        vgrads[i] = (vec_mixer, vec_dense)
        xgrads[i] = xgrad
        r, r_spec = xgrad, full_spec

    def settle(a, b):
        here = jnp.where(first, a, b)
        there = other_core(jnp.where(first, b, a))
        return jnp.where(first, jnp.concatenate([here, there], -1), jnp.concatenate([there, here], -1))

    grad_in, grad_out, grad_up, grad_down = (
        settle(a, b)[None] for a, b in zip(shards[0], shards[1])
    )

    def settle_rows(pair):
        here = jnp.where(first, pair[0], pair[1])
        there = other_core(jnp.where(first, pair[1], pair[0]))
        whole_rows = jnp.where(
            first, jnp.concatenate([here, there], 0), jnp.concatenate([there, here], 0)
        )
        return whole_rows.reshape((1,) + tokens.shape)

    layer_out = settle_rows(ys)
    input_grads = settle_rows(xgrads)

    vec = jnp.concatenate([vgrads[0][0], vgrads[0][1], vgrads[1][0], vgrads[1][1]], axis=0)
    if fast:
        vec = vec + other_core(vec)
        for bits in xy_bits:
            vec = vec + lax.ppermute(vec, both, axis_pairs(*bits, dp))
    else:
        vec = lax.psum(vec, both)
    vec = jnp.where(first, vec[:4], vec[4:])
    per = D // dp
    vec = lax.dynamic_slice(vec, (0, me * per), (4, per))
    return (
        layer_out,
        input_grads,
        vec[0:1],
        vec[1:2],
        grad_in,
        grad_out,
        vec[2:3],
        vec[3:4],
        grad_up,
        grad_down,
    )


def solution(mesh):
    row = P(None, "dp", None, None)
    vec = P("section", None)
    mat = P("section", None, None)
    outs = P("section", None, "dp", None, None)
    out_vec = P("section", "dp")
    out_mat = P("section", "dp", None)
    return jax.shard_map(
        body,
        mesh=mesh,
        in_specs=(row, row, P(None, "dp"), vec, vec, mat, mat, vec, vec, mat, mat),
        out_specs=(outs, outs, out_vec, out_vec, out_mat, out_mat, out_vec, out_vec, out_mat, out_mat),
        check_vma=False,
    )
```

```python
import functools
import math

import jax
import jax.numpy as jnp
import numpy as np
from jax import lax
from jax.experimental import pallas as pl
from jax.experimental.pallas import tpu as pltpu
from jax.sharding import PartitionSpec as P

D = 768
HEADS = 12
HEAD = 64
FF = 3072
BLK = 16
SEQ = 64
SLOTS = 2 * SEQ
PAIRS = HEADS // 2
LANES = 2 * HEAD
BLOCKS = 16
FT = 512
NFT = FF // FT

norm_eps = 1e-05
masked_score = -1000000000.0
gelu_c = math.sqrt(2.0 / math.pi)
gelu_a = 0.044715

F32 = jnp.float32
BF16 = jnp.bfloat16
VMEM_LIMIT = 60 * 1024 * 1024


def dot(a, b, ca=1, cb=0):
    return lax.dot_general(a, b, (((ca,), (cb,)), ((), ())), preferred_element_type=F32)


def rotary_tables():
    places = (np.arange(SLOTS) % SEQ).astype(np.float32)
    half = HEAD // 2
    freqs = (10000.0 ** (-np.arange(half).astype(np.float32) * 2.0 / HEAD)).astype(np.float32)
    angles = (places[:, None] * freqs[None, :]).astype(np.float32)
    cos, sin = np.cos(angles), np.sin(angles)
    return np.stack(
        [
            np.concatenate([cos] * 4, axis=1),
            np.concatenate([-sin, sin, -sin, sin], axis=1),
        ]
    ).astype(np.float32)


def swap_halves(v):
    lane = lax.broadcasted_iota(jnp.int32, v.shape, 1)
    first = lax.rem(lane, HEAD) < HEAD // 2
    return jnp.where(first, pltpu.roll(v, LANES - 32, 1), pltpu.roll(v, 32, 1))


def open_keys_t(length):
    key = lax.broadcasted_iota(jnp.int32, (SLOTS, SLOTS), 0)
    query = lax.broadcasted_iota(jnp.int32, (SLOTS, SLOTS), 1)
    key_clean, query_clean = key >= SEQ, query >= SEQ
    key_place, query_place = lax.rem(key, SEQ), lax.rem(query, SEQ)
    kb, qb = lax.div(key_place, BLK), lax.div(query_place, BLK)
    both_noisy = jnp.logical_and(jnp.logical_not(key_clean), jnp.logical_not(query_clean))
    both_clean = jnp.logical_and(key_clean, query_clean)
    crossed = jnp.logical_and(key_clean, jnp.logical_not(query_clean))
    structure = (
        (both_noisy & (kb == qb)) | (crossed & (kb < qb)) | (both_clean & (kb <= qb))
    )
    return structure & ((key_place < length) | (key == query))


def norm_stats(v):
    centered = v - jnp.mean(v, axis=-1, keepdims=True)
    spread = jnp.mean(centered * centered, axis=-1, keepdims=True)
    return centered, lax.rsqrt(spread + norm_eps)


def norm_back(dy, source, gain):
    centered, scale = norm_stats(source)
    xhat = centered * scale
    g = dy * gain
    part = scale * (
        g
        - jnp.mean(g, axis=-1, keepdims=True)
        - xhat * jnp.mean(g * xhat, axis=-1, keepdims=True)
    )
    return part, jnp.sum(dy * xhat, axis=0, keepdims=True), jnp.sum(dy, axis=0, keepdims=True)


def col_pieces(rows, cols, n):
    w = cols // n
    return [(slice(0, rows), slice(i * w, (i + 1) * w)) for i in range(n)]


def row_pieces(rows, cols, n):
    w = rows // n
    return [(slice(i * w, (i + 1) * w), slice(0, cols)) for i in range(n)]


IN_PIECES = col_pieces(D, 3 * D, 3)
OUT_PIECES = row_pieces(D, D, 1)
UP_PIECES = col_pieces(D, FF, NFT)
DOWN_PIECES = row_pieces(FF, D, NFT)


class Feed:
    def __init__(self):
        self.queue = []

    def weight(self, own, mine, other, piece, dst, sem):
        def issue():
            @pl.when(own)
            def _():
                pltpu.make_async_copy(mine.at[piece], dst.at[piece], sem).start()

            @pl.when(jnp.logical_not(own))
            def _():
                pltpu.make_async_copy(other.at[piece], dst.at[piece], sem).start()

        self.queue.append(issue)
        return pltpu.make_async_copy(mine.at[piece], dst.at[piece], sem)

    def plain(self, src, dst, sem):
        c = pltpu.make_async_copy(src, dst, sem)
        self.queue.append(c.start)
        return c

    def go(self, n=1):
        while n > 0 and self.queue:
            self.queue.pop(0)()
            n -= 1


class Drain:
    def __init__(self, sems):
        self.sems, self.copies = sems, []

    def put(self, src, dst):
        c = pltpu.make_async_copy(src, dst, self.sems.at[len(self.copies)])
        c.start()
        self.copies.append(c)
        return c

    def finish(self, skip=()):
        for c in self.copies:
            if not any(c is done for done in skip):
                c.wait()


def make_mask(mask, seqs, scal):
    for s in range(seqs):
        keep = open_keys_t(scal[1 + scal[0] * seqs + s])
        shut = jnp.where(keep, 0.0, 1.0)
        mask[s, :, 0:SLOTS] = shut
        mask[s, :, SLOTS : 2 * SLOTS] = shut


def pair_tile(ref, rows, part, p):
    lo = part * D + p * LANES
    return ref[rows, lo : lo + LANES]


def both_heads(v):
    left = lax.broadcasted_iota(jnp.int32, (SLOTS, LANES), 1) < HEAD
    zero = jnp.zeros((SLOTS, LANES), BF16)
    return jnp.concatenate([jnp.where(left, v, zero), jnp.where(left, zero, v)], axis=0)


def norm_into(dst, source, gain, bias):
    centered, scale = norm_stats(source)
    dst[...] = (centered * scale * gain + bias).astype(BF16)


def project(seqs, normed, w_in, waits, rot_ref, qkv, feed):
    cos, sin = rot_ref[0], rot_ref[1]
    for part in range(3):
        waits[part].wait()
        for tile in range(D // 256):
            lo = part * D + tile * 256
            val = dot(normed[...], w_in[:, lo : lo + 256])
            if part == 2:
                qkv[:, lo : lo + 256] = val.astype(BF16)
                continue
            for u in range(2):
                for s in range(seqs):
                    v = val[s * SLOTS : (s + 1) * SLOTS, u * LANES : (u + 1) * LANES]
                    v = v * cos + swap_halves(v) * sin
                    if part == 0:
                        v = v * HEAD ** (-0.5)
                    qkv[
                        s * SLOTS : (s + 1) * SLOTS, lo + u * LANES : lo + (u + 1) * LANES
                    ] = v.astype(BF16)


def attend(seqs, qkv, mask, scores, probs, mixed):
    for s in range(seqs):
        rows = slice(s * SLOTS, (s + 1) * SLOTS)
        for p in range(PAIRS):
            scores[s * PAIRS + p] = dot(
                pair_tile(qkv, rows, 1, p), both_heads(pair_tile(qkv, rows, 0, p)), 1, 1
            )
        for p in range(PAIRS):
            i = s * PAIRS + p
            st = jnp.where(mask[s] > 0.5, masked_score, scores[i])
            e = jnp.exp(st - jnp.max(st, axis=0, keepdims=True))
            low = (e * (1.0 / jnp.sum(e, axis=0, keepdims=True))).astype(BF16)
            probs[i, 0:SLOTS] = low[:, :SLOTS]
            probs[i, SLOTS : 2 * SLOTS] = low[:, SLOTS:]
        for p in range(PAIRS):
            mixed[rows, p * LANES : (p + 1) * LANES] = dot(
                probs[s * PAIRS + p], both_heads(pair_tile(qkv, rows, 2, p)), 0, 0
            ).astype(BF16)


def activate(dense, w_up, slope, active, waits, ready, feed):
    for t in range(FF // 256):
        if t * 256 % FT == 0:
            waits[t * 256 // FT].wait()
        cols = slice(t * 256, (t + 1) * 256)
        u = dot(dense[...], w_up[:, cols])
        u2 = u * u
        th = jnp.tanh(u * (gelu_c + (gelu_c * gelu_a) * u2))
        h = 0.5 * (1.0 + th)
        active[:, cols] = (u * h).astype(BF16)
        slope[:, cols] = (
            h + u * (1.0 - th * th) * (0.5 * gelu_c + (1.5 * gelu_c * gelu_a) * u2)
        ).astype(BF16)
        if (t + 1) * 256 % FT == 0:
            ready(t * 256 // FT)


def open_kernel(seqs, scal, x_ref, vec_mine, vec_other, rot_ref, in_mine, in_other,
                normed_o, mixed_o, qkv_o, probs_o,
                normed, mixed, qkv, scores, probs, w_in, mask, sems, out_sems):
    own = scal[0] == 0
    feed, drain = Feed(), Drain(out_sems)
    w_waits = [feed.weight(own, in_mine, in_other, IN_PIECES[i], w_in, sems.at[i]) for i in range(3)]
    feed.go(3)
    vec = jnp.where(own, vec_mine[...], vec_other[...])
    norm_into(normed, x_ref[...].astype(F32), vec[0:1], vec[1:2])
    drain.put(normed, normed_o)
    make_mask(mask, seqs, scal)
    project(seqs, normed, w_in, w_waits, rot_ref, qkv, feed)
    drain.put(qkv, qkv_o)
    attend(seqs, qkv, mask, scores, probs, mixed)
    drain.put(probs, probs_o)
    drain.put(mixed, mixed_o)
    drain.finish()


def ff_back(r_ref, hidden, gain, w_up, w_down, w_out, slope, ug, bgrad, hgrad, mgrad, vgrad, waits, drain, outs):
    tile_waits, up_waits, out_wait = waits
    ug_o, bgrad_o = outs
    for t in range(FF // 256):
        i = t * 256 // FT
        if t * 256 % FT == 0:
            for c in tile_waits[i]:
                c.wait()
        cols = slice(t * 256, (t + 1) * 256)
        ug[:, cols] = (dot(r_ref[...], w_down[cols, :], 1, 1) * slope[:, cols].astype(F32)).astype(BF16)
        if (t + 1) * 256 % FT == 0:
            done = slice(i * FT, (i + 1) * FT)
            drain.put(ug.at[:, done], ug_o.at[:, done])
    for c in up_waits:
        c.wait()
    part, dg, db = norm_back(dot(ug[...], w_up[...], 1, 1), hidden[...], gain)
    vgrad[2:3] = dg
    vgrad[3:4] = db
    total = r_ref[...].astype(F32) + part
    hgrad[...] = total
    bgrad[...] = total.astype(BF16)
    drain.put(bgrad, bgrad_o)
    for c in out_wait:
        c.wait()
    mgrad[...] = dot(bgrad[...], w_out[...], 1, 1).astype(BF16)


def attn_back(seqs, x_ref, gain, rot_ref, w_in, qkv, probs, dpt, mgrad, hgrad, pgrad, xgrad, vgrad, waits, drain, outs):
    in_waits, w_waits = waits
    pgrad_o, xgrad_o = outs
    cos, sin = rot_ref[0], rot_ref[1]
    for c in in_waits:
        c.wait()
    for s in range(seqs):
        rows = slice(s * SLOTS, (s + 1) * SLOTS)
        for p in range(PAIRS):
            dm = both_heads(mgrad[rows, p * LANES : (p + 1) * LANES])
            dpt[p] = dot(pair_tile(qkv, rows, 2, p), dm, 1, 1)
        for p in range(PAIRS):
            i = s * PAIRS + p
            low = jnp.concatenate([probs[i, 0:SLOTS], probs[i, SLOTS : 2 * SLOTS]], axis=1)
            pt = low.astype(F32)
            pd = pt * dpt[p]
            dst = (pd - pt * jnp.sum(pd, axis=0, keepdims=True)).astype(BF16)
            dm = both_heads(mgrad[rows, p * LANES : (p + 1) * LANES])
            dv = dot(low, dm)
            dk = dot(dst, both_heads(pair_tile(qkv, rows, 0, p)))
            stacked = jnp.concatenate([dst[:, :SLOTS], dst[:, SLOTS:]], axis=0)
            dq = dot(stacked, both_heads(pair_tile(qkv, rows, 1, p)), 0, 0) * HEAD ** (-0.5)
            dq = dq * cos - swap_halves(dq) * sin
            dk = dk * cos - swap_halves(dk) * sin
            pgrad[rows, p * LANES : (p + 1) * LANES] = dq.astype(BF16)
            pgrad[rows, D + p * LANES : D + (p + 1) * LANES] = dk.astype(BF16)
            pgrad[rows, 2 * D + p * LANES : 2 * D + (p + 1) * LANES] = dv.astype(BF16)
        drain.put(pgrad.at[rows], pgrad_o.at[rows])
    for c in w_waits:
        c.wait()
    part, dg, db = norm_back(dot(pgrad[...], w_in[...], 1, 1), x_ref[...].astype(F32), gain)
    vgrad[0:1] = dg
    vgrad[1:2] = db
    xgrad[...] = (hgrad[...] + part).astype(BF16)
    drain.put(xgrad, xgrad_o)


def middle_kernel(seqs, scal, x_ref, cot_ref, mixed0, vec_mine, vec_other, rot_ref,
                  in_mine, in_other, out_mine, out_other, up_mine, up_other, down_mine, down_other,
                  dense0_o, hidden0_o, slope0_o, active0_o, y0_o,
                  normed1_o, mixed1_o, dense1_o, active1_o, y1_o, ug1_o, bgrad1_o, pgrad1_o, xgrad1_o, vgrad_ref,
                  w_in, w_out0, w_out1, w_up0, w_up1, w_down0, w_down1,
                  dense, hidden, slope, active, y, normed, mixed, qkv, scores, probs, mask,
                  ug, bgrad, hgrad, mgrad, pgrad, xgrad,
                  in_sems, out_sems, up_sems, down_sems, drain_sems):
    own = scal[0] == 0
    not_own = jnp.logical_not(own)
    feed, drain = Feed(), Drain(drain_sems)

    def weights(layer, mine_too, w_out, w_up, w_down):
        out = feed.weight(mine_too, out_mine, out_other, OUT_PIECES[0], w_out, out_sems.at[layer])
        up = [
            feed.weight(mine_too, up_mine, up_other, UP_PIECES[i], w_up, up_sems.at[layer * NFT + i])
            for i in range(NFT)
        ]
        down = [
            feed.weight(mine_too, down_mine, down_other, DOWN_PIECES[i], w_down, down_sems.at[layer * NFT + i])
            for i in range(NFT)
        ]
        return out, up, down

    waits0 = weights(0, own, w_out0, w_up0, w_down0)
    in_waits = [feed.weight(not_own, in_mine, in_other, IN_PIECES[i], w_in, in_sems.at[i]) for i in range(3)]
    waits1 = weights(1, not_own, w_out1, w_up1, w_down1)
    feed.go(1 + 2 * NFT)
    vec0 = jnp.where(own, vec_mine[...], vec_other[...])
    vec1 = jnp.where(own, vec_other[...], vec_mine[...])

    def tail(layer, x, mixed_in, w_out, w_up, w_down, waits, vec, outs, held):
        dense_o, hidden_o, slope_o, active_o, y_o = outs
        waits[0].wait()
        hidden[layer] = x + dot(mixed_in[...], w_out[...])
        if hidden_o is not None:
            drain.put(hidden.at[layer], hidden_o)
        norm_into(dense.at[layer], hidden[layer], vec[2:3], vec[3:4])
        drain.put(dense.at[layer], dense_o)
        for c in held:
            c.wait()
        copies = []

        def ready(i):
            cols = slice(i * FT, (i + 1) * FT)
            if slope_o is not None:
                copies.append(drain.put(slope.at[:, cols], slope_o.at[:, cols]))
            copies.append(drain.put(active.at[:, cols], active_o.at[:, cols]))

        activate(dense.at[layer], w_up, slope, active, waits[1], ready, feed)
        for c in waits[2]:
            c.wait()
        y[layer] = (hidden[layer] + dot(active[...], w_down[...])).astype(BF16)
        drain.put(y.at[layer], y_o)
        return copies

    make_mask(mask, seqs, scal)
    copies = tail(
        0, x_ref[...].astype(F32), mixed0, w_out0, w_up0, w_down0, waits0, vec0,
        (dense0_o, hidden0_o, slope0_o, active0_o, y0_o), (),
    )
    feed.go(len(feed.queue))
    norm_into(normed, y[0].astype(F32), vec1[0:1], vec1[1:2])
    drain.put(normed, normed1_o)
    project(seqs, normed, w_in, in_waits, rot_ref, qkv, feed)
    attend(seqs, qkv, mask, scores, probs, mixed)
    drain.put(mixed, mixed1_o)
    tail(
        1, y[0].astype(F32), mixed, w_out1, w_up1, w_down1, waits1, vec1,
        (dense1_o, None, None, active1_o, y1_o), copies,
    )
    ff_back(
        cot_ref, hidden.at[1], vec1[2:3], w_up1, w_down1, w_out1, slope, ug, bgrad, hgrad, mgrad, vgrad_ref,
        ([()] * NFT, (), ()), drain, (ug1_o, bgrad1_o),
    )
    attn_back(
        seqs, y.at[0], vec1[0:1], rot_ref, w_in, qkv, probs, scores, mgrad, hgrad, pgrad, xgrad, vgrad_ref,
        ((), ()), drain, (pgrad1_o, xgrad1_o),
    )
    drain.finish(copies)


def last_kernel(seqs, scal, x_ref, r_ref, hidden_ref, vec_mine, vec_other, rot_ref, slope_ref, qkv_ref, probs_ref,
                in_mine, in_other, out_mine, out_other, up_mine, up_other, down_mine, down_other,
                ug_o, bgrad_o, pgrad_o, xgrad_o, vgrad_ref,
                w_in, w_up, w_down, w_out, slope, qkv, probs, dpt, ug, bgrad, hgrad, mgrad, pgrad, xgrad,
                sems, drain_sems):
    own = scal[0] == 0
    feed, drain = Feed(), Drain(drain_sems)
    tiles = []
    for i in range(NFT):
        cols = slice(i * FT, (i + 1) * FT)
        tiles.append(
            [
                feed.weight(own, down_mine, down_other, DOWN_PIECES[i], w_down, sems.at[i]),
                feed.plain(slope_ref.at[:, cols], slope.at[:, cols], sems.at[2 * NFT + i]),
            ]
        )
    ups = [feed.weight(own, up_mine, up_other, UP_PIECES[i], w_up, sems.at[NFT + i]) for i in range(NFT)]
    out = [feed.weight(own, out_mine, out_other, OUT_PIECES[0], w_out, sems.at[3 * NFT])]
    loads = [
        feed.plain(qkv_ref, qkv, sems.at[3 * NFT + 1]),
        feed.plain(probs_ref, probs, sems.at[3 * NFT + 2]),
    ]
    w_waits = [
        feed.weight(own, in_mine, in_other, IN_PIECES[i], w_in, sems.at[3 * NFT + 3 + i]) for i in range(3)
    ]
    feed.go(len(feed.queue))
    vec = jnp.where(own, vec_mine[...], vec_other[...])
    ff_back(
        r_ref, hidden_ref, vec[2:3], w_up, w_down, w_out, slope, ug, bgrad, hgrad, mgrad, vgrad_ref,
        (tiles, ups, out), drain, (ug_o, bgrad_o),
    )
    attn_back(
        seqs, x_ref, vec[0:1], rot_ref, w_in, qkv, probs, dpt, mgrad, hgrad, pgrad, xgrad, vgrad_ref,
        (loads, w_waits), drain, (pgrad_o, xgrad_o),
    )
    drain.finish()


def wgrad_kernel(groups, scal, *refs):
    plan = [term for group in groups for term in group]
    n, g = len(plan), len(groups)
    ins, outs, rest = refs[: 4 * n], refs[4 * n : 4 * n + 2 * g], refs[4 * n + 2 * g :]
    held, (results, staged) = rest[: 4 * n], (rest[4 * n : 4 * n + g], rest[4 * n + g : 4 * n + 2 * g])
    sems, drain_sems = rest[4 * n + 2 * g :]
    core = scal[0]
    jobs = []

    def load(src, dst):
        c = pltpu.make_async_copy(src, dst, sems.at[len(jobs)])
        c.start()
        jobs.append(c)

    for i, (rows, width, _, b_rows) in enumerate(plan):
        for j in range(2):
            tokens = held[4 * i + 2 + j].shape[0]
            at = pl.ds(pl.multiple_of(core * width, 128), width)
            row = pl.ds(pl.multiple_of(b_rows(core, j), 16), tokens)
            load(ins[4 * i + 2 + j].at[row, at], held[4 * i + 2 + j])
        for lo in range(0, rows, D):
            for j in range(2):
                load(ins[4 * i + j].at[:, lo : lo + D], held[4 * i + j].at[:, lo : lo + D])
    jobs = iter(jobs)
    drain = Drain(drain_sems)
    i = 0
    for k, group in enumerate(groups):
        res, stage, base = results[k], staged[k], 0
        for rows, width, _, _ in group:
            a0, a1, b0, b1 = held[4 * i : 4 * i + 4]
            i += 1
            next(jobs).wait()
            next(jobs).wait()
            step = 512 if width % 512 == 0 else 384
            for lo in range(0, rows, D):
                next(jobs).wait()
                next(jobs).wait()
                cut = slice(lo, lo + D)
                for c in range(0, width, step):
                    res[cut, base + c : base + c + step] = dot(a0[:, cut], b0[:, c : c + step], 0, 0) + dot(
                        a1[:, cut], b1[:, c : c + step], 0, 0
                    )
            base += width
        per, table = group[0][0] // BLOCKS, group[0][2]
        keep_o, send_o = outs[2 * k], outs[2 * k + 1]
        half = BLOCKS // 2
        for r in list(range(half, BLOCKS)) + list(range(half)):
            at = pl.multiple_of(scal[table + r] * per, per)
            stage[r] = res[pl.ds(at, per), :].astype(BF16)
            if r % 4 == 3:
                cut = slice(r - 3, r + 1)
                if r < half:
                    drain.put(stage.at[cut], keep_o.at[cut])
                else:
                    drain.put(stage.at[cut], send_o.at[slice(r - 3 - half, r + 1 - half)])
    drain.finish()


def whole(shape):
    return pl.BlockSpec(shape, lambda i, s: (0,) * len(shape))


def shape_of(shape, dtype):
    return jax.ShapeDtypeStruct(shape, dtype)


HBM = pl.BlockSpec(memory_space=pl.ANY)


class Chain:
    def __init__(self):
        self.token = ()

    def call(self, kernel, scal, ins, in_specs, outs, out_specs, scratch, micros, after=()):
        after = tuple(self.token) + tuple(after)
        n, extra = 1 + len(ins), len(after)

        def ordered(*refs):
            kernel(*refs[:n], *refs[n + extra :])

        result = pl.pallas_call(
            ordered,
            grid_spec=pltpu.PrefetchScalarGridSpec(
                num_scalar_prefetch=1,
                grid=(1,),
                in_specs=list(in_specs) + [HBM] * extra,
                out_specs=out_specs,
                scratch_shapes=scratch,
            ),
            out_shape=outs,
            compiler_params=pltpu.CompilerParams(vmem_limit_bytes=VMEM_LIMIT),
            cost_estimate=pl.CostEstimate(
                flops=int(micros * 1e9), bytes_accessed=2**20, transcendentals=0
            ),
        )(scal, *ins, *after)
        self.token = (result[-1],)
        return result


def axis_pairs(first, second, size):
    return [(i, i ^ first) for i in range(size)] + [
        (size + i, size + (i ^ second)) for i in range(size)
    ]


def body(
    tokens, cotangent, lengths, mixer_gain, mixer_bias, project_in, project_out,
    dense_gain, dense_bias, up_weight, down_weight,
):
    micro, rows = tokens.shape[:2]
    total = micro * rows
    seqs = total // 2
    t = seqs * SLOTS
    core = lax.axis_index("section")
    first = core == 0
    me = lax.axis_index("dp")
    dp = lax.axis_size("dp")
    fast = dp == BLOCKS
    both = ("section", "dp")
    chain = Chain()

    def other_core(v):
        return lax.ppermute(v, "section", [(0, 1), (1, 0)])

    mine = {
        "vec": jnp.concatenate([mixer_gain, mixer_bias, dense_gain, dense_bias], axis=0),
        "in": project_in[0],
        "out": project_out[0],
        "up": up_weight[0],
        "down": down_weight[0],
    }
    other = {name: other_core(mine[name]) for name in ("vec", "in")}
    other["in"], out_held, up_held, down_held = lax.optimization_barrier(
        (other["in"], mine["out"], mine["up"], mine["down"])
    )
    other["out"], other["up"], other["down"] = map(other_core, (out_held, up_held, down_held))
    rot = jnp.asarray(rotary_tables())
    scal = jnp.concatenate([core.reshape(1), lengths.reshape(total)]).astype(jnp.int32)

    xy_bits = ((1, 2), (2, 1), (4, 4), (8, 8))
    z_bits = ((4, 4), (8, 8), (1, 2), (2, 1))

    def places(bits):
        if not fast:
            return jnp.asarray(np.arange(BLOCKS), jnp.int32)
        rel = np.zeros((2, BLOCKS), np.int32)
        for c in range(2):
            for r in range(BLOCKS):
                for stage in range(4):
                    if r >> (3 - stage) & 1:
                        rel[c, r] ^= bits[stage][c]
        return me ^ jnp.where(first, jnp.asarray(rel[0]), jnp.asarray(rel[1]))

    order = jnp.concatenate([core.reshape(1), places(xy_bits), places(z_bits)]).astype(jnp.int32)
    xy_table, z_table = 1, 1 + BLOCKS

    class Batch:
        def __init__(self, pair, bits):
            self.keep, self.send = pair
            self.bits, self.stage, self.result = bits, 0, None
            if not fast:
                per, width = self.keep.shape[1:]
                flat = jnp.concatenate(pair, axis=0).reshape(BLOCKS * per, width)
                self.result = lax.psum_scatter(flat.astype(F32), "dp", scatter_dimension=0, tiled=True)
            else:
                self.start()

        def start(self):
            self.got = lax.ppermute(self.send, both, axis_pairs(*self.bits[self.stage], dp))
            self.stage += 1

        def advance(self):
            half = self.keep.shape[0] // 2
            if half == 0:
                self.result = self.keep[0].astype(F32) + self.got[0].astype(F32)
                return self.result
            self.send, self.keep = self.keep[half:] + self.got[half:], self.keep[:half] + self.got[:half]
            return self.send

    class Vector:
        def __init__(self, value):
            self.value, self.stage, self.result = value, 0, None
            if not fast:
                self.result = lax.psum(value, both)
            else:
                self.got = other_core(value)

        def held(self):
            return [self.value, self.got]

        def start(self):
            self.got = lax.ppermute(self.value, both, axis_pairs(*xy_bits[self.stage], dp))
            self.stage += 1

        def advance(self):
            self.value = self.value + self.got
            if self.stage == 4:
                self.result = self.value
            return self.value

    def tick(*batches):
        batches = [b for b in batches if b.result is None]
        if not batches:
            return
        held = []
        for b in batches:
            held += [b.value, b.got] if isinstance(b, Vector) else [b.keep, b.got]
        held = lax.optimization_barrier(tuple(held) + tuple(chain.token))
        tokens_out = []
        for i, b in enumerate(batches):
            if isinstance(b, Vector):
                b.value, b.got = held[2 * i], held[2 * i + 1]
            else:
                b.keep, b.got = held[2 * i], held[2 * i + 1]
            tokens_out.append(b.advance())
        for b in batches:
            if b.result is None:
                b.start()
        chain.token = tuple(tokens_out)

    x0 = tokens.reshape(total * SLOTS, D)
    cot = cotangent.reshape(total * SLOTS, D)
    half_spec = pl.BlockSpec((t, D), lambda i, s: (s[0], 0))
    tok = whole((t, D))
    vec_spec, rot_spec = whole((4, D)), whole((2, SLOTS, LANES))
    scores_shape = (seqs * PAIRS, SLOTS, 2 * SLOTS)
    probs_shape = (seqs * PAIRS, 2 * SLOTS, SLOTS)
    vmem, dma = pltpu.VMEM, pltpu.SemaphoreType.DMA
    vecs = (mine["vec"], other["vec"], rot)
    vec_specs = [vec_spec, vec_spec, rot_spec]
    weights = (
        mine["in"], other["in"], mine["out"], other["out"],
        mine["up"], other["up"], mine["down"], other["down"],
    )
    row16, row32, wide16 = shape_of((t, D), BF16), shape_of((t, D), F32), shape_of((t, FF), BF16)
    three16 = shape_of((t, 3 * D), BF16)
    small = vmem((t, D), BF16)
    wide = vmem((t, FF), BF16)
    three = vmem((t, 3 * D), BF16)
    probs_mem, scores_mem = vmem(probs_shape, BF16), vmem(scores_shape, F32)
    mask_mem = vmem((seqs, SLOTS, 2 * SLOTS), F32)
    mem_in, mem_out, mem_up, mem_down = (
        vmem((D, 3 * D), BF16), vmem((D, D), BF16), vmem((D, FF), BF16), vmem((FF, D), BF16),
    )

    normed0, mixed0, qkv0, probs0 = chain.call(
        functools.partial(open_kernel, seqs), scal,
        (x0,) + vecs + weights[:2],
        [half_spec] + vec_specs + [HBM] * 2,
        [row16, row16, three16, shape_of(probs_shape, BF16)],
        [HBM] * 4,
        [small, small, three, scores_mem, probs_mem, mem_in, mask_mem, dma((3,)), dma((4,))],
        8.0,
    )
    (dense0, hidden0, slope0, active0, y0,
     normed1, mixed1, dense1, active1, y1, ug1, bgrad1, pgrad1, xgrad1, vgrad1) = chain.call(
        functools.partial(middle_kernel, seqs), scal,
        (x0, cot, mixed0) + vecs + weights,
        [half_spec, half_spec, tok] + vec_specs + [HBM] * 8,
        [row16, row32, wide16, wide16, row16,
         row16, row16, row16, wide16, row16, wide16, row16, three16, row16, shape_of((4, D), F32)],
        [HBM] * 14 + [whole((4, D))],
        [mem_in, mem_out, mem_out, mem_up, mem_up, mem_down, mem_down,
         vmem((2, t, D), BF16), vmem((2, t, D), F32), wide, wide, vmem((2, t, D), BF16), small, small, three,
         scores_mem, probs_mem, mask_mem, wide, small, vmem((t, D), F32), small, three, small,
         dma((3,)), dma((2,)), dma((2 * NFT,)), dma((2 * NFT,)), dma((10 + 4 * NFT + seqs,))],
        30.0,
    )
    saved = [
        dict(normed=normed0, mixed=mixed0, dense=dense0, active=active0),
        dict(normed=normed1, mixed=mixed1, dense=dense1, active=active1),
    ]
    theirs = [{k: other_core(v) for k, v in layer.items()} for layer in saved]
    half_in = 3 * D // 2

    def start_row(core, j):
        return 0

    def cot_row(core, j):
        return jnp.where(core == j, 0, 1) * t

    def wgrads(i, ug, bgrad, pgrad, r, r_rows, attn_table):
        ug_pair, bgrad_pair, pgrad_pair = ((v, other_core(v)) for v in (ug, bgrad, pgrad))
        acts = {k: (saved[i][k], theirs[i][k]) for k in saved[i]}
        groups = [
            [(FF, D // 2, xy_table, r_rows)],
            [(D, FF // 2, xy_table, start_row)],
            [(D, half_in, attn_table, start_row), (D, D // 2, attn_table, start_row)],
        ]
        ins = acts["active"] + r + acts["dense"] + ug_pair + acts["normed"] + pgrad_pair + acts["mixed"] + bgrad_pair
        outs, held, results, staged, jobs = [], [], [], [], 0
        for group in groups:
            rows, width = group[0][0], sum(term[1] for term in group)
            per = rows // BLOCKS
            outs += [shape_of((BLOCKS // 2, per, width), BF16)] * 2
            results.append(vmem((rows, width), F32))
            staged.append(vmem((BLOCKS, per, width), BF16))
            for term in group:
                held += [vmem((t, term[0]), BF16)] * 2 + [vmem((t, term[1]), BF16)] * 2
                jobs += 2 + 2 * (term[0] // D)
        res = chain.call(
            functools.partial(wgrad_kernel, groups), order, ins, [HBM] * len(ins), outs, [HBM] * len(outs),
            held + results + staged + [dma((jobs,)), dma((4 * len(groups),))], 10.0,
        )
        return res[0:2], res[2:4], res[4:6]

    pairs = wgrads(1, ug1, bgrad1, pgrad1, (cot, cot), cot_row, z_table)
    down1, up1, attn1 = (Batch(p, b) for p, b in zip(pairs, (xy_bits, xy_bits, z_bits)))
    xgrad1_o = other_core(xgrad1)
    ug0, bgrad0, pgrad0, xgrad0, vgrad0 = chain.call(
        functools.partial(last_kernel, seqs), scal,
        (x0, xgrad1, hidden0) + vecs + (slope0, qkv0, probs0) + weights,
        [half_spec, tok, tok] + vec_specs + [HBM] * 11,
        [wide16, row16, three16, row16, shape_of((4, D), F32)],
        [HBM] * 4 + [whole((4, D))],
        [mem_in, mem_up, mem_down, mem_out, wide, three, probs_mem, vmem((PAIRS, SLOTS, 2 * SLOTS), F32),
         wide, small, vmem((t, D), F32), small, three, small, dma((3 * NFT + 6,)), dma((NFT + 2 + seqs,))],
        14.0,
    )
    tick(down1)
    pairs = wgrads(0, ug0, bgrad0, pgrad0, (xgrad1, xgrad1_o), start_row, xy_table)
    down0, up0, attn0 = (Batch(p, xy_bits) for p in pairs)
    vec_sum = Vector(jnp.concatenate([vgrad0, vgrad1], axis=0))
    tick(up1, attn1, vec_sum)
    tick(down1)
    tick(down0)
    tick(up1, up0)
    tick(attn0, attn1, vec_sum)
    tick(down0, down1)
    tick(up1, up0, attn1)
    tick(down0, attn0)
    tick(up1, up0, vec_sum)
    tick(down0, attn1, attn0)
    tick(up0, vec_sum)
    tick(attn0, vec_sum)
    for _ in range(4):
        tick(down1, up1, attn1, down0, up0, attn0, vec_sum)
    ys, xgrads = [y0, y1], [xgrad0, xgrad1]
    shards = [
        (a.result[:, :half_in], a.result[:, half_in:], u.result, d.result)
        for a, u, d in ((attn0, up0, down0), (attn1, up1, down1))
    ]

    def settle(a, b):
        here = jnp.where(first, a, b)
        there = other_core(jnp.where(first, b, a))
        return jnp.where(first, jnp.concatenate([here, there], -1), jnp.concatenate([there, here], -1))

    grad_in, grad_out, grad_up, grad_down = (
        settle(a, b)[None] for a, b in zip(shards[0], shards[1])
    )

    def settle_rows(pair):
        here = jnp.where(first, pair[0], pair[1])
        there = other_core(jnp.where(first, pair[1], pair[0]))
        whole_rows = jnp.where(
            first, jnp.concatenate([here, there], 0), jnp.concatenate([there, here], 0)
        )
        return whole_rows.reshape((1,) + tokens.shape)

    layer_out = settle_rows(ys)
    input_grads = settle_rows(xgrads)

    vec = vec_sum.result
    vec = jnp.where(first, vec[:4], vec[4:])
    per = D // dp
    vec = lax.dynamic_slice(vec, (0, me * per), (4, per))
    return (
        layer_out,
        input_grads,
        vec[0:1],
        vec[1:2],
        grad_in,
        grad_out,
        vec[2:3],
        vec[3:4],
        grad_up,
        grad_down,
    )


def solution(mesh):
    row = P(None, "dp", None, None)
    vec = P("section", None)
    mat = P("section", None, None)
    outs = P("section", None, "dp", None, None)
    out_vec = P("section", "dp")
    out_mat = P("section", "dp", None)
    return jax.shard_map(
        body,
        mesh=mesh,
        in_specs=(row, row, P(None, "dp"), vec, vec, mat, mat, vec, vec, mat, mat),
        out_specs=(outs, outs, out_vec, out_vec, out_mat, out_mat, out_vec, out_vec, out_mat, out_mat),
        check_vma=False,
    )
```

```python
import functools
import math

import jax
import jax.numpy as jnp
import numpy as np
from jax import lax
from jax.experimental import pallas as pl
from jax.experimental.pallas import tpu as pltpu
from jax.sharding import PartitionSpec as P

D = 768
HEADS = 12
HEAD = 64
FF = 3072
BLK = 16
SEQ = 64
SLOTS = 2 * SEQ
PAIRS = HEADS // 2
LANES = 2 * HEAD
BLOCKS = 16
FT = 1536
NFT = FF // FT

norm_eps = 1e-05
masked_score = -1000000000.0
gelu_c = math.sqrt(2.0 / math.pi)
gelu_a = 0.044715

F32 = jnp.float32
BF16 = jnp.bfloat16
VMEM_LIMIT = 60 * 1024 * 1024


def dot(a, b, ca=1, cb=0):
    return lax.dot_general(a, b, (((ca,), (cb,)), ((), ())), preferred_element_type=F32)


def rotary_tables():
    places = (np.arange(SLOTS) % SEQ).astype(np.float32)
    half = HEAD // 2
    freqs = (10000.0 ** (-np.arange(half).astype(np.float32) * 2.0 / HEAD)).astype(np.float32)
    angles = (places[:, None] * freqs[None, :]).astype(np.float32)
    cos, sin = np.cos(angles), np.sin(angles)
    return np.stack(
        [
            np.concatenate([cos] * 4, axis=1),
            np.concatenate([-sin, sin, -sin, sin], axis=1),
        ]
    ).astype(np.float32)


def swap_halves(v):
    lane = lax.broadcasted_iota(jnp.int32, v.shape, 1)
    first = lax.rem(lane, HEAD) < HEAD // 2
    return jnp.where(first, pltpu.roll(v, LANES - 32, 1), pltpu.roll(v, 32, 1))


def open_keys_t(length):
    key = lax.broadcasted_iota(jnp.int32, (SLOTS, SLOTS), 0)
    query = lax.broadcasted_iota(jnp.int32, (SLOTS, SLOTS), 1)
    key_clean, query_clean = key >= SEQ, query >= SEQ
    key_place, query_place = lax.rem(key, SEQ), lax.rem(query, SEQ)
    kb, qb = lax.div(key_place, BLK), lax.div(query_place, BLK)
    both_noisy = jnp.logical_and(jnp.logical_not(key_clean), jnp.logical_not(query_clean))
    both_clean = jnp.logical_and(key_clean, query_clean)
    crossed = jnp.logical_and(key_clean, jnp.logical_not(query_clean))
    structure = (
        (both_noisy & (kb == qb)) | (crossed & (kb < qb)) | (both_clean & (kb <= qb))
    )
    return structure & ((key_place < length) | (key == query))


def norm_stats(v):
    centered = v - jnp.mean(v, axis=-1, keepdims=True)
    spread = jnp.mean(centered * centered, axis=-1, keepdims=True)
    return centered, lax.rsqrt(spread + norm_eps)


def norm_back(dy, source, gain):
    centered, scale = norm_stats(source)
    xhat = centered * scale
    g = dy * gain
    part = scale * (
        g
        - jnp.mean(g, axis=-1, keepdims=True)
        - xhat * jnp.mean(g * xhat, axis=-1, keepdims=True)
    )
    return part, jnp.sum(dy * xhat, axis=0, keepdims=True), jnp.sum(dy, axis=0, keepdims=True)


def col_pieces(rows, cols, n):
    w = cols // n
    return [(slice(0, rows), slice(i * w, (i + 1) * w)) for i in range(n)]


def row_pieces(rows, cols, n):
    w = rows // n
    return [(slice(i * w, (i + 1) * w), slice(0, cols)) for i in range(n)]


IN_PIECES = col_pieces(D, 3 * D, 3)
IN_ALL = col_pieces(D, 3 * D, 1)
OUT_PIECES = row_pieces(D, D, 1)
UP_PIECES = col_pieces(D, FF, NFT)
DOWN_PIECES = row_pieces(FF, D, 1)


class Feed:
    def __init__(self, own):
        self.own, self.queue = own, []

    def weight(self, mine, other, piece, dst, sem):
        self.queue.append((mine, other, piece, dst, sem))
        return pltpu.make_async_copy(mine.at[piece], dst.at[piece], sem)

    def begin(self, count=None):
        count = len(self.queue) if count is None else count
        queue, self.queue = self.queue[:count], self.queue[count:]

        @pl.when(self.own)
        def _():
            for mine, _, piece, dst, sem in queue:
                pltpu.make_async_copy(mine.at[piece], dst.at[piece], sem).start()

        @pl.when(jnp.logical_not(self.own))
        def _():
            for _, other, piece, dst, sem in queue:
                pltpu.make_async_copy(other.at[piece], dst.at[piece], sem).start()


class Drain:
    def __init__(self, sems):
        self.sems, self.copies = sems, []

    def put(self, src, dst):
        c = pltpu.make_async_copy(src, dst, self.sems.at[len(self.copies)])
        c.start()
        self.copies.append(c)
        return c

    def finish(self, skip=()):
        for c in self.copies:
            if not any(c is done for done in skip):
                c.wait()


def make_mask(mask, seqs, scal):
    for s in range(seqs):
        keep = open_keys_t(scal[1 + scal[0] * seqs + s])
        shut = jnp.where(keep, 0.0, 1.0)
        mask[s, :, 0:SLOTS] = shut
        mask[s, :, SLOTS : 2 * SLOTS] = shut


def pair_tile(ref, rows, part, p):
    lo = part * D + p * LANES
    return ref[rows, lo : lo + LANES]


def both_heads(v):
    left = lax.broadcasted_iota(jnp.int32, (SLOTS, LANES), 1) < HEAD
    zero = jnp.zeros((SLOTS, LANES), BF16)
    return jnp.concatenate([jnp.where(left, v, zero), jnp.where(left, zero, v)], axis=0)


def norm_into(dst, source, gain, bias):
    centered, scale = norm_stats(source)
    dst[...] = (centered * scale * gain + bias).astype(BF16)


def project(seqs, normed, w_in, waits, rot_ref, qkv):
    cos, sin = rot_ref[0], rot_ref[1]
    for part in range(3):
        if part < len(waits):
            waits[part].wait()
        for tile in range(D // 256):
            lo = part * D + tile * 256
            val = dot(normed[...], w_in[:, lo : lo + 256])
            if part == 2:
                qkv[:, lo : lo + 256] = val.astype(BF16)
                continue
            for u in range(2):
                for s in range(seqs):
                    v = val[s * SLOTS : (s + 1) * SLOTS, u * LANES : (u + 1) * LANES]
                    v = v * cos + swap_halves(v) * sin
                    if part == 0:
                        v = v * HEAD ** (-0.5)
                    qkv[
                        s * SLOTS : (s + 1) * SLOTS, lo + u * LANES : lo + (u + 1) * LANES
                    ] = v.astype(BF16)


def attend(seqs, qkv, mask, scores, probs, mixed):
    for s in range(seqs):
        rows = slice(s * SLOTS, (s + 1) * SLOTS)
        for p in range(PAIRS):
            scores[s * PAIRS + p] = dot(
                pair_tile(qkv, rows, 1, p), both_heads(pair_tile(qkv, rows, 0, p)), 1, 1
            )
        for p in range(PAIRS):
            i = s * PAIRS + p
            st = jnp.where(mask[s] > 0.5, masked_score, scores[i])
            e = jnp.exp(st - jnp.max(st, axis=0, keepdims=True))
            low = (e * (1.0 / jnp.sum(e, axis=0, keepdims=True))).astype(BF16)
            probs[i, 0:SLOTS] = low[:, :SLOTS]
            probs[i, SLOTS : 2 * SLOTS] = low[:, SLOTS:]
        for p in range(PAIRS):
            mixed[rows, p * LANES : (p + 1) * LANES] = dot(
                probs[s * PAIRS + p], both_heads(pair_tile(qkv, rows, 2, p)), 0, 0
            ).astype(BF16)


def activate(dense, w_up, slope, active, waits):
    for t in range(FF // 256):
        if t * 256 % FT == 0:
            waits[t * 256 // FT].wait()
        cols = slice(t * 256, (t + 1) * 256)
        u = dot(dense[...], w_up[:, cols])
        u2 = u * u
        th = jnp.tanh(u * (gelu_c + (gelu_c * gelu_a) * u2))
        h = 0.5 * (1.0 + th)
        active[:, cols] = (u * h).astype(BF16)
        slope[:, cols] = (
            h + u * (1.0 - th * th) * (0.5 * gelu_c + (1.5 * gelu_c * gelu_a) * u2)
        ).astype(BF16)


def open_kernel(seqs, scal, x_ref, vec_mine, vec_other, rot_ref, in_mine, in_other,
                acts_o, qkv_o, probs_o,
                acts, qkv, scores, probs, w_in, mask, sems, out_sems):
    own = scal[0] == 0
    feed, drain = Feed(own), Drain(out_sems)
    w_waits = [feed.weight(in_mine, in_other, IN_PIECES[i], w_in, sems.at[i]) for i in range(3)]
    feed.begin()
    vec = jnp.where(own, vec_mine[...], vec_other[...])
    normed, mixed = acts.at[:, 0:D], acts.at[:, D : 2 * D]
    norm_into(normed, x_ref[...].astype(F32), vec[0:1], vec[1:2])
    make_mask(mask, seqs, scal)
    project(seqs, normed, w_in, w_waits, rot_ref, qkv)
    drain.put(qkv, qkv_o)
    attend(seqs, qkv, mask, scores, probs, mixed)
    drain.put(probs, probs_o)
    drain.put(acts, acts_o)
    drain.finish()


def halves(core, width):
    keep = pl.ds(pl.multiple_of(core * width, 128), width)
    send = pl.ds(pl.multiple_of((1 - core) * width, 128), width)
    return keep, send


def split_out(drain, core, src, width, at, keep_o, send_o, send_base):
    keep, send = halves(core, width)
    drain.put(src.at[:, keep], keep_o.at[:, at : at + width])
    drain.put(src.at[:, send], send_o.at[:, send_base + at : send_base + at + width])


def ff_back(r_ref, hidden, gain, w_up, w_down, w_out, slope, ug, bgrad, hgrad, mgrad, vgrad, waits):
    down_waits, up_waits, out_waits = waits
    for c in down_waits:
        c.wait()
    for t in range(FF // 256):
        cols = slice(t * 256, (t + 1) * 256)
        ug[:, cols] = (dot(r_ref[...], w_down[cols, :], 1, 1) * slope[:, cols].astype(F32)).astype(BF16)
    for c in up_waits:
        c.wait()
    part, dg, db = norm_back(dot(ug[...], w_up[...], 1, 1), hidden[...], gain)
    vgrad[2:3] = dg
    vgrad[3:4] = db
    total = r_ref[...].astype(F32) + part
    hgrad[...] = total
    bgrad[...] = total.astype(BF16)
    for c in out_waits:
        c.wait()
    mgrad[...] = dot(bgrad[...], w_out[...], 1, 1).astype(BF16)


def attn_back(seqs, x_ref, gain, rot_ref, w_in, qkv, probs, dpt, mgrad, hgrad, pgrad, xgrad, vgrad, waits):
    in_waits, w_waits = waits
    cos, sin = rot_ref[0], rot_ref[1]
    for c in in_waits:
        c.wait()
    for s in range(seqs):
        rows = slice(s * SLOTS, (s + 1) * SLOTS)
        for p in range(PAIRS):
            dm = both_heads(mgrad[rows, p * LANES : (p + 1) * LANES])
            dpt[p] = dot(pair_tile(qkv, rows, 2, p), dm, 1, 1)
        for p in range(PAIRS):
            i = s * PAIRS + p
            low = jnp.concatenate([probs[i, 0:SLOTS], probs[i, SLOTS : 2 * SLOTS]], axis=1)
            pt = low.astype(F32)
            pd = pt * dpt[p]
            dst = (pd - pt * jnp.sum(pd, axis=0, keepdims=True)).astype(BF16)
            dm = both_heads(mgrad[rows, p * LANES : (p + 1) * LANES])
            dv = dot(low, dm)
            dk = dot(dst, both_heads(pair_tile(qkv, rows, 0, p)))
            stacked = jnp.concatenate([dst[:, :SLOTS], dst[:, SLOTS:]], axis=0)
            dq = dot(stacked, both_heads(pair_tile(qkv, rows, 1, p)), 0, 0) * HEAD ** (-0.5)
            dq = dq * cos - swap_halves(dq) * sin
            dk = dk * cos - swap_halves(dk) * sin
            pgrad[rows, p * LANES : (p + 1) * LANES] = dq.astype(BF16)
            pgrad[rows, D + p * LANES : D + (p + 1) * LANES] = dk.astype(BF16)
            pgrad[rows, 2 * D + p * LANES : 2 * D + (p + 1) * LANES] = dv.astype(BF16)
    for c in w_waits:
        c.wait()
    part, dg, db = norm_back(dot(pgrad[...], w_in[...], 1, 1), x_ref[...].astype(F32), gain)
    vgrad[0:1] = dg
    vgrad[1:2] = db
    xgrad[...] = (hgrad[...] + part).astype(BF16)


ACTIVE_AT, DENSE_AT, NORMED_AT, MIXED_AT = 0, FF, FF + D, FF + 2 * D
HALF_IN, HALF_OUT, HALF_UP = 3 * D // 2, D // 2, FF // 2
UG_AT, PG_AT, BG_AT = 0, HALF_UP, HALF_UP + HALF_IN
GRAD_COLS = HALF_UP + HALF_IN + HALF_OUT


def middle_kernel(seqs, scal, x_ref, cot_ref, acts0, vec_mine, vec_other, rot_ref,
                  in_mine, in_other, out_mine, out_other, up_mine, up_other, down_mine, down_other,
                  ff0_o, hidden0_o, slope0_o, y0_o, send1_o, keep1_o, y1_o, xgrad1_o, vgrad_ref,
                  w_in, w_out0, w_out1, w_up0, w_up1, w_down0, w_down1,
                  dense, hidden, slope, active, y, normed, mixed, qkv, scores, probs, mask,
                  ug, bgrad, hgrad, mgrad, pgrad, xgrad, sems, drain_sems):
    core = scal[0]
    own = core == 0
    drain = Drain(drain_sems)

    def weights(feed, base, w_out, w_up, w_down):
        out = feed.weight(out_mine, out_other, OUT_PIECES[0], w_out, sems.at[base])
        up = [feed.weight(up_mine, up_other, UP_PIECES[i], w_up, sems.at[base + 1 + i]) for i in range(NFT)]
        down = feed.weight(down_mine, down_other, DOWN_PIECES[0], w_down, sems.at[base + 1 + NFT])
        return out, up, down

    feed0, feed1 = Feed(own), Feed(jnp.logical_not(own))
    waits0 = weights(feed0, 0, w_out0, w_up0, w_down0)
    in_waits = [feed1.weight(in_mine, in_other, IN_ALL[0], w_in, sems.at[4 + 2 * NFT])]
    waits1 = weights(feed1, 2 + NFT, w_out1, w_up1, w_down1)
    feed0.begin(1 + NFT)
    vec0 = jnp.where(own, vec_mine[...], vec_other[...])
    vec1 = jnp.where(own, vec_other[...], vec_mine[...])
    make_mask(mask, seqs, scal)

    def tail(layer, x, mixed_in, w_out, w_up, w_down, waits, vec, held, following):
        waits[0].wait()
        if layer == 0:
            feed0.begin()
        hidden[layer] = x + dot(mixed_in[...], w_out[...])
        norm_into(dense.at[layer], hidden[layer], vec[2:3], vec[3:4])
        for c in held:
            c.wait()
        activate(dense.at[layer], w_up, slope, active, waits[1])
        waits[2].wait()
        following()
        y[layer] = (hidden[layer] + dot(active[...], w_down[...])).astype(BF16)

    tail(
        0, x_ref[...].astype(F32), acts0.at[:, D : 2 * D], w_out0, w_up0, w_down0, waits0, vec0, (), feed1.begin
    )
    copies = [drain.put(slope, slope0_o), drain.put(active, ff0_o.at[:, ACTIVE_AT : ACTIVE_AT + FF])]
    drain.put(dense.at[0], ff0_o.at[:, DENSE_AT : DENSE_AT + D])
    drain.put(hidden.at[0], hidden0_o)
    drain.put(y.at[0], y0_o)
    norm_into(normed, y[0].astype(F32), vec1[0:1], vec1[1:2])
    project(seqs, normed, w_in, in_waits, rot_ref, qkv)
    attend(seqs, qkv, mask, scores, probs, mixed)
    tail(
        1, y[0].astype(F32), mixed, w_out1, w_up1, w_down1, waits1, vec1, copies, lambda: None
    )
    drain.put(active, send1_o.at[:, ACTIVE_AT : ACTIVE_AT + FF])
    drain.put(dense.at[1], send1_o.at[:, DENSE_AT : DENSE_AT + D])
    drain.put(normed, send1_o.at[:, NORMED_AT : NORMED_AT + D])
    drain.put(mixed, send1_o.at[:, MIXED_AT : MIXED_AT + D])
    drain.put(y.at[1], y1_o)
    ff_back(
        cot_ref, hidden.at[1], vec1[2:3], w_up1, w_down1, w_out1, slope, ug, bgrad, hgrad, mgrad, vgrad_ref,
        ((), (), ()),
    )
    grads_at = MIXED_AT + D
    split_out(drain, core, ug, HALF_UP, UG_AT, keep1_o, send1_o, grads_at)
    split_out(drain, core, bgrad, HALF_OUT, BG_AT, keep1_o, send1_o, grads_at)
    attn_back(
        seqs, y.at[0], vec1[0:1], rot_ref, w_in, qkv, probs, scores, mgrad, hgrad, pgrad, xgrad, vgrad_ref,
        ((), ()),
    )
    split_out(drain, core, pgrad, HALF_IN, PG_AT, keep1_o, send1_o, grads_at)
    drain.put(xgrad, xgrad1_o)
    drain.finish(copies)


def ff_last_kernel(scal, r_ref, hidden_ref, vec_mine, vec_other, slope_ref,
                   out_mine, out_other, up_mine, up_other, down_mine, down_other,
                   keep0_o, send0_o, hgrad_ref, mgrad_ref, vgrad_ref,
                   w_up, w_down, w_out, slope, ug, bgrad, sems, drain_sems):
    core = scal[0]
    own = core == 0
    feed, drain = Feed(own), Drain(drain_sems)
    downs = [feed.weight(down_mine, down_other, DOWN_PIECES[0], w_down, sems.at[0])]
    feed.begin()
    slopes = [pltpu.make_async_copy(slope_ref, slope, sems.at[1])]
    slopes[0].start()
    ups = [feed.weight(up_mine, up_other, UP_PIECES[i], w_up, sems.at[3 + i]) for i in range(NFT)]
    out = [feed.weight(out_mine, out_other, OUT_PIECES[0], w_out, sems.at[2])]
    feed.begin()
    vec = jnp.where(own, vec_mine[...], vec_other[...])
    ff_back(
        r_ref, hidden_ref, vec[2:3], w_up, w_down, w_out, slope, ug, bgrad, hgrad_ref, mgrad_ref, vgrad_ref,
        (slopes + downs, ups, out),
    )
    split_out(drain, core, ug, HALF_UP, UG_AT, keep0_o, send0_o, 0)
    split_out(drain, core, bgrad, HALF_OUT, UG_AT + HALF_UP, keep0_o, send0_o, 0)
    drain.finish()


def attn_last_kernel(seqs, scal, x_ref, mgrad_ref, hgrad_ref, vec_mine, vec_other, rot_ref, qkv_ref, probs_ref,
                     in_mine, in_other,
                     keep0_o, send0_o, xgrad_o, vgrad_ref,
                     w_in, qkv, probs, dpt, pgrad, xgrad, sems, drain_sems):
    core = scal[0]
    own = core == 0
    feed, drain = Feed(own), Drain(drain_sems)
    plain = [
        pltpu.make_async_copy(src, dst, sems.at[i])
        for i, (src, dst) in enumerate(((qkv_ref, qkv), (probs_ref, probs)))
    ]
    for c in plain:
        c.start()
    w_waits = [feed.weight(in_mine, in_other, IN_ALL[0], w_in, sems.at[2])]
    feed.begin()
    vec = jnp.where(own, vec_mine[...], vec_other[...])
    attn_back(
        seqs, x_ref, vec[0:1], rot_ref, w_in, qkv, probs, dpt, mgrad_ref, hgrad_ref, pgrad, xgrad, vgrad_ref,
        (plain, w_waits),
    )
    split_out(drain, core, pgrad, HALF_IN, 0, keep0_o, send0_o, 0)
    drain.put(xgrad, xgrad_o)
    drain.finish()


def wgrad_kernel(terms, is_ff, scal, *refs):
    n = len(terms)
    srcs, (keep_o, send_o) = refs[: 4 * n], refs[4 * n : 4 * n + 2]
    held, rest = refs[4 * n + 2 : 6 * n + 2], refs[6 * n + 2 :]
    results, (sems, drain_sems) = rest[:-2], rest[-2:]
    core = scal[0]
    loads = []
    for i, (rows, width, a_at, b_at) in enumerate(terms):
        tokens = held[2 * i].shape[0] // 2
        for j in range(2):
            mine = slice(j * tokens, (j + 1) * tokens)
            col, row = b_at[j](core)
            src = srcs[4 * i + 2 + j].at[pl.ds(row, tokens), pl.ds(col, width)]
            loads.append(pltpu.make_async_copy(src, held[2 * i + 1].at[mine], sems.at[len(loads)]))
            src = srcs[4 * i + j].at[:, a_at[j] : a_at[j] + rows]
            loads.append(pltpu.make_async_copy(src, held[2 * i].at[mine], sems.at[len(loads)]))
    for c in loads[:4]:
        c.start()
    half, per, chunk = BLOCKS // 2, D // BLOCKS, D // 2
    drain = Drain(drain_sems)

    def wait_for(i):
        for c in loads[4 * i : 4 * i + 4]:
            c.wait()
        for c in loads[4 * i + 4 : 4 * i + 8]:
            c.start()

    def send_block(r, src, at, count):
        dst = keep_o.at[r] if r < half else send_o.at[r - half]
        drain.put(src, dst.at[at : at + count])

    def side_by_side(i, res, base):
        a, b = held[2 * i], held[2 * i + 1]
        count = terms[i][1] // chunk
        for j in range(0, count, 2):
            m = min(2, count - j)
            val = dot(a[...], b[:, j * chunk : (j + m) * chunk], 0, 0).astype(BF16)
            for k in range(m):
                res[base + j + k] = val[:, k * chunk : (k + 1) * chunk].reshape(BLOCKS, per, chunk)
        return base + count

    wait_for(0)
    if is_ff:
        count = side_by_side(0, results[0], 0)
        for r in list(range(half, BLOCKS)) + list(range(half)):
            send_block(r, results[0].at[:, scal[1 + r]], 0, count)
        wait_for(1)
        a, b = held[2:4]
        deep = FF // D
        for q in range(deep):
            val = dot(a[:, q * D : (q + 1) * D], b[...], 0, 0).astype(BF16)
            results[1][q * BLOCKS : (q + 1) * BLOCKS] = val.reshape(BLOCKS, per, chunk)
        for r in list(range(half, BLOCKS)) + list(range(half)):
            send_block(r, results[1].at[pl.ds(scal[1 + r] * deep, deep)], count, deep)
    else:
        count = side_by_side(0, results[0], 0)
        wait_for(1)
        count = side_by_side(1, results[0], count)
        for r in list(range(half, BLOCKS)) + list(range(half)):
            send_block(r, results[0].at[:, scal[1 + r]], 0, count)
    drain.finish()


def whole(shape):
    return pl.BlockSpec(shape, lambda i, s: (0,) * len(shape))


def shape_of(shape, dtype):
    return jax.ShapeDtypeStruct(shape, dtype)


HBM = pl.BlockSpec(memory_space=pl.ANY)


class Chain:
    def __init__(self):
        self.token = ()

    def call(self, kernel, scal, ins, in_specs, outs, out_specs, scratch, micros, after=()):
        after = tuple(self.token) + tuple(after)
        n, extra = 1 + len(ins), len(after)

        def ordered(*refs):
            kernel(*refs[:n], *refs[n + extra :])

        result = pl.pallas_call(
            ordered,
            grid_spec=pltpu.PrefetchScalarGridSpec(
                num_scalar_prefetch=1,
                grid=(1,),
                in_specs=list(in_specs) + [HBM] * extra,
                out_specs=out_specs,
                scratch_shapes=scratch,
            ),
            out_shape=outs,
            compiler_params=pltpu.CompilerParams(vmem_limit_bytes=VMEM_LIMIT),
            cost_estimate=pl.CostEstimate(
                flops=int(micros * 1e9), bytes_accessed=2**20, transcendentals=0
            ),
        )(scal, *ins, *after)
        self.token = (result[-1],)
        return result


def axis_pairs(first, second, size):
    return [(i, i ^ first) for i in range(size)] + [
        (size + i, size + (i ^ second)) for i in range(size)
    ]


def body(
    tokens, cotangent, lengths, mixer_gain, mixer_bias, project_in, project_out,
    dense_gain, dense_bias, up_weight, down_weight,
):
    micro, rows = tokens.shape[:2]
    total = micro * rows
    seqs = total // 2
    t = seqs * SLOTS
    core = lax.axis_index("section")
    first = core == 0
    me = lax.axis_index("dp")
    dp = lax.axis_size("dp")
    fast = dp == BLOCKS
    both = ("section", "dp")
    chain = Chain()

    def other_core(v):
        return lax.ppermute(v, "section", [(0, 1), (1, 0)])

    mine = {
        "vec": jnp.concatenate([mixer_gain, mixer_bias, dense_gain, dense_bias], axis=0),
        "in": project_in[0],
        "out": project_out[0],
        "up": up_weight[0],
        "down": down_weight[0],
    }
    other = {name: other_core(mine[name]) for name in ("vec", "in")}
    other["in"], out_held, up_held, down_held = lax.optimization_barrier(
        (other["in"], mine["out"], mine["up"], mine["down"])
    )
    other["out"], other["up"], other["down"] = map(other_core, (out_held, up_held, down_held))
    rot = jnp.asarray(rotary_tables())
    scal = jnp.concatenate([core.reshape(1), lengths.reshape(total)]).astype(jnp.int32)

    xy_bits = ((1, 2), (2, 1), (4, 4), (8, 8))
    z_bits = ((4, 4), (8, 8), (1, 2), (2, 1))

    def places(bits):
        if not fast:
            return jnp.asarray(np.arange(BLOCKS), jnp.int32)
        rel = np.zeros((2, BLOCKS), np.int32)
        for c in range(2):
            for r in range(BLOCKS):
                for stage in range(4):
                    if r >> (3 - stage) & 1:
                        rel[c, r] ^= bits[stage][c]
        return me ^ jnp.where(first, jnp.asarray(rel[0]), jnp.asarray(rel[1]))

    xy_order, z_order = places(xy_bits), places(z_bits)
    xy_order = jnp.concatenate([core.reshape(1), xy_order]).astype(jnp.int32)
    z_order = jnp.concatenate([core.reshape(1), z_order]).astype(jnp.int32)

    class Batch:
        def __init__(self, pair, bits):
            self.keep, self.send = pair
            self.bits, self.stage, self.result = bits, 0, None
            if not fast:
                flat = jnp.concatenate(pair, axis=0).astype(F32)
                n, count, per, chunk = flat.shape
                side = flat[:, :4].transpose(0, 2, 1, 3).reshape(n * per, 4 * chunk)
                self.result = [lax.psum_scatter(side, "dp", scatter_dimension=0, tiled=True)]
                if count > 4:
                    deep = flat[:, 4:].reshape(n * 4 * per, chunk)
                    self.result.append(lax.psum_scatter(deep, "dp", scatter_dimension=0, tiled=True))
            else:
                self.start()

        def start(self):
            self.got = lax.ppermute(self.send, both, axis_pairs(*self.bits[self.stage], dp))
            self.stage += 1

        def advance(self):
            half = self.keep.shape[0] // 2
            if half == 0:
                self.result = self.keep[0].astype(F32) + self.got[0].astype(F32)
                return self.result
            self.send, self.keep = self.keep[half:] + self.got[half:], self.keep[:half] + self.got[:half]
            return self.send

    class Vector:
        def __init__(self, value):
            self.value, self.stage, self.result = value, 0, None
            if not fast:
                self.result = lax.psum(value, both)
            else:
                self.got = other_core(value)

        def held(self):
            return [self.value, self.got]

        def start(self):
            self.got = lax.ppermute(self.value, both, axis_pairs(*xy_bits[self.stage], dp))
            self.stage += 1

        def advance(self):
            self.value = self.value + self.got
            if self.stage == 4:
                self.result = self.value
            return self.value

    def tick(*batches):
        batches = [b for b in batches if b.result is None]
        if not batches:
            return
        held = []
        for b in batches:
            held += [b.value, b.got] if isinstance(b, Vector) else [b.keep, b.got]
        held = lax.optimization_barrier(tuple(held) + tuple(chain.token))
        tokens_out = []
        for i, b in enumerate(batches):
            if isinstance(b, Vector):
                b.value, b.got = held[2 * i], held[2 * i + 1]
            else:
                b.keep, b.got = held[2 * i], held[2 * i + 1]
            tokens_out.append(b.advance())
        for b in batches:
            if b.result is None:
                b.start()
        chain.token = tuple(tokens_out)

    x0 = tokens.reshape(total * SLOTS, D)
    cot = cotangent.reshape(total * SLOTS, D)
    half_spec = pl.BlockSpec((t, D), lambda i, s: (s[0], 0))
    tok = whole((t, D))
    vec_spec, rot_spec = whole((4, D)), whole((2, SLOTS, LANES))
    scores_shape = (seqs * PAIRS, SLOTS, 2 * SLOTS)
    probs_shape = (seqs * PAIRS, 2 * SLOTS, SLOTS)
    vmem, dma = pltpu.VMEM, pltpu.SemaphoreType.DMA
    vecs = (mine["vec"], other["vec"], rot)
    vec_specs = [vec_spec, vec_spec, rot_spec]
    weights = (
        mine["in"], other["in"], mine["out"], other["out"],
        mine["up"], other["up"], mine["down"], other["down"],
    )
    row16, row32, wide16 = shape_of((t, D), BF16), shape_of((t, D), F32), shape_of((t, FF), BF16)
    three16 = shape_of((t, 3 * D), BF16)
    small = vmem((t, D), BF16)
    wide = vmem((t, FF), BF16)
    three = vmem((t, 3 * D), BF16)
    probs_mem, scores_mem = vmem(probs_shape, BF16), vmem(scores_shape, F32)
    mask_mem = vmem((seqs, SLOTS, 2 * SLOTS), F32)
    mem_in, mem_out, mem_up, mem_down = (
        vmem((D, 3 * D), BF16), vmem((D, D), BF16), vmem((D, FF), BF16), vmem((FF, D), BF16),
    )

    acts0, qkv0, probs0 = chain.call(
        functools.partial(open_kernel, seqs), scal,
        (x0,) + vecs + weights[:2],
        [half_spec] + vec_specs + [HBM] * 2,
        [shape_of((t, 2 * D), BF16), three16, shape_of(probs_shape, BF16)],
        [HBM] * 3,
        [vmem((t, 2 * D), BF16), three, scores_mem, probs_mem, mem_in, mask_mem, dma((3,)), dma((3,))],
        8.0,
    )
    ff_cols, all_cols = FF + D, FF + 3 * D + GRAD_COLS
    ff0, hidden0, slope0, y0, send1, keep1, y1, xgrad1, vgrad1 = chain.call(
        functools.partial(middle_kernel, seqs), scal,
        (x0, cot, acts0) + vecs + weights,
        [half_spec, half_spec, whole((t, 2 * D))] + vec_specs + [HBM] * 8,
        [shape_of((t, ff_cols), BF16), row32, wide16, row16, shape_of((t, all_cols), BF16),
         shape_of((t, GRAD_COLS), BF16), row16, row16, shape_of((4, D), F32)],
        [HBM] * 8 + [whole((4, D))],
        [mem_in, mem_out, mem_out, mem_up, mem_up, mem_down, mem_down,
         vmem((2, t, D), BF16), vmem((2, t, D), F32), wide, wide, vmem((2, t, D), BF16), small, small, three,
         scores_mem, probs_mem, mask_mem, wide, small, vmem((t, D), F32), small, three, small,
         dma((5 + 2 * NFT,)), dma((18,))],
        30.0,
    )
    send1_o = other_core(send1)

    def wgrads(order, terms, is_ff):
        ins, held, plan = [], [], []
        for (a0, a1), a_at, rows, (b0, b1), b_at, width in terms:
            ins += [a0, a1, b0, b1]
            held += [vmem((2 * t, rows), BF16), vmem((2 * t, width), BF16)]
            plan.append((rows, width, a_at, b_at))
        per, chunk = D // BLOCKS, D // 2
        half = shape_of((BLOCKS // 2, 8 if is_ff else 4, per, chunk), BF16)
        results = [vmem((4, BLOCKS, per, chunk), BF16)]
        if is_ff:
            results.append(vmem((FF // per, per, chunk), BF16))
        return chain.call(
            functools.partial(wgrad_kernel, plan, is_ff), order, ins, [HBM] * len(ins), [half] * 2, [HBM] * 2,
            held + results + [dma((4 * len(terms),)), dma((2 * BLOCKS,))],
            8.0,
        )

    def fixed(col):
        return lambda core: (col, 0)

    def own_half(core):
        return pl.multiple_of(core * HALF_OUT, 128)

    def own_cot(core):
        return own_half(core), pl.multiple_of(core * t, 16)

    def other_cot(core):
        return own_half(core), pl.multiple_of((1 - core) * t, 16)

    def own_cols(core):
        return own_half(core), 0

    keep0, send0, hgrad0, mgrad0, vgrad0_ff = chain.call(
        ff_last_kernel, scal,
        (xgrad1, hidden0) + vecs[:2] + (slope0,) + weights[2:],
        [tok, tok] + vec_specs[:2] + [HBM] * 7,
        [shape_of((t, HALF_UP + HALF_OUT), BF16)] * 2 + [row32, row16, shape_of((4, D), F32)],
        [HBM] * 2 + [tok, tok, whole((4, D))],
        [mem_up, mem_down, mem_out, wide, wide, small, dma((3 + NFT,)), dma((4,))],
        10.0,
    )
    grads_at = MIXED_AT + D
    acts1, grads1 = (send1, send1_o), (keep1, send1_o)
    ff1 = Batch(
        wgrads(
            xy_order,
            [
                (acts1, (DENSE_AT,) * 2, D, grads1, (fixed(UG_AT), fixed(grads_at + UG_AT)), HALF_UP),
                (acts1, (ACTIVE_AT,) * 2, FF, (cot, cot), (own_cot, other_cot), HALF_OUT),
            ],
            True,
        ),
        xy_bits,
    )
    attn1 = Batch(
        wgrads(
            z_order,
            [
                (acts1, (NORMED_AT,) * 2, D, grads1, (fixed(PG_AT), fixed(grads_at + PG_AT)), HALF_IN),
                (acts1, (MIXED_AT,) * 2, D, grads1, (fixed(BG_AT), fixed(grads_at + BG_AT)), HALF_OUT),
            ],
            False,
        ),
        z_bits,
    )
    ff0_o, xgrad1_o, send0_o = (other_core(v) for v in (ff0, xgrad1, send0))
    pkeep0, psend0, xgrad0, vgrad0_attn = chain.call(
        functools.partial(attn_last_kernel, seqs), scal,
        (x0, mgrad0, hgrad0) + vecs + (qkv0, probs0) + weights[:2],
        [half_spec, tok, tok] + vec_specs + [HBM] * 4,
        [shape_of((t, HALF_IN), BF16)] * 2 + [row16, shape_of((4, D), F32)],
        [HBM] * 3 + [whole((4, D))],
        [mem_in, three, probs_mem, vmem((PAIRS, SLOTS, 2 * SLOTS), F32), three, small, dma((3,)), dma((3,))],
        9.0,
    )
    acts0_o, psend0_o = other_core(acts0), other_core(psend0)
    pair_ff0 = wgrads(
        xy_order,
        [
            ((ff0, ff0_o), (DENSE_AT,) * 2, D, (keep0, send0_o), (fixed(0),) * 2, HALF_UP),
            ((ff0, ff0_o), (ACTIVE_AT,) * 2, FF, (xgrad1, xgrad1_o), (own_cols,) * 2, HALF_OUT),
        ],
        True,
    )
    tick(ff1)
    ff0_sum = Batch(pair_ff0, xy_bits)
    tick(attn1)
    attn0 = Batch(
        wgrads(
            xy_order,
            [
                ((acts0, acts0_o), (0,) * 2, D, (pkeep0, psend0_o), (fixed(0),) * 2, HALF_IN),
                ((acts0, acts0_o), (D,) * 2, D, (keep0, send0_o), (fixed(HALF_UP),) * 2, HALF_OUT),
            ],
            False,
        ),
        xy_bits,
    )
    vgrad0 = jnp.concatenate([vgrad0_attn[:2], vgrad0_ff[2:]], axis=0)
    tick(ff1)
    tick(ff0_sum)
    tick(attn1)
    tick(attn0)
    vec_sum = Vector(jnp.concatenate([vgrad0, vgrad1], axis=0))
    tick(attn1)
    tick(ff1)
    tick(ff0_sum, attn1)
    tick(attn0)
    tick(ff1, vec_sum)
    tick(ff0_sum, vec_sum)
    tick(attn0, vec_sum)
    tick(ff0_sum, vec_sum)
    tick(attn0, vec_sum)
    for _ in range(4):
        tick(ff1, attn1, ff0_sum, attn0, vec_sum)
    ys, xgrads = [y0, y1], [xgrad0, xgrad1]
    per = D // dp

    def side(v):
        return v.transpose(1, 0, 2).reshape(v.shape[1], -1)

    def parts(ff, attn):
        if fast:
            ff, attn = ff.result, attn.result
            return side(attn[:3]), attn[3], side(ff[:4]), ff[4:].reshape(FF // dp, D // 2)
        (up, down), (both_attn,) = ff.result, attn.result
        return both_attn[:, :HALF_IN], both_attn[:, HALF_IN:], up, down

    shards = [parts(ff0_sum, attn0), parts(ff1, attn1)]

    def settle(a, b):
        here = jnp.where(first, a, b)
        there = other_core(jnp.where(first, b, a))
        return jnp.where(first, jnp.concatenate([here, there], -1), jnp.concatenate([there, here], -1))

    grad_in, grad_out, grad_up, grad_down = (
        settle(a, b)[None] for a, b in zip(shards[0], shards[1])
    )

    def settle_rows(pair):
        here = jnp.where(first, pair[0], pair[1])
        there = other_core(jnp.where(first, pair[1], pair[0]))
        whole_rows = jnp.where(
            first, jnp.concatenate([here, there], 0), jnp.concatenate([there, here], 0)
        )
        return whole_rows.reshape((1,) + tokens.shape)

    layer_out = settle_rows(ys)
    input_grads = settle_rows(xgrads)

    vec = vec_sum.result
    vec = jnp.where(first, vec[:4], vec[4:])
    vec = lax.dynamic_slice(vec, (0, me * per), (4, per))
    return (
        layer_out,
        input_grads,
        vec[0:1],
        vec[1:2],
        grad_in,
        grad_out,
        vec[2:3],
        vec[3:4],
        grad_up,
        grad_down,
    )


def solution(mesh):
    row = P(None, "dp", None, None)
    vec = P("section", None)
    mat = P("section", None, None)
    outs = P("section", None, "dp", None, None)
    out_vec = P("section", "dp")
    out_mat = P("section", "dp", None)
    return jax.shard_map(
        body,
        mesh=mesh,
        in_specs=(row, row, P(None, "dp"), vec, vec, mat, mat, vec, vec, mat, mat),
        out_specs=(outs, outs, out_vec, out_vec, out_mat, out_mat, out_vec, out_vec, out_mat, out_mat),
        check_vma=False,
    )
```

```python
import functools
import math

import jax
import jax.numpy as jnp
import numpy as np
from jax import lax
from jax.experimental import pallas as pl
from jax.experimental.pallas import tpu as pltpu
from jax.sharding import PartitionSpec as P

D = 768
HEADS = 12
HEAD = 64
FF = 3072
BLK = 16
SEQ = 64
SLOTS = 2 * SEQ
PAIRS = HEADS // 2
LANES = 2 * HEAD
BLOCKS = 16
FT = 1536
NFT = FF // FT

norm_eps = 1e-05
masked_score = -1000000000.0
gelu_c = math.sqrt(2.0 / math.pi)
gelu_a = 0.044715

F32 = jnp.float32
BF16 = jnp.bfloat16
VMEM_LIMIT = 60 * 1024 * 1024


def dot(a, b, ca=1, cb=0):
    return lax.dot_general(a, b, (((ca,), (cb,)), ((), ())), preferred_element_type=F32)


def rotary_tables():
    places = (np.arange(SLOTS) % SEQ).astype(np.float32)
    half = HEAD // 2
    freqs = (10000.0 ** (-np.arange(half).astype(np.float32) * 2.0 / HEAD)).astype(np.float32)
    angles = (places[:, None] * freqs[None, :]).astype(np.float32)
    cos, sin = np.cos(angles), np.sin(angles)
    return np.stack(
        [
            np.concatenate([cos] * 4, axis=1),
            np.concatenate([-sin, sin, -sin, sin], axis=1),
        ]
    ).astype(np.float32)


def swap_halves(v):
    lane = lax.broadcasted_iota(jnp.int32, v.shape, 1)
    first = lax.rem(lane, HEAD) < HEAD // 2
    return jnp.where(first, pltpu.roll(v, LANES - 32, 1), pltpu.roll(v, 32, 1))


def open_keys_t(length):
    key = lax.broadcasted_iota(jnp.int32, (SLOTS, SLOTS), 0)
    query = lax.broadcasted_iota(jnp.int32, (SLOTS, SLOTS), 1)
    key_clean, query_clean = key >= SEQ, query >= SEQ
    key_place, query_place = lax.rem(key, SEQ), lax.rem(query, SEQ)
    kb, qb = lax.div(key_place, BLK), lax.div(query_place, BLK)
    both_noisy = jnp.logical_and(jnp.logical_not(key_clean), jnp.logical_not(query_clean))
    both_clean = jnp.logical_and(key_clean, query_clean)
    crossed = jnp.logical_and(key_clean, jnp.logical_not(query_clean))
    structure = (
        (both_noisy & (kb == qb)) | (crossed & (kb < qb)) | (both_clean & (kb <= qb))
    )
    return structure & ((key_place < length) | (key == query))


def norm_stats(v):
    centered = v - jnp.mean(v, axis=-1, keepdims=True)
    spread = jnp.mean(centered * centered, axis=-1, keepdims=True)
    return centered, lax.rsqrt(spread + norm_eps)


def norm_back(dy, source, gain):
    centered, scale = norm_stats(source)
    xhat = centered * scale
    g = dy * gain
    part = scale * (
        g
        - jnp.mean(g, axis=-1, keepdims=True)
        - xhat * jnp.mean(g * xhat, axis=-1, keepdims=True)
    )
    return part, jnp.sum(dy * xhat, axis=0, keepdims=True), jnp.sum(dy, axis=0, keepdims=True)


def col_pieces(rows, cols, n):
    w = cols // n
    return [(slice(0, rows), slice(i * w, (i + 1) * w)) for i in range(n)]


def row_pieces(rows, cols, n):
    w = rows // n
    return [(slice(i * w, (i + 1) * w), slice(0, cols)) for i in range(n)]


IN_PIECES = col_pieces(D, 3 * D, 3)
IN_ALL = col_pieces(D, 3 * D, 1)
OUT_PIECES = row_pieces(D, D, 1)
UP_PIECES = col_pieces(D, FF, NFT)
DOWN_PIECES = row_pieces(FF, D, 1)


class Feed:
    def __init__(self, own):
        self.own, self.queue = own, []

    def weight(self, mine, other, piece, dst, sem):
        self.queue.append((mine, other, piece, dst, sem))
        return pltpu.make_async_copy(mine.at[piece], dst.at[piece], sem)

    def begin(self, count=None):
        count = len(self.queue) if count is None else count
        queue, self.queue = self.queue[:count], self.queue[count:]

        @pl.when(self.own)
        def _():
            for mine, _, piece, dst, sem in queue:
                pltpu.make_async_copy(mine.at[piece], dst.at[piece], sem).start()

        @pl.when(jnp.logical_not(self.own))
        def _():
            for _, other, piece, dst, sem in queue:
                pltpu.make_async_copy(other.at[piece], dst.at[piece], sem).start()


class Drain:
    def __init__(self, sems):
        self.sems, self.copies = sems, []

    def put(self, src, dst):
        c = pltpu.make_async_copy(src, dst, self.sems.at[len(self.copies)])
        c.start()
        self.copies.append(c)
        return c

    def finish(self, skip=()):
        for c in self.copies:
            if not any(c is done for done in skip):
                c.wait()


def make_mask(mask, seqs, scal):
    for s in range(seqs):
        keep = open_keys_t(scal[1 + scal[0] * seqs + s])
        shut = jnp.where(keep, 0.0, 1.0)
        mask[s, :, 0:SLOTS] = shut
        mask[s, :, SLOTS : 2 * SLOTS] = shut


def pair_tile(ref, rows, part, p):
    lo = part * D + p * LANES
    return ref[rows, lo : lo + LANES]


def both_heads(v):
    left = lax.broadcasted_iota(jnp.int32, (SLOTS, LANES), 1) < HEAD
    zero = jnp.zeros((SLOTS, LANES), BF16)
    return jnp.concatenate([jnp.where(left, v, zero), jnp.where(left, zero, v)], axis=0)


def norm_into(dst, source, gain, bias):
    centered, scale = norm_stats(source)
    dst[...] = (centered * scale * gain + bias).astype(BF16)


def project(seqs, normed, w_in, waits, rot_ref, qkv):
    cos, sin = rot_ref[0], rot_ref[1]
    for part in range(3):
        if part < len(waits):
            waits[part].wait()
        for tile in range(D // 256):
            lo = part * D + tile * 256
            val = dot(normed[...], w_in[:, lo : lo + 256])
            if part == 2:
                qkv[:, lo : lo + 256] = val.astype(BF16)
                continue
            for u in range(2):
                for s in range(seqs):
                    v = val[s * SLOTS : (s + 1) * SLOTS, u * LANES : (u + 1) * LANES]
                    v = v * cos + swap_halves(v) * sin
                    if part == 0:
                        v = v * HEAD ** (-0.5)
                    qkv[
                        s * SLOTS : (s + 1) * SLOTS, lo + u * LANES : lo + (u + 1) * LANES
                    ] = v.astype(BF16)


def attend(seqs, qkv, mask, scores, probs, mixed):
    for s in range(seqs):
        rows = slice(s * SLOTS, (s + 1) * SLOTS)
        for p in range(PAIRS):
            scores[s * PAIRS + p] = dot(
                pair_tile(qkv, rows, 1, p), both_heads(pair_tile(qkv, rows, 0, p)), 1, 1
            )
        for p in range(PAIRS):
            i = s * PAIRS + p
            st = jnp.where(mask[s] > 0.5, masked_score, scores[i])
            e = jnp.exp(st - jnp.max(st, axis=0, keepdims=True))
            low = (e * (1.0 / jnp.sum(e, axis=0, keepdims=True))).astype(BF16)
            probs[i, 0:SLOTS] = low[:, :SLOTS]
            probs[i, SLOTS : 2 * SLOTS] = low[:, SLOTS:]
        for p in range(PAIRS):
            mixed[rows, p * LANES : (p + 1) * LANES] = dot(
                probs[s * PAIRS + p], both_heads(pair_tile(qkv, rows, 2, p)), 0, 0
            ).astype(BF16)


def activate(dense, w_up, slope, active, waits):
    for t in range(FF // 256):
        if t * 256 % FT == 0:
            waits[t * 256 // FT].wait()
        cols = slice(t * 256, (t + 1) * 256)
        u = dot(dense[...], w_up[:, cols])
        u2 = u * u
        th = jnp.tanh(u * (gelu_c + (gelu_c * gelu_a) * u2))
        h = 0.5 * (1.0 + th)
        active[:, cols] = (u * h).astype(BF16)
        slope[:, cols] = (
            h + u * (1.0 - th * th) * (0.5 * gelu_c + (1.5 * gelu_c * gelu_a) * u2)
        ).astype(BF16)


def open_kernel(seqs, scal, x_ref, vec_mine, vec_other, rot_ref, in_mine, in_other,
                acts_o, qkv_o, probs_o,
                acts, qkv, scores, probs, w_in, mask, sems, out_sems):
    own = scal[0] == 0
    feed, drain = Feed(own), Drain(out_sems)
    w_waits = [feed.weight(in_mine, in_other, IN_PIECES[i], w_in, sems.at[i]) for i in range(3)]
    feed.begin()
    vec = jnp.where(own, vec_mine[...], vec_other[...])
    normed, mixed = acts.at[:, 0:D], acts.at[:, D : 2 * D]
    norm_into(normed, x_ref[...].astype(F32), vec[0:1], vec[1:2])
    make_mask(mask, seqs, scal)
    project(seqs, normed, w_in, w_waits, rot_ref, qkv)
    drain.put(qkv, qkv_o)
    attend(seqs, qkv, mask, scores, probs, mixed)
    drain.put(probs, probs_o)
    drain.put(acts, acts_o)
    drain.finish()


def halves(core, width):
    keep = pl.ds(pl.multiple_of(core * width, 128), width)
    send = pl.ds(pl.multiple_of((1 - core) * width, 128), width)
    return keep, send


def split_out(drain, core, src, width, at, keep_o, send_o, send_base):
    keep, send = halves(core, width)
    drain.put(src.at[:, keep], keep_o.at[:, at : at + width])
    drain.put(src.at[:, send], send_o.at[:, send_base + at : send_base + at + width])


def ff_back(r_ref, hidden, gain, w_up, w_down, w_out, slope, ug, bgrad, hgrad, mgrad, vgrad, waits):
    down_waits, up_waits, out_waits = waits
    for c in down_waits:
        c.wait()
    for t in range(FF // 256):
        cols = slice(t * 256, (t + 1) * 256)
        ug[:, cols] = (dot(r_ref[...], w_down[cols, :], 1, 1) * slope[:, cols].astype(F32)).astype(BF16)
    for c in up_waits:
        c.wait()
    part, dg, db = norm_back(dot(ug[...], w_up[...], 1, 1), hidden[...], gain)
    vgrad[2:3] = dg
    vgrad[3:4] = db
    total = r_ref[...].astype(F32) + part
    hgrad[...] = total
    bgrad[...] = total.astype(BF16)
    for c in out_waits:
        c.wait()
    mgrad[...] = dot(bgrad[...], w_out[...], 1, 1).astype(BF16)


def attn_back(seqs, x_ref, gain, rot_ref, w_in, qkv, probs, dpt, mgrad, hgrad, pgrad, xgrad, vgrad, waits):
    in_waits, w_waits = waits
    cos, sin = rot_ref[0], rot_ref[1]
    for c in in_waits:
        c.wait()
    for s in range(seqs):
        rows = slice(s * SLOTS, (s + 1) * SLOTS)
        for p in range(PAIRS):
            dm = both_heads(mgrad[rows, p * LANES : (p + 1) * LANES])
            dpt[p] = dot(pair_tile(qkv, rows, 2, p), dm, 1, 1)
        for p in range(PAIRS):
            i = s * PAIRS + p
            low = jnp.concatenate([probs[i, 0:SLOTS], probs[i, SLOTS : 2 * SLOTS]], axis=1)
            pt = low.astype(F32)
            pd = pt * dpt[p]
            dst = (pd - pt * jnp.sum(pd, axis=0, keepdims=True)).astype(BF16)
            dm = both_heads(mgrad[rows, p * LANES : (p + 1) * LANES])
            dv = dot(low, dm)
            dk = dot(dst, both_heads(pair_tile(qkv, rows, 0, p)))
            stacked = jnp.concatenate([dst[:, :SLOTS], dst[:, SLOTS:]], axis=0)
            dq = dot(stacked, both_heads(pair_tile(qkv, rows, 1, p)), 0, 0) * HEAD ** (-0.5)
            dq = dq * cos - swap_halves(dq) * sin
            dk = dk * cos - swap_halves(dk) * sin
            pgrad[rows, p * LANES : (p + 1) * LANES] = dq.astype(BF16)
            pgrad[rows, D + p * LANES : D + (p + 1) * LANES] = dk.astype(BF16)
            pgrad[rows, 2 * D + p * LANES : 2 * D + (p + 1) * LANES] = dv.astype(BF16)
    for c in w_waits:
        c.wait()
    part, dg, db = norm_back(dot(pgrad[...], w_in[...], 1, 1), x_ref[...].astype(F32), gain)
    vgrad[0:1] = dg
    vgrad[1:2] = db
    xgrad[...] = (hgrad[...] + part).astype(BF16)


ACTIVE_AT, DENSE_AT, NORMED_AT, MIXED_AT = 0, FF, FF + D, FF + 2 * D
HALF_IN, HALF_OUT, HALF_UP = 3 * D // 2, D // 2, FF // 2
UG_AT, PG_AT, BG_AT = 0, HALF_UP, HALF_UP + HALF_IN
GRAD_COLS = HALF_UP + HALF_IN + HALF_OUT
GRADS_AT = FF + 3 * D


def middle_kernel(seqs, scal, x_ref, cot_ref, acts0, vec_mine, vec_other, rot_ref,
                  in_mine, in_other, out_mine, out_other, up_mine, up_other, down_mine, down_other,
                  ff0_o, hidden0_o, slope0_o, y0_o, send1_o, keep1_o, y1_o, xgrad1_o, vgrad_ref,
                  w_in, w_out0, w_out1, w_up0, w_up1, w_down0, w_down1,
                  dense, hidden, slope, active, y, normed, mixed, qkv, scores, probs, mask,
                  ug, bgrad, hgrad, mgrad, pgrad, xgrad, sems, drain_sems):
    core = scal[0]
    own = core == 0
    drain = Drain(drain_sems)

    def weights(feed, base, w_out, w_up, w_down):
        out = feed.weight(out_mine, out_other, OUT_PIECES[0], w_out, sems.at[base])
        up = [feed.weight(up_mine, up_other, UP_PIECES[i], w_up, sems.at[base + 1 + i]) for i in range(NFT)]
        down = feed.weight(down_mine, down_other, DOWN_PIECES[0], w_down, sems.at[base + 1 + NFT])
        return out, up, down

    feed0, feed1 = Feed(own), Feed(jnp.logical_not(own))
    waits0 = weights(feed0, 0, w_out0, w_up0, w_down0)
    in_waits = [feed1.weight(in_mine, in_other, IN_ALL[0], w_in, sems.at[4 + 2 * NFT])]
    waits1 = weights(feed1, 2 + NFT, w_out1, w_up1, w_down1)
    feed0.begin(1 + NFT)
    vec0 = jnp.where(own, vec_mine[...], vec_other[...])
    vec1 = jnp.where(own, vec_other[...], vec_mine[...])
    make_mask(mask, seqs, scal)

    def tail(layer, x, mixed_in, w_out, w_up, w_down, waits, vec, held, following):
        waits[0].wait()
        if layer == 0:
            feed0.begin()
        hidden[layer] = x + dot(mixed_in[...], w_out[...])
        norm_into(dense.at[layer], hidden[layer], vec[2:3], vec[3:4])
        for c in held:
            c.wait()
        activate(dense.at[layer], w_up, slope, active, waits[1])
        waits[2].wait()
        following()
        y[layer] = (hidden[layer] + dot(active[...], w_down[...])).astype(BF16)

    tail(
        0, x_ref[...].astype(F32), acts0.at[:, D : 2 * D], w_out0, w_up0, w_down0, waits0, vec0, (), feed1.begin
    )
    copies = [drain.put(slope, slope0_o), drain.put(active, ff0_o.at[:, ACTIVE_AT : ACTIVE_AT + FF])]
    drain.put(dense.at[0], ff0_o.at[:, DENSE_AT : DENSE_AT + D])
    drain.put(acts0, ff0_o.at[:, NORMED_AT : NORMED_AT + 2 * D])
    drain.put(hidden.at[0], hidden0_o)
    drain.put(y.at[0], y0_o)
    norm_into(normed, y[0].astype(F32), vec1[0:1], vec1[1:2])
    project(seqs, normed, w_in, in_waits, rot_ref, qkv)
    attend(seqs, qkv, mask, scores, probs, mixed)
    tail(
        1, y[0].astype(F32), mixed, w_out1, w_up1, w_down1, waits1, vec1, copies, lambda: None
    )
    drain.put(active, send1_o.at[:, ACTIVE_AT : ACTIVE_AT + FF])
    drain.put(dense.at[1], send1_o.at[:, DENSE_AT : DENSE_AT + D])
    drain.put(normed, send1_o.at[:, NORMED_AT : NORMED_AT + D])
    drain.put(mixed, send1_o.at[:, MIXED_AT : MIXED_AT + D])
    drain.put(y.at[1], y1_o)
    ff_back(
        cot_ref, hidden.at[1], vec1[2:3], w_up1, w_down1, w_out1, slope, ug, bgrad, hgrad, mgrad, vgrad_ref,
        ((), (), ()),
    )
    split_out(drain, core, ug, HALF_UP, UG_AT, keep1_o, send1_o, GRADS_AT)
    split_out(drain, core, bgrad, HALF_OUT, BG_AT, keep1_o, send1_o, GRADS_AT)
    attn_back(
        seqs, y.at[0], vec1[0:1], rot_ref, w_in, qkv, probs, scores, mgrad, hgrad, pgrad, xgrad, vgrad_ref,
        ((), ()),
    )
    split_out(drain, core, pgrad, HALF_IN, PG_AT, keep1_o, send1_o, GRADS_AT)
    drain.put(xgrad, xgrad1_o)
    drain.put(xgrad, send1_o.at[:, GRADS_AT + GRAD_COLS : GRADS_AT + GRAD_COLS + D])
    drain.finish(copies)


def ff_last_kernel(scal, r_ref, hidden_ref, vec_mine, vec_other, slope_ref,
                   out_mine, out_other, up_mine, up_other, down_mine, down_other,
                   keep0_o, send0_o, hgrad_ref, mgrad_ref, vgrad_ref,
                   w_up, w_down, w_out, slope, ug, bgrad, sems, drain_sems):
    core = scal[0]
    own = core == 0
    feed, drain = Feed(own), Drain(drain_sems)
    downs = [feed.weight(down_mine, down_other, DOWN_PIECES[0], w_down, sems.at[0])]
    feed.begin()
    slopes = [pltpu.make_async_copy(slope_ref, slope, sems.at[1])]
    slopes[0].start()
    ups = [feed.weight(up_mine, up_other, UP_PIECES[i], w_up, sems.at[3 + i]) for i in range(NFT)]
    out = [feed.weight(out_mine, out_other, OUT_PIECES[0], w_out, sems.at[2])]
    feed.begin()
    vec = jnp.where(own, vec_mine[...], vec_other[...])
    ff_back(
        r_ref, hidden_ref, vec[2:3], w_up, w_down, w_out, slope, ug, bgrad, hgrad_ref, mgrad_ref, vgrad_ref,
        (slopes + downs, ups, out),
    )
    split_out(drain, core, ug, HALF_UP, UG_AT, keep0_o, send0_o, 0)
    split_out(drain, core, bgrad, HALF_OUT, UG_AT + HALF_UP, keep0_o, send0_o, 0)
    drain.finish()


def attn_last_kernel(seqs, scal, x_ref, mgrad_ref, hgrad_ref, vec_mine, vec_other, rot_ref, qkv_ref, probs_ref,
                     in_mine, in_other,
                     keep0_o, send0_o, xgrad_o, vgrad_ref,
                     w_in, qkv, probs, dpt, pgrad, xgrad, sems, drain_sems):
    core = scal[0]
    own = core == 0
    feed, drain = Feed(own), Drain(drain_sems)
    plain = [
        pltpu.make_async_copy(src, dst, sems.at[i])
        for i, (src, dst) in enumerate(((qkv_ref, qkv), (probs_ref, probs)))
    ]
    for c in plain:
        c.start()
    w_waits = [feed.weight(in_mine, in_other, IN_ALL[0], w_in, sems.at[2])]
    feed.begin()
    vec = jnp.where(own, vec_mine[...], vec_other[...])
    attn_back(
        seqs, x_ref, vec[0:1], rot_ref, w_in, qkv, probs, dpt, mgrad_ref, hgrad_ref, pgrad, xgrad, vgrad_ref,
        (plain, w_waits),
    )
    split_out(drain, core, pgrad, HALF_IN, 0, keep0_o, send0_o, 0)
    drain.put(xgrad, xgrad_o)
    drain.finish()


def wgrad_kernel(terms, is_ff, table, scal, *refs):
    n = len(terms)
    srcs, (keep_o, send_o) = refs[: 4 * n], refs[4 * n : 4 * n + 2]
    held, rest = refs[4 * n + 2 : 6 * n + 2], refs[6 * n + 2 :]
    results, (sems, drain_sems) = rest[:-2], rest[-2:]
    core = scal[0]
    loads = []
    for i, (rows, width, a_at, b_at) in enumerate(terms):
        tokens = held[2 * i].shape[0] // 2
        for j in range(2):
            mine = slice(j * tokens, (j + 1) * tokens)
            col, row = b_at[j](core)
            src = srcs[4 * i + 2 + j].at[pl.ds(row, tokens), pl.ds(col, width)]
            loads.append(pltpu.make_async_copy(src, held[2 * i + 1].at[mine], sems.at[len(loads)]))
            src = srcs[4 * i + j].at[:, a_at[j] : a_at[j] + rows]
            loads.append(pltpu.make_async_copy(src, held[2 * i].at[mine], sems.at[len(loads)]))
    for c in loads[:4]:
        c.start()
    half, per, chunk = BLOCKS // 2, D // BLOCKS, D // 2
    drain = Drain(drain_sems)

    def wait_for(i):
        for c in loads[4 * i : 4 * i + 4]:
            c.wait()
        for c in loads[4 * i + 4 : 4 * i + 8]:
            c.start()

    def send_block(r, src, at, count):
        dst = keep_o.at[r] if r < half else send_o.at[r - half]
        drain.put(src, dst.at[at : at + count])

    def side_by_side(i, res, base):
        a, b = held[2 * i], held[2 * i + 1]
        count = terms[i][1] // chunk
        for j in range(0, count, 2):
            m = min(2, count - j)
            val = dot(a[...], b[:, j * chunk : (j + m) * chunk], 0, 0).astype(BF16)
            for k in range(m):
                res[base + j + k] = val[:, k * chunk : (k + 1) * chunk].reshape(BLOCKS, per, chunk)
        return base + count

    wait_for(0)
    if is_ff:
        count = side_by_side(0, results[0], 0)
        for r in list(range(half, BLOCKS)) + list(range(half)):
            send_block(r, results[0].at[:, scal[table + r]], 0, count)
        wait_for(1)
        a, b = held[2:4]
        deep = FF // D
        for q in range(deep):
            val = dot(a[:, q * D : (q + 1) * D], b[...], 0, 0).astype(BF16)
            results[1][q * BLOCKS : (q + 1) * BLOCKS] = val.reshape(BLOCKS, per, chunk)
        for r in list(range(half, BLOCKS)) + list(range(half)):
            send_block(r, results[1].at[pl.ds(scal[table + r] * deep, deep)], count, deep)
    else:
        count = side_by_side(0, results[0], 0)
        wait_for(1)
        count = side_by_side(1, results[0], count)
        for r in list(range(half, BLOCKS)) + list(range(half)):
            send_block(r, results[0].at[:, scal[table + r]], 0, count)
    drain.finish()


def whole(shape):
    return pl.BlockSpec(shape, lambda i, s: (0,) * len(shape))


def shape_of(shape, dtype):
    return jax.ShapeDtypeStruct(shape, dtype)


HBM = pl.BlockSpec(memory_space=pl.ANY)


class Chain:
    def __init__(self):
        self.token = ()

    def call(self, kernel, scal, ins, in_specs, outs, out_specs, scratch, micros, after=()):
        after = tuple(self.token) + tuple(after)
        n, extra = 1 + len(ins), len(after)

        def ordered(*refs):
            kernel(*refs[:n], *refs[n + extra :])

        result = pl.pallas_call(
            ordered,
            grid_spec=pltpu.PrefetchScalarGridSpec(
                num_scalar_prefetch=1,
                grid=(1,),
                in_specs=list(in_specs) + [HBM] * extra,
                out_specs=out_specs,
                scratch_shapes=scratch,
            ),
            out_shape=outs,
            compiler_params=pltpu.CompilerParams(vmem_limit_bytes=VMEM_LIMIT),
            cost_estimate=pl.CostEstimate(
                flops=int(micros * 1e6), bytes_accessed=2**10, transcendentals=0
            ),
        )(scal, *ins, *after)
        self.token = (result[-1],)
        return result


def axis_pairs(first, second, size):
    return [(i, i ^ first) for i in range(size)] + [
        (size + i, size + (i ^ second)) for i in range(size)
    ]


def body(
    tokens, cotangent, lengths, mixer_gain, mixer_bias, project_in, project_out,
    dense_gain, dense_bias, up_weight, down_weight,
):
    micro, rows = tokens.shape[:2]
    total = micro * rows
    seqs = total // 2
    t = seqs * SLOTS
    core = lax.axis_index("section")
    first = core == 0
    me = lax.axis_index("dp")
    dp = lax.axis_size("dp")
    fast = dp == BLOCKS
    both = ("section", "dp")
    chain = Chain()

    def other_core(v):
        return lax.ppermute(v, "section", [(0, 1), (1, 0)])

    mine = {
        "vec": jnp.concatenate([mixer_gain, mixer_bias, dense_gain, dense_bias], axis=0),
        "in": project_in[0],
        "out": project_out[0],
        "up": up_weight[0],
        "down": down_weight[0],
    }
    other = {name: other_core(mine[name]) for name in ("vec", "in")}
    other["in"], out_held, up_held, down_held = lax.optimization_barrier(
        (other["in"], mine["out"], mine["up"], mine["down"])
    )
    other["out"], other["up"], other["down"] = map(other_core, (out_held, up_held, down_held))
    rot = jnp.asarray(rotary_tables())
    scal = jnp.concatenate([core.reshape(1), lengths.reshape(total)]).astype(jnp.int32)

    steps = {"A": (1, 2), "B": (2, 1), "l": (4, 4), "h": (8, 8)}
    names = ("ff1", "attn1", "ff0", "attn0")
    orders = dict(zip(names, ("AlBh", "lABh", "AlBh", "ABlh")))
    bits_of = {name: [steps[c] for c in orders[name]] for name in names}
    table_of = {name: 1 + BLOCKS * i for i, name in enumerate(names)}
    xy_bits = [steps[c] for c in "ABlh"]

    def places(bits):
        if not fast:
            return jnp.asarray(np.arange(BLOCKS), jnp.int32)
        rel = np.zeros((2, BLOCKS), np.int32)
        for c in range(2):
            for r in range(BLOCKS):
                for stage in range(4):
                    if r >> (3 - stage) & 1:
                        rel[c, r] ^= bits[stage][c]
        return me ^ jnp.where(first, jnp.asarray(rel[0]), jnp.asarray(rel[1]))

    order = jnp.concatenate([core.reshape(1)] + [places(bits_of[name]) for name in names]).astype(jnp.int32)

    class Batch:
        def __init__(self, pair, bits):
            self.keep, self.send = pair
            self.bits, self.stage, self.result = bits, 0, None
            if not fast:
                flat = jnp.concatenate(pair, axis=0).astype(F32)
                n, count, per, chunk = flat.shape
                side = flat[:, :4].transpose(0, 2, 1, 3).reshape(n * per, 4 * chunk)
                self.result = [lax.psum_scatter(side, "dp", scatter_dimension=0, tiled=True)]
                if count > 4:
                    deep = flat[:, 4:].reshape(n * 4 * per, chunk)
                    self.result.append(lax.psum_scatter(deep, "dp", scatter_dimension=0, tiled=True))
            else:
                self.start()

        def start(self):
            self.got = lax.ppermute(self.send, both, axis_pairs(*self.bits[self.stage], dp))
            self.stage += 1

        def advance(self):
            half = self.keep.shape[0] // 2
            if half == 0:
                self.result = self.keep[0].astype(F32) + self.got[0].astype(F32)
                return self.result
            self.send, self.keep = self.keep[half:] + self.got[half:], self.keep[:half] + self.got[:half]
            return self.send

    class Vector:
        def __init__(self, value):
            self.value, self.stage, self.result = value, 0, None
            if not fast:
                self.result = lax.psum(value, both)
            else:
                self.got = other_core(value)

        def held(self):
            return [self.value, self.got]

        def start(self):
            self.got = lax.ppermute(self.value, both, axis_pairs(*xy_bits[self.stage], dp))
            self.stage += 1

        def advance(self):
            self.value = self.value + self.got
            if self.stage == 4:
                self.result = self.value
            return self.value

    def tick(*batches):
        batches = [b for b in batches if b.result is None]
        if not batches:
            return
        held = []
        for b in batches:
            held += [b.value, b.got] if isinstance(b, Vector) else [b.keep, b.got]
        held = lax.optimization_barrier(tuple(held) + tuple(chain.token))
        tokens_out = []
        for i, b in enumerate(batches):
            if isinstance(b, Vector):
                b.value, b.got = held[2 * i], held[2 * i + 1]
            else:
                b.keep, b.got = held[2 * i], held[2 * i + 1]
            tokens_out.append(b.advance())
        for b in batches:
            if b.result is None:
                b.start()
        chain.token = tuple(tokens_out)

    x0 = tokens.reshape(total * SLOTS, D)
    cot = cotangent.reshape(total * SLOTS, D)
    half_spec = pl.BlockSpec((t, D), lambda i, s: (s[0], 0))
    tok = whole((t, D))
    vec_spec, rot_spec = whole((4, D)), whole((2, SLOTS, LANES))
    scores_shape = (seqs * PAIRS, SLOTS, 2 * SLOTS)
    probs_shape = (seqs * PAIRS, 2 * SLOTS, SLOTS)
    vmem, dma = pltpu.VMEM, pltpu.SemaphoreType.DMA
    vecs = (mine["vec"], other["vec"], rot)
    vec_specs = [vec_spec, vec_spec, rot_spec]
    weights = (
        mine["in"], other["in"], mine["out"], other["out"],
        mine["up"], other["up"], mine["down"], other["down"],
    )
    row16, row32, wide16 = shape_of((t, D), BF16), shape_of((t, D), F32), shape_of((t, FF), BF16)
    three16 = shape_of((t, 3 * D), BF16)
    small = vmem((t, D), BF16)
    wide = vmem((t, FF), BF16)
    three = vmem((t, 3 * D), BF16)
    probs_mem, scores_mem = vmem(probs_shape, BF16), vmem(scores_shape, F32)
    mask_mem = vmem((seqs, SLOTS, 2 * SLOTS), F32)
    mem_in, mem_out, mem_up, mem_down = (
        vmem((D, 3 * D), BF16), vmem((D, D), BF16), vmem((D, FF), BF16), vmem((FF, D), BF16),
    )

    acts0, qkv0, probs0 = chain.call(
        functools.partial(open_kernel, seqs), scal,
        (x0,) + vecs + weights[:2],
        [half_spec] + vec_specs + [HBM] * 2,
        [shape_of((t, 2 * D), BF16), three16, shape_of(probs_shape, BF16)],
        [HBM] * 3,
        [vmem((t, 2 * D), BF16), three, scores_mem, probs_mem, mem_in, mask_mem, dma((3,)), dma((3,))],
        8.0,
    )
    ff0, hidden0, slope0, y0, send1, keep1, y1, xgrad1, vgrad1 = chain.call(
        functools.partial(middle_kernel, seqs), scal,
        (x0, cot, acts0) + vecs + weights,
        [half_spec, half_spec, whole((t, 2 * D))] + vec_specs + [HBM] * 8,
        [shape_of((t, GRADS_AT), BF16), row32, wide16, row16, shape_of((t, GRADS_AT + GRAD_COLS + D), BF16),
         shape_of((t, GRAD_COLS), BF16), row16, row16, shape_of((4, D), F32)],
        [HBM] * 8 + [whole((4, D))],
        [mem_in, mem_out, mem_out, mem_up, mem_up, mem_down, mem_down,
         vmem((2, t, D), BF16), vmem((2, t, D), F32), wide, wide, vmem((2, t, D), BF16), small, small, three,
         scores_mem, probs_mem, mask_mem, wide, small, vmem((t, D), F32), small, three, small,
         dma((5 + 2 * NFT,)), dma((20,))],
        30.0,
    )
    send1_o = other_core(send1)
    ff0_o = other_core(ff0)

    def wgrads(name, terms, is_ff):
        ins, held, plan = [], [], []
        for (a0, a1), a_at, rows, (b0, b1), b_at, width in terms:
            ins += [a0, a1, b0, b1]
            held += [vmem((2 * t, rows), BF16), vmem((2 * t, width), BF16)]
            plan.append((rows, width, a_at, b_at))
        per, chunk = D // BLOCKS, D // 2
        half = shape_of((BLOCKS // 2, 8 if is_ff else 4, per, chunk), BF16)
        results = [vmem((4, BLOCKS, per, chunk), BF16)]
        if is_ff:
            results.append(vmem((FF // per, per, chunk), BF16))
        return chain.call(
            functools.partial(wgrad_kernel, plan, is_ff, table_of[name]), order, ins, [HBM] * len(ins), [half] * 2, [HBM] * 2,
            held + results + [dma((4 * len(terms),)), dma((2 * BLOCKS,))],
            8.0,
        )

    def fixed(col):
        return lambda core: (col, 0)

    def own_half(core):
        return pl.multiple_of(core * HALF_OUT, 128)

    def own_cot(core):
        return own_half(core), pl.multiple_of(core * t, 16)

    def other_cot(core):
        return own_half(core), pl.multiple_of((1 - core) * t, 16)

    def own_cols(core):
        return own_half(core), 0

    def own_xgrad(core):
        return pl.multiple_of(GRADS_AT + GRAD_COLS + core * HALF_OUT, 128), 0

    keep0, send0, hgrad0, mgrad0, vgrad0_ff = chain.call(
        ff_last_kernel, scal,
        (xgrad1, hidden0) + vecs[:2] + (slope0,) + weights[2:],
        [tok, tok] + vec_specs[:2] + [HBM] * 7,
        [shape_of((t, HALF_UP + HALF_OUT), BF16)] * 2 + [row32, row16, shape_of((4, D), F32)],
        [HBM] * 2 + [tok, tok, whole((4, D))],
        [mem_up, mem_down, mem_out, wide, wide, small, dma((3 + NFT,)), dma((4,))],
        10.0,
    )
    send0_o = other_core(send0)
    grads_at = GRADS_AT
    acts1, grads1 = (send1, send1_o), (keep1, send1_o)
    ff1 = Batch(
        wgrads(
            "ff1",
            [
                (acts1, (DENSE_AT,) * 2, D, grads1, (fixed(UG_AT), fixed(grads_at + UG_AT)), HALF_UP),
                (acts1, (ACTIVE_AT,) * 2, FF, (cot, cot), (own_cot, other_cot), HALF_OUT),
            ],
            True,
        ),
        bits_of["ff1"],
    )
    attn1 = Batch(
        wgrads(
            "attn1",
            [
                (acts1, (NORMED_AT,) * 2, D, grads1, (fixed(PG_AT), fixed(grads_at + PG_AT)), HALF_IN),
                (acts1, (MIXED_AT,) * 2, D, grads1, (fixed(BG_AT), fixed(grads_at + BG_AT)), HALF_OUT),
            ],
            False,
        ),
        bits_of["attn1"],
    )
    ff0_sum = Batch(
        wgrads(
            "ff0",
            [
                ((ff0, ff0_o), (DENSE_AT,) * 2, D, (keep0, send0_o), (fixed(0),) * 2, HALF_UP),
                ((ff0, ff0_o), (ACTIVE_AT,) * 2, FF, (xgrad1, send1_o), (own_cols, own_xgrad), HALF_OUT),
            ],
            True,
        ),
        bits_of["ff0"],
    )
    pkeep0, psend0, xgrad0, vgrad0_attn = chain.call(
        functools.partial(attn_last_kernel, seqs), scal,
        (x0, mgrad0, hgrad0) + vecs + (qkv0, probs0) + weights[:2],
        [half_spec, tok, tok] + vec_specs + [HBM] * 4,
        [shape_of((t, HALF_IN), BF16)] * 2 + [row16, shape_of((4, D), F32)],
        [HBM] * 3 + [whole((4, D))],
        [mem_in, three, probs_mem, vmem((PAIRS, SLOTS, 2 * SLOTS), F32), three, small, dma((3,)), dma((3,))],
        9.0,
    )
    psend0_o = other_core(psend0)
    tick(ff1)
    attn0 = Batch(
        wgrads(
            "attn0",
            [
                ((ff0, ff0_o), (NORMED_AT,) * 2, D, (pkeep0, psend0_o), (fixed(0),) * 2, HALF_IN),
                ((ff0, ff0_o), (MIXED_AT,) * 2, D, (keep0, send0_o), (fixed(HALF_UP),) * 2, HALF_OUT),
            ],
            False,
        ),
        bits_of["attn0"],
    )
    vgrad0 = jnp.concatenate([vgrad0_attn[:2], vgrad0_ff[2:]], axis=0)
    vec_sum = Vector(jnp.concatenate([vgrad0, vgrad1], axis=0))

    def settle_rows(pair):
        held = lax.optimization_barrier(tuple(pair) + tuple(chain.token))
        pair = held[:2]
        here = jnp.where(first, pair[0], pair[1])
        there = other_core(jnp.where(first, pair[1], pair[0]))
        both_rows = jnp.where(
            first, jnp.concatenate([here, there], 0), jnp.concatenate([there, here], 0)
        )
        return both_rows.reshape((1,) + tokens.shape)

    tick(attn1, vec_sum)
    layer_out = settle_rows((y0, y1))
    tick(ff0_sum)
    tick(attn1, vec_sum)
    tick(ff1)
    input_grads = settle_rows((xgrad0, xgrad1))
    tick(attn0, vec_sum)
    tick(attn1)
    tick(ff1)
    tick(ff0_sum, vec_sum)
    tick(attn0)
    tick(attn1)
    tick(ff0_sum, vec_sum)
    tick(attn0)
    tick(ff1)
    tick(ff0_sum)
    tick(attn0)
    for _ in range(4):
        tick(ff1, attn1, ff0_sum, attn0, vec_sum)
    per = D // dp

    def side(v):
        return v.transpose(1, 0, 2).reshape(v.shape[1], -1)

    def parts(ff, attn):
        if fast:
            ff, attn = ff.result, attn.result
            return side(attn[:3]), attn[3], side(ff[:4]), ff[4:].reshape(FF // dp, D // 2)
        (up, down), (both_attn,) = ff.result, attn.result
        return both_attn[:, :HALF_IN], both_attn[:, HALF_IN:], up, down

    shards = [parts(ff0_sum, attn0), parts(ff1, attn1)]

    def settle(a, b):
        here = jnp.where(first, a, b)
        there = other_core(jnp.where(first, b, a))
        return jnp.where(first, jnp.concatenate([here, there], -1), jnp.concatenate([there, here], -1))

    grad_in, grad_out, grad_up, grad_down = (
        settle(a, b)[None] for a, b in zip(shards[0], shards[1])
    )

    vec = vec_sum.result
    vec = jnp.where(first, vec[:4], vec[4:])
    vec = lax.dynamic_slice(vec, (0, me * per), (4, per))
    return (
        layer_out,
        input_grads,
        vec[0:1],
        vec[1:2],
        grad_in,
        grad_out,
        vec[2:3],
        vec[3:4],
        grad_up,
        grad_down,
    )


def solution(mesh):
    row = P(None, "dp", None, None)
    vec = P("section", None)
    mat = P("section", None, None)
    outs = P("section", None, "dp", None, None)
    out_vec = P("section", "dp")
    out_mat = P("section", "dp", None)
    return jax.shard_map(
        body,
        mesh=mesh,
        in_specs=(row, row, P(None, "dp"), vec, vec, mat, mat, vec, vec, mat, mat),
        out_specs=(outs, outs, out_vec, out_vec, out_mat, out_mat, out_vec, out_vec, out_mat, out_mat),
        check_vma=False,
    )
```

```python
import functools
import math

import jax
import jax.numpy as jnp
import numpy as np
from jax import lax
from jax.experimental import pallas as pl
from jax.experimental.pallas import tpu as pltpu
from jax.sharding import PartitionSpec as P

D = 768
HEADS = 12
HEAD = 64
FF = 3072
BLK = 16
SEQ = 64
SLOTS = 2 * SEQ
PAIRS = HEADS // 2
LANES = 2 * HEAD
BLOCKS = 16
FT = 1536
NFT = FF // FT

norm_eps = 1e-05
masked_score = -1000000000.0
gelu_c = math.sqrt(2.0 / math.pi)
gelu_a = 0.044715

F32 = jnp.float32
BF16 = jnp.bfloat16
VMEM_LIMIT = 63 * 1024 * 1024


def dot(a, b, ca=1, cb=0):
    return lax.dot_general(a, b, (((ca,), (cb,)), ((), ())), preferred_element_type=F32)


def rotary_tables():
    places = (np.arange(SLOTS) % SEQ).astype(np.float32)
    half = HEAD // 2
    freqs = (10000.0 ** (-np.arange(half).astype(np.float32) * 2.0 / HEAD)).astype(np.float32)
    angles = (places[:, None] * freqs[None, :]).astype(np.float32)
    cos, sin = np.cos(angles), np.sin(angles)
    return np.stack(
        [
            np.concatenate([cos] * 4, axis=1),
            np.concatenate([-sin, sin, -sin, sin], axis=1),
        ]
    ).astype(np.float32)


def swap_halves(v):
    lane = lax.broadcasted_iota(jnp.int32, v.shape, 1)
    first = lax.rem(lane, HEAD) < HEAD // 2
    return jnp.where(first, pltpu.roll(v, LANES - 32, 1), pltpu.roll(v, 32, 1))


def open_keys_t(length):
    key = lax.broadcasted_iota(jnp.int32, (SLOTS, SLOTS), 0)
    query = lax.broadcasted_iota(jnp.int32, (SLOTS, SLOTS), 1)
    key_clean, query_clean = key >= SEQ, query >= SEQ
    key_place, query_place = lax.rem(key, SEQ), lax.rem(query, SEQ)
    kb, qb = lax.div(key_place, BLK), lax.div(query_place, BLK)
    both_noisy = jnp.logical_and(jnp.logical_not(key_clean), jnp.logical_not(query_clean))
    both_clean = jnp.logical_and(key_clean, query_clean)
    crossed = jnp.logical_and(key_clean, jnp.logical_not(query_clean))
    structure = (
        (both_noisy & (kb == qb)) | (crossed & (kb < qb)) | (both_clean & (kb <= qb))
    )
    return structure & ((key_place < length) | (key == query))


def norm_stats(v):
    centered = v - jnp.mean(v, axis=-1, keepdims=True)
    spread = jnp.mean(centered * centered, axis=-1, keepdims=True)
    return centered, lax.rsqrt(spread + norm_eps)


def norm_back(dy, source, gain):
    centered, scale = norm_stats(source)
    xhat = centered * scale
    g = dy * gain
    part = scale * (
        g
        - jnp.mean(g, axis=-1, keepdims=True)
        - xhat * jnp.mean(g * xhat, axis=-1, keepdims=True)
    )
    return part, jnp.sum(dy * xhat, axis=0, keepdims=True), jnp.sum(dy, axis=0, keepdims=True)


def col_pieces(rows, cols, n):
    w = cols // n
    return [(slice(0, rows), slice(i * w, (i + 1) * w)) for i in range(n)]


def row_pieces(rows, cols, n):
    w = rows // n
    return [(slice(i * w, (i + 1) * w), slice(0, cols)) for i in range(n)]


IN_PIECES = col_pieces(D, 3 * D, 3)
IN_ALL = col_pieces(D, 3 * D, 1)
OUT_PIECES = row_pieces(D, D, 1)
UP_PIECES = col_pieces(D, FF, NFT)
DOWN_PIECES = row_pieces(FF, D, 1)


class Feed:
    def __init__(self, own):
        self.own, self.queue = own, []

    def weight(self, mine, other, piece, dst, sem):
        self.queue.append((mine, other, piece, dst, sem))
        return pltpu.make_async_copy(mine.at[piece], dst.at[piece], sem)

    def begin(self, count=None):
        count = len(self.queue) if count is None else count
        queue, self.queue = self.queue[:count], self.queue[count:]

        @pl.when(self.own)
        def _():
            for mine, _, piece, dst, sem in queue:
                pltpu.make_async_copy(mine.at[piece], dst.at[piece], sem).start()

        @pl.when(jnp.logical_not(self.own))
        def _():
            for _, other, piece, dst, sem in queue:
                pltpu.make_async_copy(other.at[piece], dst.at[piece], sem).start()


class Drain:
    def __init__(self, sems):
        self.sems, self.copies = sems, []

    def put(self, src, dst):
        c = pltpu.make_async_copy(src, dst, self.sems.at[len(self.copies)])
        c.start()
        self.copies.append(c)
        return c

    def finish(self, skip=()):
        for c in self.copies:
            if not any(c is done for done in skip):
                c.wait()


def make_mask(mask, seqs, scal):
    for s in range(seqs):
        keep = open_keys_t(scal[1 + scal[0] * seqs + s])
        shut = jnp.where(keep, 0.0, 1.0)
        mask[s, :, 0:SLOTS] = shut
        mask[s, :, SLOTS : 2 * SLOTS] = shut


def pair_tile(ref, rows, part, p):
    lo = part * D + p * LANES
    return ref[rows, lo : lo + LANES]


def both_heads(v):
    left = lax.broadcasted_iota(jnp.int32, (SLOTS, LANES), 1) < HEAD
    zero = jnp.zeros((SLOTS, LANES), BF16)
    return jnp.concatenate([jnp.where(left, v, zero), jnp.where(left, zero, v)], axis=0)


def norm_into(dst, source, gain, bias):
    centered, scale = norm_stats(source)
    dst[...] = (centered * scale * gain + bias).astype(BF16)


def project(seqs, normed, w_in, waits, rot_ref, qkv):
    cos, sin = rot_ref[0], rot_ref[1]
    for part in range(3):
        if part < len(waits):
            waits[part].wait()
        for tile in range(D // 256):
            lo = part * D + tile * 256
            val = dot(normed[...], w_in[:, lo : lo + 256])
            if part == 2:
                qkv[:, lo : lo + 256] = val.astype(BF16)
                continue
            for u in range(2):
                for s in range(seqs):
                    v = val[s * SLOTS : (s + 1) * SLOTS, u * LANES : (u + 1) * LANES]
                    v = v * cos + swap_halves(v) * sin
                    if part == 0:
                        v = v * HEAD ** (-0.5)
                    qkv[
                        s * SLOTS : (s + 1) * SLOTS, lo + u * LANES : lo + (u + 1) * LANES
                    ] = v.astype(BF16)


def attend(seqs, qkv, mask, scores, probs, mixed):
    for s in range(seqs):
        rows = slice(s * SLOTS, (s + 1) * SLOTS)
        for p in range(PAIRS):
            scores[s * PAIRS + p] = dot(
                pair_tile(qkv, rows, 1, p), both_heads(pair_tile(qkv, rows, 0, p)), 1, 1
            )
        for p in range(PAIRS):
            i = s * PAIRS + p
            st = jnp.where(mask[s] > 0.5, masked_score, scores[i])
            e = jnp.exp(st - jnp.max(st, axis=0, keepdims=True))
            low = (e * (1.0 / jnp.sum(e, axis=0, keepdims=True))).astype(BF16)
            probs[i, 0:SLOTS] = low[:, :SLOTS]
            probs[i, SLOTS : 2 * SLOTS] = low[:, SLOTS:]
        for p in range(PAIRS):
            mixed[rows, p * LANES : (p + 1) * LANES] = dot(
                probs[s * PAIRS + p], both_heads(pair_tile(qkv, rows, 2, p)), 0, 0
            ).astype(BF16)


def activate(dense, w_up, slope, active, waits):
    for t in range(FF // 256):
        if t * 256 % FT == 0:
            waits[t * 256 // FT].wait()
        cols = slice(t * 256, (t + 1) * 256)
        u = dot(dense[...], w_up[:, cols])
        u2 = u * u
        th = jnp.tanh(u * (gelu_c + (gelu_c * gelu_a) * u2))
        h = 0.5 * (1.0 + th)
        active[:, cols] = (u * h).astype(BF16)
        slope[:, cols] = (
            h + u * (1.0 - th * th) * (0.5 * gelu_c + (1.5 * gelu_c * gelu_a) * u2)
        ).astype(BF16)


def open_kernel(seqs, scal, x_ref, vec_mine, vec_other, rot_ref, in_mine, in_other,
                acts_o, qkv_o, probs_o,
                acts, qkv, scores, probs, w_in, mask, sems, out_sems):
    own = scal[0] == 0
    feed, drain = Feed(own), Drain(out_sems)
    w_waits = [feed.weight(in_mine, in_other, IN_PIECES[i], w_in, sems.at[i]) for i in range(3)]
    feed.begin()
    vec = jnp.where(own, vec_mine[...], vec_other[...])
    normed, mixed = acts.at[:, 0:D], acts.at[:, D : 2 * D]
    norm_into(normed, x_ref[...].astype(F32), vec[0:1], vec[1:2])
    make_mask(mask, seqs, scal)
    project(seqs, normed, w_in, w_waits, rot_ref, qkv)
    drain.put(qkv, qkv_o)
    attend(seqs, qkv, mask, scores, probs, mixed)
    drain.put(probs, probs_o)
    drain.put(acts, acts_o)
    drain.finish()


def halves(core, width):
    keep = pl.ds(pl.multiple_of(core * width, 128), width)
    send = pl.ds(pl.multiple_of((1 - core) * width, 128), width)
    return keep, send


def split_out(drain, core, src, width, at, keep_o, send_o, send_base):
    keep, send = halves(core, width)
    drain.put(src.at[:, keep], keep_o.at[:, at : at + width])
    drain.put(src.at[:, send], send_o.at[:, send_base + at : send_base + at + width])


def ff_back(r_ref, hidden, gain, w_up, w_down, w_out, slope, ug, bgrad, hgrad, mgrad, vgrad, waits):
    down_waits, up_waits, out_waits = waits
    for t in range(FF // 256):
        if t * 256 % FT == 0 and down_waits:
            for c in down_waits[t * 256 // FT]:
                c.wait()
        cols = slice(t * 256, (t + 1) * 256)
        ug[:, cols] = (dot(r_ref[...], w_down[cols, :], 1, 1) * slope[:, cols].astype(F32)).astype(BF16)
    for c in up_waits:
        c.wait()
    part, dg, db = norm_back(dot(ug[...], w_up[...], 1, 1), hidden[...], gain)
    vgrad[2:3] = dg
    vgrad[3:4] = db
    total = r_ref[...].astype(F32) + part
    hgrad[...] = total
    bgrad[...] = total.astype(BF16)
    for c in out_waits:
        c.wait()
    mgrad[...] = dot(bgrad[...], w_out[...], 1, 1).astype(BF16)


def attn_back(seqs, x_ref, gain, rot_ref, w_in, qkv, probs, dpt, mgrad, hgrad, pgrad, xgrad, vgrad, waits):
    in_waits, w_waits = waits
    cos, sin = rot_ref[0], rot_ref[1]
    for c in in_waits:
        c.wait()
    for s in range(seqs):
        rows = slice(s * SLOTS, (s + 1) * SLOTS)
        for p in range(PAIRS):
            dm = both_heads(mgrad[rows, p * LANES : (p + 1) * LANES])
            dpt[p] = dot(pair_tile(qkv, rows, 2, p), dm, 1, 1)
        for p in range(PAIRS):
            i = s * PAIRS + p
            low = jnp.concatenate([probs[i, 0:SLOTS], probs[i, SLOTS : 2 * SLOTS]], axis=1)
            pt = low.astype(F32)
            pd = pt * dpt[p]
            dst = (pd - pt * jnp.sum(pd, axis=0, keepdims=True)).astype(BF16)
            dm = both_heads(mgrad[rows, p * LANES : (p + 1) * LANES])
            dv = dot(low, dm)
            dk = dot(dst, both_heads(pair_tile(qkv, rows, 0, p)))
            stacked = jnp.concatenate([dst[:, :SLOTS], dst[:, SLOTS:]], axis=0)
            dq = dot(stacked, both_heads(pair_tile(qkv, rows, 1, p)), 0, 0) * HEAD ** (-0.5)
            dq = dq * cos - swap_halves(dq) * sin
            dk = dk * cos - swap_halves(dk) * sin
            pgrad[rows, p * LANES : (p + 1) * LANES] = dq.astype(BF16)
            pgrad[rows, D + p * LANES : D + (p + 1) * LANES] = dk.astype(BF16)
            pgrad[rows, 2 * D + p * LANES : 2 * D + (p + 1) * LANES] = dv.astype(BF16)
    for c in w_waits:
        c.wait()
    part, dg, db = norm_back(dot(pgrad[...], w_in[...], 1, 1), x_ref[...].astype(F32), gain)
    vgrad[0:1] = dg
    vgrad[1:2] = db
    xgrad[...] = (hgrad[...] + part).astype(BF16)


ACTIVE_AT, DENSE_AT, NORMED_AT, MIXED_AT = 0, FF, FF + D, FF + 2 * D
HALF_IN, HALF_OUT, HALF_UP = 3 * D // 2, D // 2, FF // 2
UG_AT, PG_AT, BG_AT = 0, HALF_UP, HALF_UP + HALF_IN
GRAD_COLS = HALF_UP + HALF_IN + HALF_OUT
GRADS_AT = FF + 3 * D


def middle_kernel(seqs, scal, x_ref, cot_ref, acts0, vec_mine, vec_other, rot_ref,
                  in_mine, in_other, out_mine, out_other, up_mine, up_other, down_mine, down_other,
                  ff0_o, hidden0_o, slope0_o, y0_o, send1_o, keep1_o, y1_o, xgrad1_o, vgrad_ref,
                  w_in, w_out0, w_out1, w_up0, w_up1, w_down0, w_down1,
                  dense, hidden, slope, active, y, normed, mixed, qkv, scores, probs, mask,
                  ug, bgrad, hgrad, mgrad, pgrad, xgrad, sems, drain_sems):
    core = scal[0]
    own = core == 0
    drain = Drain(drain_sems)

    def weights(feed, base, w_out, w_up, w_down):
        out = feed.weight(out_mine, out_other, OUT_PIECES[0], w_out, sems.at[base])
        up = [feed.weight(up_mine, up_other, UP_PIECES[i], w_up, sems.at[base + 1 + i]) for i in range(NFT)]
        down = feed.weight(down_mine, down_other, DOWN_PIECES[0], w_down, sems.at[base + 1 + NFT])
        return out, up, down

    feed0, feed1 = Feed(own), Feed(jnp.logical_not(own))
    waits0 = weights(feed0, 0, w_out0, w_up0, w_down0)
    in_waits = [feed1.weight(in_mine, in_other, IN_ALL[0], w_in, sems.at[4 + 2 * NFT])]
    waits1 = weights(feed1, 2 + NFT, w_out1, w_up1, w_down1)
    feed0.begin(1 + NFT)
    vec0 = jnp.where(own, vec_mine[...], vec_other[...])
    vec1 = jnp.where(own, vec_other[...], vec_mine[...])
    make_mask(mask, seqs, scal)

    def tail(layer, x, mixed_in, w_out, w_up, w_down, waits, vec, held, following):
        waits[0].wait()
        if layer == 0:
            feed0.begin()
        hidden[layer] = x + dot(mixed_in[...], w_out[...])
        norm_into(dense.at[layer], hidden[layer], vec[2:3], vec[3:4])
        for c in held:
            c.wait()
        activate(dense.at[layer], w_up, slope, active, waits[1])
        waits[2].wait()
        following()
        y[layer] = (hidden[layer] + dot(active[...], w_down[...])).astype(BF16)

    tail(
        0, x_ref[...].astype(F32), acts0.at[:, D : 2 * D], w_out0, w_up0, w_down0, waits0, vec0, (), feed1.begin
    )
    copies = [drain.put(slope, slope0_o), drain.put(active, ff0_o.at[:, ACTIVE_AT : ACTIVE_AT + FF])]
    drain.put(dense.at[0], ff0_o.at[:, DENSE_AT : DENSE_AT + D])
    drain.put(acts0, ff0_o.at[:, NORMED_AT : NORMED_AT + 2 * D])
    drain.put(hidden.at[0], hidden0_o)
    drain.put(y.at[0], y0_o)
    norm_into(normed, y[0].astype(F32), vec1[0:1], vec1[1:2])
    project(seqs, normed, w_in, in_waits, rot_ref, qkv)
    attend(seqs, qkv, mask, scores, probs, mixed)
    tail(
        1, y[0].astype(F32), mixed, w_out1, w_up1, w_down1, waits1, vec1, copies, lambda: None
    )
    drain.put(active, send1_o.at[:, ACTIVE_AT : ACTIVE_AT + FF])
    drain.put(dense.at[1], send1_o.at[:, DENSE_AT : DENSE_AT + D])
    drain.put(normed, send1_o.at[:, NORMED_AT : NORMED_AT + D])
    drain.put(mixed, send1_o.at[:, MIXED_AT : MIXED_AT + D])
    drain.put(y.at[1], y1_o)
    ff_back(
        cot_ref, hidden.at[1], vec1[2:3], w_up1, w_down1, w_out1, slope, ug, bgrad, hgrad, mgrad, vgrad_ref,
        ((), (), ()),
    )
    split_out(drain, core, ug, HALF_UP, UG_AT, keep1_o, send1_o, GRADS_AT)
    split_out(drain, core, bgrad, HALF_OUT, BG_AT, keep1_o, send1_o, GRADS_AT)
    attn_back(
        seqs, y.at[0], vec1[0:1], rot_ref, w_in, qkv, probs, scores, mgrad, hgrad, pgrad, xgrad, vgrad_ref,
        ((), ()),
    )
    split_out(drain, core, pgrad, HALF_IN, PG_AT, keep1_o, send1_o, GRADS_AT)
    drain.put(xgrad, xgrad1_o)
    drain.put(xgrad, send1_o.at[:, GRADS_AT + GRAD_COLS : GRADS_AT + GRAD_COLS + D])
    drain.finish(copies)


def ff_last_kernel(scal, r_ref, hidden_ref, vec_mine, vec_other, slope_ref,
                   out_mine, out_other, up_mine, up_other, down_mine, down_other,
                   keep0_o, send0_o, hgrad_ref, mgrad_ref, vgrad_ref,
                   w_up, w_down, w_out, slope, ug, bgrad, sems, drain_sems):
    core = scal[0]
    own = core == 0
    feed, drain = Feed(own), Drain(drain_sems)
    pieces = row_pieces(FF, D, NFT)
    tiles = []
    for i in range(NFT):
        cols = slice(i * FT, (i + 1) * FT)
        load = pltpu.make_async_copy(slope_ref.at[:, cols], slope.at[:, cols], sems.at[1 + NFT + i])
        tiles.append([feed.weight(down_mine, down_other, pieces[i], w_down, sems.at[1 + i]), load])
        feed.begin()
        load.start()
    ups = [feed.weight(up_mine, up_other, UP_PIECES[i], w_up, sems.at[1 + 2 * NFT + i]) for i in range(NFT)]
    out = [feed.weight(out_mine, out_other, OUT_PIECES[0], w_out, sems.at[0])]
    feed.begin()
    vec = jnp.where(own, vec_mine[...], vec_other[...])
    ff_back(
        r_ref, hidden_ref, vec[2:3], w_up, w_down, w_out, slope, ug, bgrad, hgrad_ref, mgrad_ref, vgrad_ref,
        (tiles, ups, out),
    )
    split_out(drain, core, ug, HALF_UP, UG_AT, keep0_o, send0_o, 0)
    split_out(drain, core, bgrad, HALF_OUT, UG_AT + HALF_UP, keep0_o, send0_o, 0)
    drain.finish()


def attn_last_kernel(seqs, scal, x_ref, mgrad_ref, hgrad_ref, vec_mine, vec_other, rot_ref, qkv_ref, probs_ref,
                     in_mine, in_other,
                     keep0_o, send0_o, xgrad_o, vgrad_ref,
                     w_in, qkv, probs, dpt, pgrad, xgrad, sems, drain_sems):
    core = scal[0]
    own = core == 0
    feed, drain = Feed(own), Drain(drain_sems)
    plain = [
        pltpu.make_async_copy(src, dst, sems.at[i])
        for i, (src, dst) in enumerate(((qkv_ref, qkv), (probs_ref, probs)))
    ]
    for c in plain:
        c.start()
    w_waits = [feed.weight(in_mine, in_other, IN_ALL[0], w_in, sems.at[2])]
    feed.begin()
    vec = jnp.where(own, vec_mine[...], vec_other[...])
    attn_back(
        seqs, x_ref, vec[0:1], rot_ref, w_in, qkv, probs, dpt, mgrad_ref, hgrad_ref, pgrad, xgrad, vgrad_ref,
        (plain, w_waits),
    )
    split_out(drain, core, pgrad, HALF_IN, 0, keep0_o, send0_o, 0)
    drain.put(xgrad, xgrad_o)
    drain.finish()


def wgrad_kernel(terms, is_ff, table, scal, *refs):
    n = len(terms)
    srcs, (keep_o, send_o) = refs[: 4 * n], refs[4 * n : 4 * n + 2]
    held, rest = refs[4 * n + 2 : 6 * n + 2], refs[6 * n + 2 :]
    results, (sems, drain_sems) = rest[:-2], rest[-2:]
    core = scal[0]
    loads = []
    for i, (rows, width, a_at, b_at) in enumerate(terms):
        tokens = held[2 * i].shape[0] // 2
        for j in range(2):
            mine = slice(j * tokens, (j + 1) * tokens)
            col, row = b_at[j](core)
            src = srcs[4 * i + 2 + j].at[pl.ds(row, tokens), pl.ds(col, width)]
            loads.append(pltpu.make_async_copy(src, held[2 * i + 1].at[mine], sems.at[len(loads)]))
            src = srcs[4 * i + j].at[:, a_at[j] : a_at[j] + rows]
            loads.append(pltpu.make_async_copy(src, held[2 * i].at[mine], sems.at[len(loads)]))
    for c in loads[:4]:
        c.start()
    half, per, chunk = BLOCKS // 2, D // BLOCKS, D // 2
    drain = Drain(drain_sems)

    def wait_for(i):
        for c in loads[4 * i : 4 * i + 4]:
            c.wait()
        for c in loads[4 * i + 4 : 4 * i + 8]:
            c.start()

    def send_block(r, src, at, count):
        dst = keep_o.at[r] if r < half else send_o.at[r - half]
        drain.put(src, dst.at[at : at + count])

    def side_by_side(i, res, base):
        a, b = held[2 * i], held[2 * i + 1]
        count = terms[i][1] // chunk
        for j in range(0, count, 2):
            m = min(2, count - j)
            val = dot(a[...], b[:, j * chunk : (j + m) * chunk], 0, 0).astype(BF16)
            for k in range(m):
                res[base + j + k] = val[:, k * chunk : (k + 1) * chunk].reshape(BLOCKS, per, chunk)
        return base + count

    wait_for(0)
    if is_ff:
        count = side_by_side(0, results[0], 0)
        for r in list(range(half, BLOCKS)) + list(range(half)):
            send_block(r, results[0].at[:, scal[table + r]], 0, count)
        wait_for(1)
        a, b = held[2:4]
        deep = FF // D
        for q in range(deep):
            val = dot(a[:, q * D : (q + 1) * D], b[...], 0, 0).astype(BF16)
            results[1][q * BLOCKS : (q + 1) * BLOCKS] = val.reshape(BLOCKS, per, chunk)
        for r in list(range(half, BLOCKS)) + list(range(half)):
            send_block(r, results[1].at[pl.ds(scal[table + r] * deep, deep)], count, deep)
    else:
        count = side_by_side(0, results[0], 0)
        wait_for(1)
        count = side_by_side(1, results[0], count)
        for r in list(range(half, BLOCKS)) + list(range(half)):
            send_block(r, results[0].at[:, scal[table + r]], 0, count)
    drain.finish()


def whole(shape):
    return pl.BlockSpec(shape, lambda i, s: (0,) * len(shape))


def shape_of(shape, dtype):
    return jax.ShapeDtypeStruct(shape, dtype)


HBM = pl.BlockSpec(memory_space=pl.ANY)


class Chain:
    def __init__(self):
        self.token = ()

    def call(self, kernel, scal, ins, in_specs, outs, out_specs, scratch, micros, after=()):
        after = tuple(self.token) + tuple(after)
        n, extra = 1 + len(ins), len(after)

        def ordered(*refs):
            kernel(*refs[:n], *refs[n + extra :])

        result = pl.pallas_call(
            ordered,
            grid_spec=pltpu.PrefetchScalarGridSpec(
                num_scalar_prefetch=1,
                grid=(1,),
                in_specs=list(in_specs) + [HBM] * extra,
                out_specs=out_specs,
                scratch_shapes=scratch,
            ),
            out_shape=outs,
            compiler_params=pltpu.CompilerParams(vmem_limit_bytes=VMEM_LIMIT),
            cost_estimate=pl.CostEstimate(
                flops=int(micros * 1e6), bytes_accessed=2**10, transcendentals=0
            ),
        )(scal, *ins, *after)
        self.token = (result[-1],)
        return result


def axis_pairs(first, second, size):
    return [(i, i ^ first) for i in range(size)] + [
        (size + i, size + (i ^ second)) for i in range(size)
    ]


def body(
    tokens, cotangent, lengths, mixer_gain, mixer_bias, project_in, project_out,
    dense_gain, dense_bias, up_weight, down_weight,
):
    micro, rows = tokens.shape[:2]
    total = micro * rows
    seqs = total // 2
    t = seqs * SLOTS
    core = lax.axis_index("section")
    first = core == 0
    me = lax.axis_index("dp")
    dp = lax.axis_size("dp")
    fast = dp == BLOCKS
    both = ("section", "dp")
    chain = Chain()

    def other_core(v):
        return lax.ppermute(v, "section", [(0, 1), (1, 0)])

    mine = {
        "vec": jnp.concatenate([mixer_gain, mixer_bias, dense_gain, dense_bias], axis=0),
        "in": project_in[0],
        "out": project_out[0],
        "up": up_weight[0],
        "down": down_weight[0],
    }
    other = {name: other_core(mine[name]) for name in ("vec", "in")}
    other["in"], out_held, up_held, down_held = lax.optimization_barrier(
        (other["in"], mine["out"], mine["up"], mine["down"])
    )
    other["out"], other["up"], other["down"] = map(other_core, (out_held, up_held, down_held))
    rot = jnp.asarray(rotary_tables())
    scal = jnp.concatenate([core.reshape(1), lengths.reshape(total)]).astype(jnp.int32)

    steps = {"A": (1, 2), "B": (2, 1), "l": (4, 8), "h": (8, 4)}
    names = ("ff1", "attn1", "ff0", "attn0")
    orders = dict(zip(names, ("AlBh", "lABh", "AlBh", "ABlh")))
    bits_of = {name: [steps[c] for c in orders[name]] for name in names}
    table_of = {name: 1 + BLOCKS * i for i, name in enumerate(names)}
    xy_bits = [steps[c] for c in "ABlh"]

    def places(bits):
        if not fast:
            return jnp.asarray(np.arange(BLOCKS), jnp.int32)
        rel = np.zeros((2, BLOCKS), np.int32)
        for c in range(2):
            for r in range(BLOCKS):
                for stage in range(4):
                    if r >> (3 - stage) & 1:
                        rel[c, r] ^= bits[stage][c]
        return me ^ jnp.where(first, jnp.asarray(rel[0]), jnp.asarray(rel[1]))

    order = jnp.concatenate([core.reshape(1)] + [places(bits_of[name]) for name in names]).astype(jnp.int32)

    class Batch:
        def __init__(self, pair, bits):
            self.keep, self.send = pair
            self.bits, self.stage, self.result = bits, 0, None
            if not fast:
                flat = jnp.concatenate(pair, axis=0).astype(F32)
                n, count, per, chunk = flat.shape
                side = flat[:, :4].transpose(0, 2, 1, 3).reshape(n * per, 4 * chunk)
                self.result = [lax.psum_scatter(side, "dp", scatter_dimension=0, tiled=True)]
                if count > 4:
                    deep = flat[:, 4:].reshape(n * 4 * per, chunk)
                    self.result.append(lax.psum_scatter(deep, "dp", scatter_dimension=0, tiled=True))
            else:
                self.start()

        def start(self):
            self.got = lax.ppermute(self.send, both, axis_pairs(*self.bits[self.stage], dp))
            self.stage += 1

        def advance(self):
            half = self.keep.shape[0] // 2
            if half == 0:
                self.result = self.keep[0].astype(F32) + self.got[0].astype(F32)
                return self.result
            self.send, self.keep = self.keep[half:] + self.got[half:], self.keep[:half] + self.got[:half]
            return self.send

    class Vector:
        def __init__(self, value):
            self.value, self.stage, self.result = value, 0, None
            if not fast:
                self.result = lax.psum(value, both)
            else:
                self.got = other_core(value)

        def held(self):
            return [self.value, self.got]

        def start(self):
            self.got = lax.ppermute(self.value, both, axis_pairs(*xy_bits[self.stage], dp))
            self.stage += 1

        def advance(self):
            self.value = self.value + self.got
            if self.stage == 4:
                self.result = self.value
            return self.value

    def tick(*batches):
        batches = [b for b in batches if b.result is None]
        if not batches:
            return
        held = []
        for b in batches:
            held += [b.value, b.got] if isinstance(b, Vector) else [b.keep, b.got]
        held = lax.optimization_barrier(tuple(held) + tuple(chain.token))
        tokens_out = []
        for i, b in enumerate(batches):
            if isinstance(b, Vector):
                b.value, b.got = held[2 * i], held[2 * i + 1]
            else:
                b.keep, b.got = held[2 * i], held[2 * i + 1]
            tokens_out.append(b.advance())
        for b in batches:
            if b.result is None:
                b.start()
        chain.token = tuple(tokens_out)

    x0 = tokens.reshape(total * SLOTS, D)
    cot = cotangent.reshape(total * SLOTS, D)
    half_spec = pl.BlockSpec((t, D), lambda i, s: (s[0], 0))
    tok = whole((t, D))
    vec_spec, rot_spec = whole((4, D)), whole((2, SLOTS, LANES))
    scores_shape = (seqs * PAIRS, SLOTS, 2 * SLOTS)
    probs_shape = (seqs * PAIRS, 2 * SLOTS, SLOTS)
    vmem, dma = pltpu.VMEM, pltpu.SemaphoreType.DMA
    vecs = (mine["vec"], other["vec"], rot)
    vec_specs = [vec_spec, vec_spec, rot_spec]
    weights = (
        mine["in"], other["in"], mine["out"], other["out"],
        mine["up"], other["up"], mine["down"], other["down"],
    )
    row16, row32, wide16 = shape_of((t, D), BF16), shape_of((t, D), F32), shape_of((t, FF), BF16)
    three16 = shape_of((t, 3 * D), BF16)
    small = vmem((t, D), BF16)
    wide = vmem((t, FF), BF16)
    three = vmem((t, 3 * D), BF16)
    probs_mem, scores_mem = vmem(probs_shape, BF16), vmem(scores_shape, F32)
    mask_mem = vmem((seqs, SLOTS, 2 * SLOTS), F32)
    mem_in, mem_out, mem_up, mem_down = (
        vmem((D, 3 * D), BF16), vmem((D, D), BF16), vmem((D, FF), BF16), vmem((FF, D), BF16),
    )

    acts0, qkv0, probs0 = chain.call(
        functools.partial(open_kernel, seqs), scal,
        (x0,) + vecs + weights[:2],
        [half_spec] + vec_specs + [HBM] * 2,
        [shape_of((t, 2 * D), BF16), three16, shape_of(probs_shape, BF16)],
        [HBM] * 3,
        [vmem((t, 2 * D), BF16), three, scores_mem, probs_mem, mem_in, mask_mem, dma((3,)), dma((3,))],
        8.0,
    )
    ff0, hidden0, slope0, y0, send1, keep1, y1, xgrad1, vgrad1 = chain.call(
        functools.partial(middle_kernel, seqs), scal,
        (x0, cot, acts0) + vecs + weights,
        [half_spec, half_spec, whole((t, 2 * D))] + vec_specs + [HBM] * 8,
        [shape_of((t, GRADS_AT), BF16), row32, wide16, row16, shape_of((t, GRADS_AT + GRAD_COLS + D), BF16),
         shape_of((t, GRAD_COLS), BF16), row16, row16, shape_of((4, D), F32)],
        [HBM] * 8 + [whole((4, D))],
        [mem_in, mem_out, mem_out, mem_up, mem_up, mem_down, mem_down,
         vmem((2, t, D), BF16), vmem((2, t, D), F32), wide, wide, vmem((2, t, D), BF16), small, small, three,
         scores_mem, probs_mem, mask_mem, wide, small, vmem((t, D), F32), small, three, small,
         dma((5 + 2 * NFT,)), dma((20,))],
        30.0,
    )
    send1_o = other_core(send1)
    ff0_o = other_core(ff0)

    def wgrads(name, terms, is_ff):
        ins, held, plan = [], [], []
        for (a0, a1), a_at, rows, (b0, b1), b_at, width in terms:
            ins += [a0, a1, b0, b1]
            held += [vmem((2 * t, rows), BF16), vmem((2 * t, width), BF16)]
            plan.append((rows, width, a_at, b_at))
        per, chunk = D // BLOCKS, D // 2
        half = shape_of((BLOCKS // 2, 8 if is_ff else 4, per, chunk), BF16)
        results = [vmem((4, BLOCKS, per, chunk), BF16)]
        if is_ff:
            results.append(vmem((FF // per, per, chunk), BF16))
        return chain.call(
            functools.partial(wgrad_kernel, plan, is_ff, table_of[name]), order, ins, [HBM] * len(ins), [half] * 2, [HBM] * 2,
            held + results + [dma((4 * len(terms),)), dma((2 * BLOCKS,))],
            8.0,
        )

    def fixed(col):
        return lambda core: (col, 0)

    def own_half(core):
        return pl.multiple_of(core * HALF_OUT, 128)

    def own_cot(core):
        return own_half(core), pl.multiple_of(core * t, 16)

    def other_cot(core):
        return own_half(core), pl.multiple_of((1 - core) * t, 16)

    def own_cols(core):
        return own_half(core), 0

    def own_xgrad(core):
        return pl.multiple_of(GRADS_AT + GRAD_COLS + core * HALF_OUT, 128), 0

    keep0, send0, hgrad0, mgrad0, vgrad0_ff = chain.call(
        ff_last_kernel, scal,
        (xgrad1, hidden0) + vecs[:2] + (slope0,) + weights[2:],
        [tok, tok] + vec_specs[:2] + [HBM] * 7,
        [shape_of((t, HALF_UP + HALF_OUT), BF16)] * 2 + [row32, row16, shape_of((4, D), F32)],
        [HBM] * 2 + [tok, tok, whole((4, D))],
        [mem_up, mem_down, mem_out, wide, wide, small, dma((1 + 3 * NFT,)), dma((4,))],
        10.0,
    )
    send0_o = other_core(send0)
    grads_at = GRADS_AT
    acts1, grads1 = (send1, send1_o), (keep1, send1_o)
    ff1 = Batch(
        wgrads(
            "ff1",
            [
                (acts1, (DENSE_AT,) * 2, D, grads1, (fixed(UG_AT), fixed(grads_at + UG_AT)), HALF_UP),
                (acts1, (ACTIVE_AT,) * 2, FF, (cot, cot), (own_cot, other_cot), HALF_OUT),
            ],
            True,
        ),
        bits_of["ff1"],
    )
    attn1 = Batch(
        wgrads(
            "attn1",
            [
                (acts1, (NORMED_AT,) * 2, D, grads1, (fixed(PG_AT), fixed(grads_at + PG_AT)), HALF_IN),
                (acts1, (MIXED_AT,) * 2, D, grads1, (fixed(BG_AT), fixed(grads_at + BG_AT)), HALF_OUT),
            ],
            False,
        ),
        bits_of["attn1"],
    )
    ff0_sum = Batch(
        wgrads(
            "ff0",
            [
                ((ff0, ff0_o), (DENSE_AT,) * 2, D, (keep0, send0_o), (fixed(0),) * 2, HALF_UP),
                ((ff0, ff0_o), (ACTIVE_AT,) * 2, FF, (xgrad1, send1_o), (own_cols, own_xgrad), HALF_OUT),
            ],
            True,
        ),
        bits_of["ff0"],
    )
    pkeep0, psend0, xgrad0, vgrad0_attn = chain.call(
        functools.partial(attn_last_kernel, seqs), scal,
        (x0, mgrad0, hgrad0) + vecs + (qkv0, probs0) + weights[:2],
        [half_spec, tok, tok] + vec_specs + [HBM] * 4,
        [shape_of((t, HALF_IN), BF16)] * 2 + [row16, shape_of((4, D), F32)],
        [HBM] * 3 + [whole((4, D))],
        [mem_in, three, probs_mem, vmem((PAIRS, SLOTS, 2 * SLOTS), F32), three, small, dma((3,)), dma((3,))],
        9.0,
    )
    psend0_o = other_core(psend0)
    tick(ff1)
    tick(attn1)
    attn0 = Batch(
        wgrads(
            "attn0",
            [
                ((ff0, ff0_o), (NORMED_AT,) * 2, D, (pkeep0, psend0_o), (fixed(0),) * 2, HALF_IN),
                ((ff0, ff0_o), (MIXED_AT,) * 2, D, (keep0, send0_o), (fixed(HALF_UP),) * 2, HALF_OUT),
            ],
            False,
        ),
        bits_of["attn0"],
    )
    vgrad0 = jnp.concatenate([vgrad0_attn[:2], vgrad0_ff[2:]], axis=0)
    vec_sum = Vector(jnp.concatenate([vgrad0, vgrad1], axis=0))

    def settle_rows(pair):
        held = lax.optimization_barrier(tuple(pair) + tuple(chain.token))
        pair = held[:2]
        here = jnp.where(first, pair[0], pair[1])
        there = other_core(jnp.where(first, pair[1], pair[0]))
        both_rows = jnp.where(
            first, jnp.concatenate([here, there], 0), jnp.concatenate([there, here], 0)
        )
        return both_rows.reshape((1,) + tokens.shape)

    tick(ff0_sum, vec_sum)
    layer_out = settle_rows((y0, y1))
    tick(ff1, vec_sum)
    tick(attn0)
    tick(attn1, vec_sum)
    input_grads = settle_rows((xgrad0, xgrad1))
    tick(ff1)
    tick(attn0)
    tick(attn1, vec_sum)
    tick(ff0_sum)
    tick(ff1, vec_sum)
    tick(attn0)
    tick(ff0_sum)
    tick(attn1)
    tick(attn0)
    tick(ff0_sum)
    for _ in range(4):
        tick(ff1, attn1, ff0_sum, attn0, vec_sum)
    per = D // dp

    def side(v):
        return v.transpose(1, 0, 2).reshape(v.shape[1], -1)

    def parts(ff, attn):
        if fast:
            ff, attn = ff.result, attn.result
            return side(attn[:3]), attn[3], side(ff[:4]), ff[4:].reshape(FF // dp, D // 2)
        (up, down), (both_attn,) = ff.result, attn.result
        return both_attn[:, :HALF_IN], both_attn[:, HALF_IN:], up, down

    shards = [parts(ff0_sum, attn0), parts(ff1, attn1)]

    def settle(a, b):
        here = jnp.where(first, a, b)
        there = other_core(jnp.where(first, b, a))
        return jnp.where(first, jnp.concatenate([here, there], -1), jnp.concatenate([there, here], -1))

    grad_in, grad_out, grad_up, grad_down = (
        settle(a, b)[None] for a, b in zip(shards[0], shards[1])
    )

    vec = vec_sum.result
    vec = jnp.where(first, vec[:4], vec[4:])
    vec = lax.dynamic_slice(vec, (0, me * per), (4, per))
    return (
        layer_out,
        input_grads,
        vec[0:1],
        vec[1:2],
        grad_in,
        grad_out,
        vec[2:3],
        vec[3:4],
        grad_up,
        grad_down,
    )


def solution(mesh):
    row = P(None, "dp", None, None)
    vec = P("section", None)
    mat = P("section", None, None)
    outs = P("section", None, "dp", None, None)
    out_vec = P("section", "dp")
    out_mat = P("section", "dp", None)
    return jax.shard_map(
        body,
        mesh=mesh,
        in_specs=(row, row, P(None, "dp"), vec, vec, mat, mat, vec, vec, mat, mat),
        out_specs=(outs, outs, out_vec, out_vec, out_mat, out_mat, out_vec, out_vec, out_mat, out_mat),
        check_vma=False,
    )
```

```python
import functools
import math

import jax
import jax.numpy as jnp
import numpy as np
from jax import lax
from jax.experimental import pallas as pl
from jax.experimental.pallas import tpu as pltpu
from jax.sharding import PartitionSpec as P

D = 768
HEADS = 12
HEAD = 64
FF = 3072
BLK = 16
SEQ = 64
SLOTS = 2 * SEQ
PAIRS = HEADS // 2
LANES = 2 * HEAD
BLOCKS = 16
FT = 1536
NFT = FF // FT

norm_eps = 1e-05
masked_score = -1000000000.0
gelu_c = math.sqrt(2.0 / math.pi)
gelu_a = 0.044715

F32 = jnp.float32
BF16 = jnp.bfloat16
VMEM_LIMIT = 63 * 1024 * 1024


def dot(a, b, ca=1, cb=0):
    return lax.dot_general(a, b, (((ca,), (cb,)), ((), ())), preferred_element_type=F32)


def rotary_tables():
    places = (np.arange(SLOTS) % SEQ).astype(np.float32)
    half = HEAD // 2
    freqs = (10000.0 ** (-np.arange(half).astype(np.float32) * 2.0 / HEAD)).astype(np.float32)
    angles = (places[:, None] * freqs[None, :]).astype(np.float32)
    cos, sin = np.cos(angles), np.sin(angles)
    return np.stack(
        [
            np.concatenate([cos] * 4, axis=1),
            np.concatenate([-sin, sin, -sin, sin], axis=1),
        ]
    ).astype(np.float32)


def swap_halves(v):
    lane = lax.broadcasted_iota(jnp.int32, v.shape, 1)
    first = lax.rem(lane, HEAD) < HEAD // 2
    return jnp.where(first, pltpu.roll(v, LANES - 32, 1), pltpu.roll(v, 32, 1))


def open_keys_t(length):
    key = lax.broadcasted_iota(jnp.int32, (SLOTS, SLOTS), 0)
    query = lax.broadcasted_iota(jnp.int32, (SLOTS, SLOTS), 1)
    key_clean, query_clean = key >= SEQ, query >= SEQ
    key_place, query_place = lax.rem(key, SEQ), lax.rem(query, SEQ)
    kb, qb = lax.div(key_place, BLK), lax.div(query_place, BLK)
    both_noisy = jnp.logical_and(jnp.logical_not(key_clean), jnp.logical_not(query_clean))
    both_clean = jnp.logical_and(key_clean, query_clean)
    crossed = jnp.logical_and(key_clean, jnp.logical_not(query_clean))
    structure = (
        (both_noisy & (kb == qb)) | (crossed & (kb < qb)) | (both_clean & (kb <= qb))
    )
    return structure & ((key_place < length) | (key == query))


def norm_stats(v):
    centered = v - jnp.mean(v, axis=-1, keepdims=True)
    spread = jnp.mean(centered * centered, axis=-1, keepdims=True)
    return centered, lax.rsqrt(spread + norm_eps)


def norm_back(dy, source, gain):
    centered, scale = norm_stats(source)
    xhat = centered * scale
    g = dy * gain
    part = scale * (
        g
        - jnp.mean(g, axis=-1, keepdims=True)
        - xhat * jnp.mean(g * xhat, axis=-1, keepdims=True)
    )
    return part, jnp.sum(dy * xhat, axis=0, keepdims=True), jnp.sum(dy, axis=0, keepdims=True)


def col_pieces(rows, cols, n):
    w = cols // n
    return [(slice(0, rows), slice(i * w, (i + 1) * w)) for i in range(n)]


def row_pieces(rows, cols, n):
    w = rows // n
    return [(slice(i * w, (i + 1) * w), slice(0, cols)) for i in range(n)]


IN_PIECES = col_pieces(D, 3 * D, 3)
IN_ALL = col_pieces(D, 3 * D, 1)
OUT_PIECES = row_pieces(D, D, 1)
UP_PIECES = col_pieces(D, FF, NFT)
DOWN_PIECES = row_pieces(FF, D, 1)


class Feed:
    def __init__(self, own):
        self.own, self.queue = own, []

    def weight(self, mine, other, piece, dst, sem):
        self.queue.append((mine, other, piece, dst, sem))
        return pltpu.make_async_copy(mine.at[piece], dst.at[piece], sem)

    def begin(self, count=None):
        count = len(self.queue) if count is None else count
        queue, self.queue = self.queue[:count], self.queue[count:]

        @pl.when(self.own)
        def _():
            for mine, _, piece, dst, sem in queue:
                pltpu.make_async_copy(mine.at[piece], dst.at[piece], sem).start()

        @pl.when(jnp.logical_not(self.own))
        def _():
            for _, other, piece, dst, sem in queue:
                pltpu.make_async_copy(other.at[piece], dst.at[piece], sem).start()


class Drain:
    def __init__(self, sems):
        self.sems, self.copies = sems, []

    def put(self, src, dst):
        c = pltpu.make_async_copy(src, dst, self.sems.at[len(self.copies)])
        c.start()
        self.copies.append(c)
        return c

    def finish(self, skip=()):
        for c in self.copies:
            if not any(c is done for done in skip):
                c.wait()


def make_mask(mask, seqs, scal):
    for s in range(seqs):
        keep = open_keys_t(scal[1 + scal[0] * seqs + s])
        shut = jnp.where(keep, 0.0, 1.0)
        mask[s, :, 0:SLOTS] = shut
        mask[s, :, SLOTS : 2 * SLOTS] = shut


def pair_tile(ref, rows, part, p):
    lo = part * D + p * LANES
    return ref[rows, lo : lo + LANES]


def both_heads(v):
    left = lax.broadcasted_iota(jnp.int32, (SLOTS, LANES), 1) < HEAD
    zero = jnp.zeros((SLOTS, LANES), BF16)
    return jnp.concatenate([jnp.where(left, v, zero), jnp.where(left, zero, v)], axis=0)


def norm_into(dst, source, gain, bias):
    centered, scale = norm_stats(source)
    dst[...] = (centered * scale * gain + bias).astype(BF16)


def project(seqs, normed, w_in, waits, rot_ref, qkv):
    cos, sin = rot_ref[0], rot_ref[1]
    for part in range(3):
        if part < len(waits):
            waits[part].wait()
        for tile in range(D // 256):
            lo = part * D + tile * 256
            val = dot(normed[...], w_in[:, lo : lo + 256])
            if part == 2:
                qkv[:, lo : lo + 256] = val.astype(BF16)
                continue
            for u in range(2):
                for s in range(seqs):
                    v = val[s * SLOTS : (s + 1) * SLOTS, u * LANES : (u + 1) * LANES]
                    v = v * cos + swap_halves(v) * sin
                    if part == 0:
                        v = v * HEAD ** (-0.5)
                    qkv[
                        s * SLOTS : (s + 1) * SLOTS, lo + u * LANES : lo + (u + 1) * LANES
                    ] = v.astype(BF16)


def attend(seqs, qkv, mask, scores, probs, mixed):
    for s in range(seqs):
        rows = slice(s * SLOTS, (s + 1) * SLOTS)
        for p in range(PAIRS):
            scores[s * PAIRS + p] = dot(
                pair_tile(qkv, rows, 1, p), both_heads(pair_tile(qkv, rows, 0, p)), 1, 1
            )
        for p in range(PAIRS):
            i = s * PAIRS + p
            st = jnp.where(mask[s] > 0.5, masked_score, scores[i])
            e = jnp.exp(st - jnp.max(st, axis=0, keepdims=True))
            low = (e * (1.0 / jnp.sum(e, axis=0, keepdims=True))).astype(BF16)
            probs[i, 0:SLOTS] = low[:, :SLOTS]
            probs[i, SLOTS : 2 * SLOTS] = low[:, SLOTS:]
        for p in range(PAIRS):
            mixed[rows, p * LANES : (p + 1) * LANES] = dot(
                probs[s * PAIRS + p], both_heads(pair_tile(qkv, rows, 2, p)), 0, 0
            ).astype(BF16)


def activate(dense, w_up, slope, active, waits):
    for t in range(FF // 256):
        if t * 256 % FT == 0:
            waits[t * 256 // FT].wait()
        cols = slice(t * 256, (t + 1) * 256)
        u = dot(dense[...], w_up[:, cols])
        u2 = u * u
        th = jnp.tanh(u * (gelu_c + (gelu_c * gelu_a) * u2))
        h = 0.5 * (1.0 + th)
        active[:, cols] = (u * h).astype(BF16)
        slope[:, cols] = (
            h + u * (1.0 - th * th) * (0.5 * gelu_c + (1.5 * gelu_c * gelu_a) * u2)
        ).astype(BF16)


def open_kernel(seqs, scal, x_ref, vec_mine, vec_other, rot_ref, in_mine, in_other,
                acts_o, qkv_o, probs_o,
                acts, qkv, scores, probs, w_in, mask, sems, out_sems):
    own = scal[0] == 0
    feed, drain = Feed(own), Drain(out_sems)
    w_waits = [feed.weight(in_mine, in_other, IN_PIECES[i], w_in, sems.at[i]) for i in range(3)]
    feed.begin()
    vec = jnp.where(own, vec_mine[...], vec_other[...])
    normed, mixed = acts.at[:, 0:D], acts.at[:, D : 2 * D]
    norm_into(normed, x_ref[...].astype(F32), vec[0:1], vec[1:2])
    make_mask(mask, seqs, scal)
    project(seqs, normed, w_in, w_waits, rot_ref, qkv)
    drain.put(qkv, qkv_o)
    attend(seqs, qkv, mask, scores, probs, mixed)
    drain.put(probs, probs_o)
    drain.put(acts, acts_o)
    drain.finish()


def halves(core, width):
    keep = pl.ds(pl.multiple_of(core * width, 128), width)
    send = pl.ds(pl.multiple_of((1 - core) * width, 128), width)
    return keep, send


def split_out(drain, core, src, width, at, keep_o, send_o, send_base):
    keep, send = halves(core, width)
    drain.put(src.at[:, keep], keep_o.at[:, at : at + width])
    drain.put(src.at[:, send], send_o.at[:, send_base + at : send_base + at + width])


def ff_back(r_ref, hidden, gain, w_up, w_down, w_out, slope, ug, bgrad, hgrad, mgrad, vgrad, waits):
    down_waits, up_waits, out_waits = waits
    for t in range(FF // 256):
        if t * 256 % FT == 0 and down_waits:
            for c in down_waits[t * 256 // FT]:
                c.wait()
        cols = slice(t * 256, (t + 1) * 256)
        ug[:, cols] = (dot(r_ref[...], w_down[cols, :], 1, 1) * slope[:, cols].astype(F32)).astype(BF16)
    for c in up_waits:
        c.wait()
    part, dg, db = norm_back(dot(ug[...], w_up[...], 1, 1), hidden[...], gain)
    vgrad[2:3] = dg
    vgrad[3:4] = db
    total = r_ref[...].astype(F32) + part
    hgrad[...] = total
    bgrad[...] = total.astype(BF16)
    for c in out_waits:
        c.wait()
    mgrad[...] = dot(bgrad[...], w_out[...], 1, 1).astype(BF16)


def attn_back(seqs, x_ref, gain, rot_ref, w_in, qkv, probs, dpt, mgrad, hgrad, pgrad, xgrad, vgrad, waits):
    in_waits, w_waits = waits
    cos, sin = rot_ref[0], rot_ref[1]
    for c in in_waits:
        c.wait()
    for s in range(seqs):
        rows = slice(s * SLOTS, (s + 1) * SLOTS)
        for p in range(PAIRS):
            dm = both_heads(mgrad[rows, p * LANES : (p + 1) * LANES])
            dpt[p] = dot(pair_tile(qkv, rows, 2, p), dm, 1, 1)
        for p in range(PAIRS):
            i = s * PAIRS + p
            low = jnp.concatenate([probs[i, 0:SLOTS], probs[i, SLOTS : 2 * SLOTS]], axis=1)
            pt = low.astype(F32)
            pd = pt * dpt[p]
            dst = (pd - pt * jnp.sum(pd, axis=0, keepdims=True)).astype(BF16)
            dm = both_heads(mgrad[rows, p * LANES : (p + 1) * LANES])
            dv = dot(low, dm)
            dk = dot(dst, both_heads(pair_tile(qkv, rows, 0, p)))
            stacked = jnp.concatenate([dst[:, :SLOTS], dst[:, SLOTS:]], axis=0)
            dq = dot(stacked, both_heads(pair_tile(qkv, rows, 1, p)), 0, 0) * HEAD ** (-0.5)
            dq = dq * cos - swap_halves(dq) * sin
            dk = dk * cos - swap_halves(dk) * sin
            pgrad[rows, p * LANES : (p + 1) * LANES] = dq.astype(BF16)
            pgrad[rows, D + p * LANES : D + (p + 1) * LANES] = dk.astype(BF16)
            pgrad[rows, 2 * D + p * LANES : 2 * D + (p + 1) * LANES] = dv.astype(BF16)
    for c in w_waits:
        c.wait()
    part, dg, db = norm_back(dot(pgrad[...], w_in[...], 1, 1), x_ref[...].astype(F32), gain)
    vgrad[0:1] = dg
    vgrad[1:2] = db
    xgrad[...] = (hgrad[...] + part).astype(BF16)


ACTIVE_AT, DENSE_AT, NORMED_AT, MIXED_AT = 0, FF, FF + D, FF + 2 * D
HALF_IN, HALF_OUT, HALF_UP = 3 * D // 2, D // 2, FF // 2
UG_AT, PG_AT, BG_AT = 0, HALF_UP, HALF_UP + HALF_IN
GRAD_COLS = HALF_UP + HALF_IN + HALF_OUT
GRADS_AT = FF + 3 * D


def middle_kernel(seqs, scal, x_ref, cot_ref, acts0, vec_mine, vec_other, rot_ref,
                  in_mine, in_other, out_mine, out_other, up_mine, up_other, down_mine, down_other,
                  ff0_o, hidden0_o, slope0_o, y0_o, send1_o, keep1_o, y1_o, xgrad1_o, vgrad_ref,
                  w_in, w_out0, w_out1, w_up0, w_up1, w_down0, w_down1,
                  dense, hidden, slope, active, y, normed, mixed, qkv, scores, probs, mask,
                  ug, bgrad, hgrad, mgrad, pgrad, xgrad, sems, drain_sems):
    core = scal[0]
    own = core == 0
    drain = Drain(drain_sems)

    def weights(feed, base, w_out, w_up, w_down):
        out = feed.weight(out_mine, out_other, OUT_PIECES[0], w_out, sems.at[base])
        up = [feed.weight(up_mine, up_other, UP_PIECES[i], w_up, sems.at[base + 1 + i]) for i in range(NFT)]
        down = feed.weight(down_mine, down_other, DOWN_PIECES[0], w_down, sems.at[base + 1 + NFT])
        return out, up, down

    feed0, feed1 = Feed(own), Feed(jnp.logical_not(own))
    waits0 = weights(feed0, 0, w_out0, w_up0, w_down0)
    in_waits = [feed1.weight(in_mine, in_other, IN_ALL[0], w_in, sems.at[4 + 2 * NFT])]
    waits1 = weights(feed1, 2 + NFT, w_out1, w_up1, w_down1)
    feed0.begin(2)
    vec0 = jnp.where(own, vec_mine[...], vec_other[...])
    vec1 = jnp.where(own, vec_other[...], vec_mine[...])
    make_mask(mask, seqs, scal)

    def tail(layer, x, mixed_in, w_out, w_up, w_down, waits, vec, held, following):
        waits[0].wait()
        following()
        hidden[layer] = x + dot(mixed_in[...], w_out[...])
        norm_into(dense.at[layer], hidden[layer], vec[2:3], vec[3:4])
        for c in held:
            c.wait()
        activate(dense.at[layer], w_up, slope, active, waits[1])
        waits[2].wait()
        y[layer] = (hidden[layer] + dot(active[...], w_down[...])).astype(BF16)

    def first_loads():
        feed0.begin()
        feed1.begin(1)

    tail(
        0, x_ref[...].astype(F32), acts0.at[:, D : 2 * D], w_out0, w_up0, w_down0, waits0, vec0, (), first_loads
    )
    copies = [drain.put(slope, slope0_o), drain.put(active, ff0_o.at[:, ACTIVE_AT : ACTIVE_AT + FF])]
    drain.put(dense.at[0], ff0_o.at[:, DENSE_AT : DENSE_AT + D])
    drain.put(acts0, ff0_o.at[:, NORMED_AT : NORMED_AT + 2 * D])
    drain.put(hidden.at[0], hidden0_o)
    drain.put(y.at[0], y0_o)
    norm_into(normed, y[0].astype(F32), vec1[0:1], vec1[1:2])
    in_waits[0].wait()
    feed1.begin()
    project(seqs, normed, w_in, (), rot_ref, qkv)
    attend(seqs, qkv, mask, scores, probs, mixed)
    tail(
        1, y[0].astype(F32), mixed, w_out1, w_up1, w_down1, waits1, vec1, copies, lambda: None
    )
    drain.put(active, send1_o.at[:, ACTIVE_AT : ACTIVE_AT + FF])
    drain.put(dense.at[1], send1_o.at[:, DENSE_AT : DENSE_AT + D])
    drain.put(normed, send1_o.at[:, NORMED_AT : NORMED_AT + D])
    drain.put(mixed, send1_o.at[:, MIXED_AT : MIXED_AT + D])
    drain.put(y.at[1], y1_o)
    ff_back(
        cot_ref, hidden.at[1], vec1[2:3], w_up1, w_down1, w_out1, slope, ug, bgrad, hgrad, mgrad, vgrad_ref,
        ((), (), ()),
    )
    split_out(drain, core, ug, HALF_UP, UG_AT, keep1_o, send1_o, GRADS_AT)
    split_out(drain, core, bgrad, HALF_OUT, BG_AT, keep1_o, send1_o, GRADS_AT)
    attn_back(
        seqs, y.at[0], vec1[0:1], rot_ref, w_in, qkv, probs, scores, mgrad, hgrad, pgrad, xgrad, vgrad_ref,
        ((), ()),
    )
    split_out(drain, core, pgrad, HALF_IN, PG_AT, keep1_o, send1_o, GRADS_AT)
    drain.put(xgrad, xgrad1_o)
    drain.put(xgrad, send1_o.at[:, GRADS_AT + GRAD_COLS : GRADS_AT + GRAD_COLS + D])
    drain.finish(copies)


def ff_last_kernel(scal, r_ref, hidden_ref, vec_mine, vec_other, slope_ref,
                   out_mine, out_other, up_mine, up_other, down_mine, down_other,
                   keep0_o, send0_o, hgrad_ref, mgrad_ref, vgrad_ref,
                   w_up, w_down, w_out, slope, ug, bgrad, sems, drain_sems):
    core = scal[0]
    own = core == 0
    feed, drain = Feed(own), Drain(drain_sems)
    pieces = row_pieces(FF, D, NFT)
    tiles = []
    for i in range(NFT):
        cols = slice(i * FT, (i + 1) * FT)
        load = pltpu.make_async_copy(slope_ref.at[:, cols], slope.at[:, cols], sems.at[1 + NFT + i])
        tiles.append([feed.weight(down_mine, down_other, pieces[i], w_down, sems.at[1 + i]), load])
        feed.begin()
        load.start()
    ups = [feed.weight(up_mine, up_other, UP_PIECES[i], w_up, sems.at[1 + 2 * NFT + i]) for i in range(NFT)]
    out = [feed.weight(out_mine, out_other, OUT_PIECES[0], w_out, sems.at[0])]
    feed.begin()
    vec = jnp.where(own, vec_mine[...], vec_other[...])
    ff_back(
        r_ref, hidden_ref, vec[2:3], w_up, w_down, w_out, slope, ug, bgrad, hgrad_ref, mgrad_ref, vgrad_ref,
        (tiles, ups, out),
    )
    split_out(drain, core, ug, HALF_UP, UG_AT, keep0_o, send0_o, 0)
    split_out(drain, core, bgrad, HALF_OUT, UG_AT + HALF_UP, keep0_o, send0_o, 0)
    drain.finish()


def attn_last_kernel(seqs, scal, x_ref, mgrad_ref, hgrad_ref, vec_mine, vec_other, rot_ref, qkv_ref, probs_ref,
                     in_mine, in_other,
                     keep0_o, send0_o, xgrad_o, vgrad_ref,
                     w_in, qkv, probs, dpt, pgrad, xgrad, sems, drain_sems):
    core = scal[0]
    own = core == 0
    feed, drain = Feed(own), Drain(drain_sems)
    plain = [
        pltpu.make_async_copy(src, dst, sems.at[i])
        for i, (src, dst) in enumerate(((qkv_ref, qkv), (probs_ref, probs)))
    ]
    for c in plain:
        c.start()
    w_waits = [feed.weight(in_mine, in_other, IN_ALL[0], w_in, sems.at[2])]
    feed.begin()
    vec = jnp.where(own, vec_mine[...], vec_other[...])
    attn_back(
        seqs, x_ref, vec[0:1], rot_ref, w_in, qkv, probs, dpt, mgrad_ref, hgrad_ref, pgrad, xgrad, vgrad_ref,
        (plain, w_waits),
    )
    split_out(drain, core, pgrad, HALF_IN, 0, keep0_o, send0_o, 0)
    drain.put(xgrad, xgrad_o)
    drain.finish()


def wgrad_kernel(terms, is_ff, table, scal, *refs):
    n = len(terms)
    srcs, (keep_o, send_o) = refs[: 4 * n], refs[4 * n : 4 * n + 2]
    held, rest = refs[4 * n + 2 : 6 * n + 2], refs[6 * n + 2 :]
    results, (sems, drain_sems) = rest[:-2], rest[-2:]
    core = scal[0]
    loads = []
    for i, (rows, width, a_at, b_at) in enumerate(terms):
        tokens = held[2 * i].shape[0] // 2
        for j in range(2):
            mine = slice(j * tokens, (j + 1) * tokens)
            col, row = b_at[j](core)
            src = srcs[4 * i + 2 + j].at[pl.ds(row, tokens), pl.ds(col, width)]
            loads.append(pltpu.make_async_copy(src, held[2 * i + 1].at[mine], sems.at[len(loads)]))
            src = srcs[4 * i + j].at[:, a_at[j] : a_at[j] + rows]
            loads.append(pltpu.make_async_copy(src, held[2 * i].at[mine], sems.at[len(loads)]))
    for c in loads[:4]:
        c.start()
    half, per, chunk = BLOCKS // 2, D // BLOCKS, D // 2
    drain = Drain(drain_sems)

    def wait_for(i):
        for c in loads[4 * i : 4 * i + 4]:
            c.wait()
        for c in loads[4 * i + 4 : 4 * i + 8]:
            c.start()

    def send_block(r, src, at, count):
        dst = keep_o.at[r] if r < half else send_o.at[r - half]
        drain.put(src, dst.at[at : at + count])

    def side_by_side(i, res, base):
        a, b = held[2 * i], held[2 * i + 1]
        count = terms[i][1] // chunk
        for j in range(0, count, 2):
            m = min(2, count - j)
            val = dot(a[...], b[:, j * chunk : (j + m) * chunk], 0, 0).astype(BF16)
            for k in range(m):
                res[base + j + k] = val[:, k * chunk : (k + 1) * chunk].reshape(BLOCKS, per, chunk)
        return base + count

    wait_for(0)
    if is_ff:
        count = side_by_side(0, results[0], 0)
        for r in list(range(half, BLOCKS)) + list(range(half)):
            send_block(r, results[0].at[:, scal[table + r]], 0, count)
        wait_for(1)
        a, b = held[2:4]
        deep = FF // D
        for q in range(deep):
            val = dot(a[:, q * D : (q + 1) * D], b[...], 0, 0).astype(BF16)
            results[1][q * BLOCKS : (q + 1) * BLOCKS] = val.reshape(BLOCKS, per, chunk)
        for r in list(range(half, BLOCKS)) + list(range(half)):
            send_block(r, results[1].at[pl.ds(scal[table + r] * deep, deep)], count, deep)
    else:
        count = side_by_side(0, results[0], 0)
        wait_for(1)
        count = side_by_side(1, results[0], count)
        for r in list(range(half, BLOCKS)) + list(range(half)):
            send_block(r, results[0].at[:, scal[table + r]], 0, count)
    drain.finish()


def whole(shape):
    return pl.BlockSpec(shape, lambda i, s: (0,) * len(shape))


def shape_of(shape, dtype):
    return jax.ShapeDtypeStruct(shape, dtype)


HBM = pl.BlockSpec(memory_space=pl.ANY)


class Chain:
    def __init__(self):
        self.token = ()

    def call(self, kernel, scal, ins, in_specs, outs, out_specs, scratch, micros, after=()):
        after = tuple(self.token) + tuple(after)
        n, extra = 1 + len(ins), len(after)

        def ordered(*refs):
            kernel(*refs[:n], *refs[n + extra :])

        result = pl.pallas_call(
            ordered,
            grid_spec=pltpu.PrefetchScalarGridSpec(
                num_scalar_prefetch=1,
                grid=(1,),
                in_specs=list(in_specs) + [HBM] * extra,
                out_specs=out_specs,
                scratch_shapes=scratch,
            ),
            out_shape=outs,
            compiler_params=pltpu.CompilerParams(vmem_limit_bytes=VMEM_LIMIT),
            cost_estimate=pl.CostEstimate(
                flops=int(micros * 1e6), bytes_accessed=2**10, transcendentals=0
            ),
        )(scal, *ins, *after)
        self.token = (result[-1],)
        return result


def axis_pairs(first, second, size):
    return [(i, i ^ first) for i in range(size)] + [
        (size + i, size + (i ^ second)) for i in range(size)
    ]


def body(
    tokens, cotangent, lengths, mixer_gain, mixer_bias, project_in, project_out,
    dense_gain, dense_bias, up_weight, down_weight,
):
    micro, rows = tokens.shape[:2]
    total = micro * rows
    seqs = total // 2
    t = seqs * SLOTS
    core = lax.axis_index("section")
    first = core == 0
    me = lax.axis_index("dp")
    dp = lax.axis_size("dp")
    fast = dp == BLOCKS
    both = ("section", "dp")
    chain = Chain()

    def other_core(v):
        return lax.ppermute(v, "section", [(0, 1), (1, 0)])

    mine = {
        "vec": jnp.concatenate([mixer_gain, mixer_bias, dense_gain, dense_bias], axis=0),
        "in": project_in[0],
        "out": project_out[0],
        "up": up_weight[0],
        "down": down_weight[0],
    }
    other = {name: other_core(mine[name]) for name in ("vec", "in")}
    other["in"], out_held, up_held, down_held = lax.optimization_barrier(
        (other["in"], mine["out"], mine["up"], mine["down"])
    )
    other["out"], other["up"], other["down"] = map(other_core, (out_held, up_held, down_held))
    rot = jnp.asarray(rotary_tables())
    scal = jnp.concatenate([core.reshape(1), lengths.reshape(total)]).astype(jnp.int32)

    steps = {"A": (1, 2), "B": (2, 1), "l": (4, 8), "h": (8, 4)}
    names = ("ff1", "attn1", "ff0", "attn0")
    orders = dict(zip(names, ("AlBh", "lABh", "AlBh", "ABlh")))
    bits_of = {name: [steps[c] for c in orders[name]] for name in names}
    table_of = {name: 1 + BLOCKS * i for i, name in enumerate(names)}
    xy_bits = [steps[c] for c in "ABlh"]

    def places(bits):
        if not fast:
            return jnp.asarray(np.arange(BLOCKS), jnp.int32)
        rel = np.zeros((2, BLOCKS), np.int32)
        for c in range(2):
            for r in range(BLOCKS):
                for stage in range(4):
                    if r >> (3 - stage) & 1:
                        rel[c, r] ^= bits[stage][c]
        return me ^ jnp.where(first, jnp.asarray(rel[0]), jnp.asarray(rel[1]))

    order = jnp.concatenate([core.reshape(1)] + [places(bits_of[name]) for name in names]).astype(jnp.int32)

    class Batch:
        def __init__(self, pair, bits):
            self.keep, self.send = pair
            self.bits, self.stage, self.result = bits, 0, None
            if not fast:
                flat = jnp.concatenate(pair, axis=0).astype(F32)
                n, count, per, chunk = flat.shape
                side = flat[:, :4].transpose(0, 2, 1, 3).reshape(n * per, 4 * chunk)
                self.result = [lax.psum_scatter(side, "dp", scatter_dimension=0, tiled=True)]
                if count > 4:
                    deep = flat[:, 4:].reshape(n * 4 * per, chunk)
                    self.result.append(lax.psum_scatter(deep, "dp", scatter_dimension=0, tiled=True))
            else:
                self.start()

        def start(self):
            self.got = lax.ppermute(self.send, both, axis_pairs(*self.bits[self.stage], dp))
            self.stage += 1

        def advance(self):
            half = self.keep.shape[0] // 2
            if half == 0:
                self.result = self.keep[0].astype(F32) + self.got[0].astype(F32)
                return self.result
            self.send = self.keep[half:] + self.got[half:]
            keep, got, self.send = lax.optimization_barrier((self.keep, self.got, self.send))
            self.keep = keep[:half] + got[:half]
            return self.send

    class Vector:
        def __init__(self, value):
            self.value, self.stage, self.result = value, 0, None
            if not fast:
                self.result = lax.psum(value, both)
            else:
                self.got = other_core(value)

        def held(self):
            return [self.value, self.got]

        def start(self):
            self.got = lax.ppermute(self.value, both, axis_pairs(*xy_bits[self.stage], dp))
            self.stage += 1

        def advance(self):
            self.value = self.value + self.got
            if self.stage == 4:
                self.result = self.value
            return self.value

    def tick(*batches):
        batches = [b for b in batches if b.result is None]
        if not batches:
            return
        held = []
        for b in batches:
            held += [b.value, b.got] if isinstance(b, Vector) else [b.keep, b.got]
        held = lax.optimization_barrier(tuple(held) + tuple(chain.token))
        tokens_out = []
        for i, b in enumerate(batches):
            if isinstance(b, Vector):
                b.value, b.got = held[2 * i], held[2 * i + 1]
            else:
                b.keep, b.got = held[2 * i], held[2 * i + 1]
            tokens_out.append(b.advance())
        for b in batches:
            if b.result is None:
                b.start()
        chain.token = tuple(tokens_out)

    x0 = tokens.reshape(total * SLOTS, D)
    cot = cotangent.reshape(total * SLOTS, D)
    half_spec = pl.BlockSpec((t, D), lambda i, s: (s[0], 0))
    tok = whole((t, D))
    vec_spec, rot_spec = whole((4, D)), whole((2, SLOTS, LANES))
    scores_shape = (seqs * PAIRS, SLOTS, 2 * SLOTS)
    probs_shape = (seqs * PAIRS, 2 * SLOTS, SLOTS)
    vmem, dma = pltpu.VMEM, pltpu.SemaphoreType.DMA
    vecs = (mine["vec"], other["vec"], rot)
    vec_specs = [vec_spec, vec_spec, rot_spec]
    weights = (
        mine["in"], other["in"], mine["out"], other["out"],
        mine["up"], other["up"], mine["down"], other["down"],
    )
    row16, row32, wide16 = shape_of((t, D), BF16), shape_of((t, D), F32), shape_of((t, FF), BF16)
    three16 = shape_of((t, 3 * D), BF16)
    small = vmem((t, D), BF16)
    wide = vmem((t, FF), BF16)
    three = vmem((t, 3 * D), BF16)
    probs_mem, scores_mem = vmem(probs_shape, BF16), vmem(scores_shape, F32)
    mask_mem = vmem((seqs, SLOTS, 2 * SLOTS), F32)
    mem_in, mem_out, mem_up, mem_down = (
        vmem((D, 3 * D), BF16), vmem((D, D), BF16), vmem((D, FF), BF16), vmem((FF, D), BF16),
    )

    acts0, qkv0, probs0 = chain.call(
        functools.partial(open_kernel, seqs), scal,
        (x0,) + vecs + weights[:2],
        [half_spec] + vec_specs + [HBM] * 2,
        [shape_of((t, 2 * D), BF16), three16, shape_of(probs_shape, BF16)],
        [HBM] * 3,
        [vmem((t, 2 * D), BF16), three, scores_mem, probs_mem, mem_in, mask_mem, dma((3,)), dma((3,))],
        8.0,
    )
    ff0, hidden0, slope0, y0, send1, keep1, y1, xgrad1, vgrad1 = chain.call(
        functools.partial(middle_kernel, seqs), scal,
        (x0, cot, acts0) + vecs + weights,
        [half_spec, half_spec, whole((t, 2 * D))] + vec_specs + [HBM] * 8,
        [shape_of((t, GRADS_AT), BF16), row32, wide16, row16, shape_of((t, GRADS_AT + GRAD_COLS + D), BF16),
         shape_of((t, GRAD_COLS), BF16), row16, row16, shape_of((4, D), F32)],
        [HBM] * 8 + [whole((4, D))],
        [mem_in, mem_out, mem_out, mem_up, mem_up, mem_down, mem_down,
         vmem((2, t, D), BF16), vmem((2, t, D), F32), wide, wide, vmem((2, t, D), BF16), small, small, three,
         scores_mem, probs_mem, mask_mem, wide, small, vmem((t, D), F32), small, three, small,
         dma((5 + 2 * NFT,)), dma((20,))],
        30.0,
    )
    send1_o = other_core(send1)
    ff0_o = other_core(ff0)

    def wgrads(name, terms, is_ff):
        ins, held, plan = [], [], []
        for (a0, a1), a_at, rows, (b0, b1), b_at, width in terms:
            ins += [a0, a1, b0, b1]
            held += [vmem((2 * t, rows), BF16), vmem((2 * t, width), BF16)]
            plan.append((rows, width, a_at, b_at))
        per, chunk = D // BLOCKS, D // 2
        half = shape_of((BLOCKS // 2, 8 if is_ff else 4, per, chunk), BF16)
        results = [vmem((4, BLOCKS, per, chunk), BF16)]
        if is_ff:
            results.append(vmem((FF // per, per, chunk), BF16))
        return chain.call(
            functools.partial(wgrad_kernel, plan, is_ff, table_of[name]), order, ins, [HBM] * len(ins), [half] * 2, [HBM] * 2,
            held + results + [dma((4 * len(terms),)), dma((2 * BLOCKS,))],
            8.0,
        )

    def fixed(col):
        return lambda core: (col, 0)

    def own_half(core):
        return pl.multiple_of(core * HALF_OUT, 128)

    def own_cot(core):
        return own_half(core), pl.multiple_of(core * t, 16)

    def other_cot(core):
        return own_half(core), pl.multiple_of((1 - core) * t, 16)

    def own_cols(core):
        return own_half(core), 0

    def own_xgrad(core):
        return pl.multiple_of(GRADS_AT + GRAD_COLS + core * HALF_OUT, 128), 0

    keep0, send0, hgrad0, mgrad0, vgrad0_ff = chain.call(
        ff_last_kernel, scal,
        (xgrad1, hidden0) + vecs[:2] + (slope0,) + weights[2:],
        [tok, tok] + vec_specs[:2] + [HBM] * 7,
        [shape_of((t, HALF_UP + HALF_OUT), BF16)] * 2 + [row32, row16, shape_of((4, D), F32)],
        [HBM] * 2 + [tok, tok, whole((4, D))],
        [mem_up, mem_down, mem_out, wide, wide, small, dma((1 + 3 * NFT,)), dma((4,))],
        10.0,
    )
    send0_o = other_core(send0)
    grads_at = GRADS_AT
    acts1, grads1 = (send1, send1_o), (keep1, send1_o)
    ff1 = Batch(
        wgrads(
            "ff1",
            [
                (acts1, (DENSE_AT,) * 2, D, grads1, (fixed(UG_AT), fixed(grads_at + UG_AT)), HALF_UP),
                (acts1, (ACTIVE_AT,) * 2, FF, (cot, cot), (own_cot, other_cot), HALF_OUT),
            ],
            True,
        ),
        bits_of["ff1"],
    )
    attn1 = Batch(
        wgrads(
            "attn1",
            [
                (acts1, (NORMED_AT,) * 2, D, grads1, (fixed(PG_AT), fixed(grads_at + PG_AT)), HALF_IN),
                (acts1, (MIXED_AT,) * 2, D, grads1, (fixed(BG_AT), fixed(grads_at + BG_AT)), HALF_OUT),
            ],
            False,
        ),
        bits_of["attn1"],
    )
    ff0_sum = Batch(
        wgrads(
            "ff0",
            [
                ((ff0, ff0_o), (DENSE_AT,) * 2, D, (keep0, send0_o), (fixed(0),) * 2, HALF_UP),
                ((ff0, ff0_o), (ACTIVE_AT,) * 2, FF, (xgrad1, send1_o), (own_cols, own_xgrad), HALF_OUT),
            ],
            True,
        ),
        bits_of["ff0"],
    )
    pkeep0, psend0, xgrad0, vgrad0_attn = chain.call(
        functools.partial(attn_last_kernel, seqs), scal,
        (x0, mgrad0, hgrad0) + vecs + (qkv0, probs0) + weights[:2],
        [half_spec, tok, tok] + vec_specs + [HBM] * 4,
        [shape_of((t, HALF_IN), BF16)] * 2 + [row16, shape_of((4, D), F32)],
        [HBM] * 3 + [whole((4, D))],
        [mem_in, three, probs_mem, vmem((PAIRS, SLOTS, 2 * SLOTS), F32), three, small, dma((3,)), dma((3,))],
        9.0,
    )
    psend0_o = other_core(psend0)
    tick(ff1)
    attn0 = Batch(
        wgrads(
            "attn0",
            [
                ((ff0, ff0_o), (NORMED_AT,) * 2, D, (pkeep0, psend0_o), (fixed(0),) * 2, HALF_IN),
                ((ff0, ff0_o), (MIXED_AT,) * 2, D, (keep0, send0_o), (fixed(HALF_UP),) * 2, HALF_OUT),
            ],
            False,
        ),
        bits_of["attn0"],
    )
    vgrad0 = jnp.concatenate([vgrad0_attn[:2], vgrad0_ff[2:]], axis=0)
    vec_sum = Vector(jnp.concatenate([vgrad0, vgrad1], axis=0))

    def settle_rows(pair):
        held = lax.optimization_barrier(tuple(pair) + tuple(chain.token))
        pair = held[:2]
        here = jnp.where(first, pair[0], pair[1])
        there = other_core(jnp.where(first, pair[1], pair[0]))
        both_rows = jnp.where(
            first, jnp.concatenate([here, there], 0), jnp.concatenate([there, here], 0)
        )
        return both_rows.reshape((1,) + tokens.shape)

    tick(attn1)
    tick(ff0_sum, vec_sum)
    layer_out = settle_rows((y0, y1))
    tick(ff1, vec_sum)
    tick(attn0)
    tick(attn1, vec_sum)
    input_grads = settle_rows((xgrad0, xgrad1))
    tick(ff1)
    tick(attn0)
    tick(attn1, vec_sum)
    tick(ff0_sum)
    tick(ff1, vec_sum)
    tick(attn0)
    tick(ff0_sum)
    tick(attn1)
    tick(attn0)
    tick(ff0_sum)
    for _ in range(4):
        tick(ff1, attn1, ff0_sum, attn0, vec_sum)
    per = D // dp

    def side(v):
        return v.transpose(1, 0, 2).reshape(v.shape[1], -1)

    def parts(ff, attn):
        if fast:
            ff, attn = ff.result, attn.result
            return side(attn[:3]), attn[3], side(ff[:4]), ff[4:].reshape(FF // dp, D // 2)
        (up, down), (both_attn,) = ff.result, attn.result
        return both_attn[:, :HALF_IN], both_attn[:, HALF_IN:], up, down

    shards = [parts(ff0_sum, attn0), parts(ff1, attn1)]

    def settle(a, b):
        here = jnp.where(first, a, b)
        there = other_core(jnp.where(first, b, a))
        return jnp.where(first, jnp.concatenate([here, there], -1), jnp.concatenate([there, here], -1))

    grad_in, grad_out, grad_up, grad_down = (
        settle(a, b)[None] for a, b in zip(shards[0], shards[1])
    )

    vec = vec_sum.result
    vec = jnp.where(first, vec[:4], vec[4:])
    vec = lax.dynamic_slice(vec, (0, me * per), (4, per))
    return (
        layer_out,
        input_grads,
        vec[0:1],
        vec[1:2],
        grad_in,
        grad_out,
        vec[2:3],
        vec[3:4],
        grad_up,
        grad_down,
    )


def solution(mesh):
    row = P(None, "dp", None, None)
    vec = P("section", None)
    mat = P("section", None, None)
    outs = P("section", None, "dp", None, None)
    out_vec = P("section", "dp")
    out_mat = P("section", "dp", None)
    return jax.shard_map(
        body,
        mesh=mesh,
        in_specs=(row, row, P(None, "dp"), vec, vec, mat, mat, vec, vec, mat, mat),
        out_specs=(outs, outs, out_vec, out_vec, out_mat, out_mat, out_vec, out_vec, out_mat, out_mat),
        check_vma=False,
    )
```
